32 devices in a mesh: bx: 4 (over y, x), by: 4 (over z), bz: 2 (over core).
Axes of the slice: x: 2, y: 2, z: 4, core: 2. Of those that a mesh axis runs over, the one named last changes fastest.
Arguments:
- position: float32 [3, 128, 128, 512], P(None, 'bx', 'by', 'bz'), may hold values from -2 to 2
- velocity: float32 [3, 128, 128, 512], P(None, 'bx', 'by', 'bz'), may hold values from -3 to 3
- density: float32 [128, 128, 512], P('bx', 'by', 'bz'), may hold values from 0.5 to 2
- energy: float32 [128, 128, 512], P('bx', 'by', 'bz'), may hold values from 0.1 to 10
- pinned: int32 [128, 128, 512], P('bx', 'by', 'bz'), may hold values 0 or 1
Outputs:
- velocity_new: float32 [3, 128, 128, 512], P(None, 'bx', 'by', 'bz')
- accel: float32 [3, 128, 128, 512], P(None, 'bx', 'by', 'bz')
- relaxed: float32 [3, 128, 128, 512], P(None, 'bx', 'by', 'bz')
- density_new: float32 [128, 128, 512], P('bx', 'by', 'bz')
- energy_new: float32 [128, 128, 512], P('bx', 'by', 'bz')
The draws below stay inside these ranges and needn't reach their ends.
All inputs are finite; a program needn't handle non-finite values. No bound on the sum of `pinned` on one device may be relied on, other than what follows from the above.
Results may differ from the reference program's by a relative error of at most 0.0003.
Values sent between devices are 32-bit elements; how exact they have to be, the bound alone decides.
No kernel may reach another device: no remote copies, remote signals or barrier semaphores. Data moves between devices by JAX's collectives and lax.ppermute only.
A program may use at most 128 MiB of HBM per device.

```python
import math
import jax
import jax.numpy as jnp

CG_ITERS = 2
SWEEPS = 3
NX = 128
NY = 128
NZ = 512


def plant(drawn, key, least, top_value):
    shape = drawn.shape
    index_at = [jax.random.randint(jax.random.fold_in(key, axis), (), 0, shape[axis]) for axis in range(len(shape))]
    drawn = drawn.at[tuple(index_at)].set(least)
    longest = shape.index(max(shape))
    index_at[longest] = (index_at[longest] + 1) % shape[longest]
    return drawn.at[tuple(index_at)].set(top_value)


def block_scale(key, extent, shards, least, largest):
    loudness = 1.0
    for axis_at, blocks in shards:
        draws = jax.random.uniform(jax.random.fold_in(jax.random.fold_in(key, 6), axis_at), (blocks,), jnp.float32, least / len(shards), largest / len(shards))
        loudness = loudness * jnp.repeat(jnp.exp(draws), extent[axis_at] // blocks).reshape((-1,) + (1,) * (len(extent) - 1 - axis_at))
    return loudness


def bell_draw(rng, dims, scale, most, shards=(), kind=jnp.bfloat16):
    values = jax.random.normal(rng, dims, jnp.float32) * scale
    if len(shards) > 0:
        values = block_scale(rng, dims, shards, -0.22, 0.18) * values
    return jnp.clip(values, min=-most, max=most).astype(kind)


def setup_inputs(seed: int = 0) -> dict:
    streams_of = jax.random.split(jax.random.key(seed), 6)
    return {
        "position": bell_draw(streams_of[0], (3, NX, NY, NZ), 0.3, 2.0, ((1, 4), (2, 4), (3, 2)), jnp.float32),
        "velocity": bell_draw(streams_of[1], (3, NX, NY, NZ), 0.4, 3.0, ((1, 4), (2, 4), (3, 2)), jnp.float32),
        "density": jnp.clip(0.5 + 1.5 * jax.random.uniform(streams_of[2], (NX, NY, NZ), jnp.float32) ** block_scale(streams_of[2], (NX, NY, NZ), ((0, 4), (1, 4), (2, 2)), -0.2, 0.2), 0.5, 2.0),
        "energy": jnp.clip(jnp.exp(math.log(10.0) - 4.6051702 * jax.random.uniform(streams_of[3], (NX, NY, NZ), jnp.float32) ** block_scale(streams_of[3], (NX, NY, NZ), ((0, 4), (1, 4), (2, 2)), -0.2, 0.2)), 0.1, 10.0),
        "pinned": plant((jax.random.randint(streams_of[4], (NX, NY, NZ), 0, 8) < 1).astype(jnp.int32), jax.random.fold_in(streams_of[4], 1), 0, 1),
    }


TIME_STEP = 0.6
RELAX_RATE = 0.8
CONSISTENT = 0.2


def pad_cells(values):
    return jnp.pad(values, [(0, 0)] * (values.ndim - 3) + [(1, 1)] * 3)


def shift_triple(along_dim, along, first, second):
    offsets = [0, 0, 0]
    offsets[along_dim] = along
    others = [d for d in range(3) if d != along_dim]
    offsets[others[0]] = first
    offsets[others[1]] = second
    return offsets


def select_at(extended, offsets):
    sizes = extended.shape[-3:]
    return extended[..., 1 + offsets[0]:sizes[0] - 1 + offsets[0], 1 + offsets[1]:sizes[1] - 1 + offsets[1], 1 + offsets[2]:sizes[2] - 1 + offsets[2]]


def corner_force(pressure_ext):
    parts = []
    for along_dim in range(3):
        summed = 0.0
        for first in (0, -1):
            for second in (0, -1):
                summed = summed + select_at(pressure_ext, shift_triple(along_dim, -1, first, second)) - select_at(pressure_ext, shift_triple(along_dim, 0, first, second))
        parts.append(0.25 * summed)
    return jnp.stack(parts)


def node_mass(density_ext):
    summed = 0.0
    for first in (0, -1):
        for second in (0, -1):
            for third in (0, -1):
                summed = summed + select_at(density_ext, [first, second, third])
    return 0.125 * summed


def neighbours(extended):
    summed = 0.0
    for along_dim in range(3):
        for along in (-1, 1):
            summed = summed + select_at(extended, shift_triple(along_dim, along, 0, 0))
    return summed


def mass_apply(vector, extended, masses):
    return masses * vector + CONSISTENT * (6.0 * vector + neighbours(extended))


def divergence(vel_ext):
    summed = 0.0
    for along_dim in range(3):
        for first in (0, 1):
            for second in (0, 1):
                summed = summed + select_at(vel_ext[along_dim], shift_triple(along_dim, 1, first, second)) - select_at(vel_ext[along_dim], shift_triple(along_dim, 0, first, second))
    return 0.25 * summed


def face_flux(packed, along_dim, along):
    speed = 0.0
    for first in (0, 1):
        for second in (0, 1):
            speed = speed + select_at(packed[along_dim], shift_triple(along_dim, along, first, second))
    speed = 0.25 * speed
    upper = select_at(packed[3:5], shift_triple(along_dim, along, 0, 0))
    lower = select_at(packed[3:5], shift_triple(along_dim, along - 1, 0, 0))
    return speed * jnp.where(speed > 0, upper, lower)


def remap_cells(packed):
    result = select_at(packed[3:5], [0, 0, 0])
    for along_dim in range(3):
        result = result + face_flux(packed, along_dim, 1) - face_flux(packed, along_dim, 0)
    return result


def inner(first, second):
    return jnp.sum(first * second, axis=(1, 2, 3), keepdims=True)


def reference(position, velocity, density, energy, pinned):
    cells = pad_cells(jnp.stack([density, energy]))
    force = corner_force(0.4 * cells[0] * cells[1])
    masses = node_mass(cells[0])
    solution = jnp.zeros_like(force)
    residual = force
    direction = force
    norm_now = inner(residual, residual)
    for step_index in range(CG_ITERS):
        image = mass_apply(direction, pad_cells(direction), masses)
        alpha = norm_now / inner(direction, image)
        solution = solution + alpha * direction
        residual = residual - alpha * image
        norm_next = inner(residual, residual)
        direction = residual + (norm_next / norm_now) * direction
        norm_now = norm_next
    velocity_new = velocity + TIME_STEP * solution
    spread = divergence(pad_cells(velocity_new))
    pressure = 0.4 * density * energy
    energy_lag = energy - TIME_STEP * pressure * spread / density
    moved = position + TIME_STEP * velocity_new
    free = 1.0 - pinned.astype(jnp.float32)
    relaxed = moved
    for step_index in range(SWEEPS):
        relaxed = relaxed + RELAX_RATE * free * (neighbours(pad_cells(relaxed)) / 6.0 - relaxed)
    packed = pad_cells(jnp.concatenate([relaxed - moved, density[None], (density * energy_lag)[None]]))
    remapped = remap_cells(packed)
    return velocity_new, solution, relaxed, remapped[0], remapped[1]
```

```python
import jax
import jax.numpy as jnp
from jax import lax
from jax.sharding import PartitionSpec as P

SWEEPS = 3


TIME_STEP = 0.6
RELAX_RATE = 0.8
CONSISTENT = 0.2


def from_behind(x, axis, by):
    length = lax.axis_size(axis)
    pairs = [(i, i + by) for i in range(length) if 0 <= i + by < length]
    return lax.ppermute(x, axis, pairs)


def padded(block, sides, width):
    for axis, dim in sides:
        count = lax.axis_size(axis)
        forward = [(i, i + 1) for i in range(count - 1)]
        backward = [(target, source) for source, target in forward]
        low = lax.ppermute(
            lax.slice_in_dim(block, block.shape[dim] - width, None, axis=dim), axis, forward
        )
        high = lax.ppermute(lax.slice_in_dim(block, 0, width, axis=dim), axis, backward)
        block = jnp.concatenate([low, block, high], axis=dim)
    return block


def shift_triple(along_dim, along, first, second):
    offsets = [0, 0, 0]
    offsets[along_dim] = along
    others = [d for d in range(3) if d != along_dim]
    offsets[others[0]] = first
    offsets[others[1]] = second
    return offsets


def select_at(extended, offsets):
    sizes = extended.shape[-3:]
    return extended[
        ...,
        1 + offsets[0] : sizes[0] - 1 + offsets[0],
        1 + offsets[1] : sizes[1] - 1 + offsets[1],
        1 + offsets[2] : sizes[2] - 1 + offsets[2],
    ]


def corner_force(pressure_ext):
    parts = []
    for along_dim in range(3):
        summed = 0.0
        for first in (0, -1):
            for second in (0, -1):
                summed = (
                    summed
                    + select_at(pressure_ext, shift_triple(along_dim, -1, first, second))
                    - select_at(pressure_ext, shift_triple(along_dim, 0, first, second))
                )
        parts.append(0.25 * summed)
    return jnp.stack(parts)


def node_mass(density_ext):
    summed = 0.0
    for first in (0, -1):
        for second in (0, -1):
            for third in (0, -1):
                summed = summed + select_at(density_ext, [first, second, third])
    return 0.125 * summed


def neighbours(extended):
    summed = 0.0
    for along_dim in range(3):
        for along in (-1, 1):
            summed = summed + select_at(extended, shift_triple(along_dim, along, 0, 0))
    return summed


def divergence(vel_ext):
    summed = 0.0
    for along_dim in range(3):
        for first in (0, 1):
            for second in (0, 1):
                summed = (
                    summed
                    + select_at(vel_ext[along_dim], shift_triple(along_dim, 1, first, second))
                    - select_at(vel_ext[along_dim], shift_triple(along_dim, 0, first, second))
                )
    return 0.25 * summed


def face_flux(packed, along_dim, along):
    speed = 0.0
    for first in (0, 1):
        for second in (0, 1):
            speed = speed + select_at(
                packed[along_dim], shift_triple(along_dim, along, first, second)
            )
    speed = 0.25 * speed
    upper = select_at(packed[3:5], shift_triple(along_dim, along, 0, 0))
    lower = select_at(packed[3:5], shift_triple(along_dim, along - 1, 0, 0))
    return speed * jnp.where(speed > 0, upper, lower)


def remap_cells(packed):
    result = select_at(packed[3:5], [0, 0, 0])
    for along_dim in range(3):
        result = result + face_flux(packed, along_dim, 1) - face_flux(packed, along_dim, 0)
    return result


def inner(first, second):
    return jnp.sum(first * second, axis=(1, 2, 3), keepdims=True)


def lower_cells(values):
    got = from_behind(values[..., -1:, :, :], "bx", 1)
    widened = jnp.concatenate([got, values], axis=-3)
    got = from_behind(widened[..., :, -1:, :], "by", 1)
    widened = jnp.concatenate([got, widened], axis=-2)
    got = from_behind(widened[..., :, :, -1:], "bz", 1)
    widened = jnp.concatenate([got, widened], axis=-1)
    return jnp.pad(widened, [(0, 0)] * (values.ndim - 3) + [(0, 1)] * 3)


def upper_nodes(values):
    got = from_behind(values[..., :1, :, :], "bx", -1)
    widened = jnp.concatenate([values, got], axis=-3)
    got = from_behind(widened[..., :, :1, :], "by", -1)
    widened = jnp.concatenate([widened, got], axis=-2)
    got = from_behind(widened[..., :, :, :1], "bz", -1)
    widened = jnp.concatenate([widened, got], axis=-1)
    return jnp.pad(widened, [(0, 0)] * (values.ndim - 3) + [(1, 0)] * 3)


def mass_apply(vector, masses):
    extended = padded(vector, (("bx", 1), ("by", 2), ("bz", 3)), 1)
    return masses * vector + CONSISTENT * (6.0 * vector + neighbours(extended))


def solve_weights(force, image, second):
    square = inner(force, force)
    shift = jnp.where(square > 0, inner(force, image) / jnp.where(square > 0, square, 1.0), 0.0)
    rest = image - shift * force
    rest_image = second - shift * image
    sums = jnp.stack(
        [
            shift,
            square,
            inner(force, rest),
            inner(rest, rest),
            inner(force, rest_image),
            inner(rest, rest_image),
        ]
    ).reshape(6, 3)
    got = lax.all_gather(sums, ("bx", "by", "bz"))
    c, p0, q1, q2, q3, q4 = [got[:, i, :] for i in range(6)]
    total = lambda x: jnp.sum(x, axis=0)
    norm_now = total(p0)
    alpha = norm_now / total(q1 + c * p0)
    a = 1.0 - alpha * c
    norm_next = total(a * a * p0 - 2.0 * a * alpha * q1 + alpha * alpha * q2)
    product = total(
        a * a * (q1 + c * p0) - a * alpha * (q3 + q2 + c * q1) + alpha * alpha * q4
    )
    ratio = norm_next / norm_now
    later = norm_next / (product - ratio * norm_next / alpha)
    return (alpha + later * (1.0 + ratio)).reshape(3, 1, 1, 1), (-later * alpha).reshape(3, 1, 1, 1)


def one_sweep(relaxed, free):
    extended = padded(relaxed, (("bx", 1), ("by", 2), ("bz", 3)), 1)
    return relaxed + RELAX_RATE * free * (neighbours(extended) / 6.0 - relaxed)


def on_device(position, velocity, density, energy, pinned):
    cells = lower_cells(jnp.stack([density, energy]))
    force = corner_force(0.4 * cells[0] * cells[1])
    masses = node_mass(cells[0])
    image = mass_apply(force, masses)
    second = mass_apply(image, masses)
    on_force, on_image = solve_weights(force, image, second)
    solution = on_force * force + on_image * image
    velocity_new = velocity + TIME_STEP * solution
    vel_ext = upper_nodes(velocity_new)
    spread = divergence(vel_ext)
    pressure = 0.4 * density * energy
    energy_lag = energy - TIME_STEP * pressure * spread / density
    moved = position + TIME_STEP * velocity_new
    free = 1.0 - pinned.astype(jnp.float32)
    relaxed = moved
    for step_index in range(SWEEPS):
        relaxed = one_sweep(relaxed, free)
    packed = padded(
        jnp.concatenate([relaxed - moved, density[None], (density * energy_lag)[None]]),
        (("bx", 1), ("by", 2), ("bz", 3)),
        1,
    )
    remapped = remap_cells(packed)
    return (velocity_new, solution, relaxed, remapped[0], remapped[1])


def solution(mesh):
    in_specs = (
        P(None, "bx", "by", "bz"),
        P(None, "bx", "by", "bz"),
        P("bx", "by", "bz"),
        P("bx", "by", "bz"),
        P("bx", "by", "bz"),
    )
    out_specs = (
        P(None, "bx", "by", "bz"),
        P(None, "bx", "by", "bz"),
        P(None, "bx", "by", "bz"),
        P("bx", "by", "bz"),
        P("bx", "by", "bz"),
    )
    return jax.shard_map(
        on_device, mesh=mesh, in_specs=in_specs, out_specs=out_specs, check_vma=False
    )
```

```python
import functools

import jax
import jax.numpy as jnp
from jax import lax
from jax.experimental import pallas as pl
from jax.experimental.pallas import tpu as pltpu
from jax.sharding import PartitionSpec as P

SWEEPS = 3
TIME_STEP = 0.6
RELAX_RATE = 0.8
CONSISTENT = 0.2

LANES = 128
ROWS = 8
MOMENTS = 6
NARROW = 2
WIDE = SWEEPS + 2
VMEM_BYTES = 62 * 2**20


class Plan:
    def __init__(self, groups, shape):
        self.groups = groups
        self.x, self.y, self.z = shape
        self.tiles = self.z // LANES
        self.low = max(low for _, low, _ in groups)
        self.high = max(high for _, _, high in groups)
        self.planes = self.low + self.x + self.high
        self.rows = self.y + 2 * ROWS
        self.fields = []
        low_at = high_at = lane_at = 0
        for group, (count, low, high) in enumerate(groups):
            for component in range(count):
                self.fields.append(
                    (group, component, low, high, low_at, high_at, lane_at + low)
                )
                low_at += low
                high_at += high
                lane_at += low + high
        assert lane_at <= LANES
        self.packed_low_at, self.packed_high_at = low_at, high_at
        self.low_rows = low_at + -(-self.low // self.tiles)
        self.high_rows = high_at + -(-self.high // self.tiles)

    def folded(self, k, at):
        return at + k // self.tiles, (k % self.tiles) * LANES


def round_up(value, step):
    return -(-value // step) * step


def from_behind(x, axis):
    count = lax.axis_size(axis)
    return lax.ppermute(x, axis, [(i, i + 1) for i in range(count - 1)])


def from_ahead(x, axis):
    count = lax.axis_size(axis)
    return lax.ppermute(x, axis, [(i + 1, i) for i in range(count - 1)])


def lane_index(shape):
    return lax.broadcasted_iota(jnp.int32, shape, len(shape) - 1)


def pack_lanes(plan, arrays):
    half = LANES // 2

    def kernel(*refs):
        out = refs[-1]
        lane = lane_index((plan.y, LANES))
        in_low_half = lane < half

        def plane(x, _):
            packed = jnp.zeros((plan.y, LANES), jnp.float32)
            for group, component, low, high, _, _, start in plan.fields:
                first, last = refs[2 * group], refs[2 * group + 1]
                edge = jnp.where(in_low_half, first[component, x], last[component, x])
                moved = pltpu.roll(edge, start, 1)
                packed = jnp.where((lane >= start - low) & (lane < start + high), moved, packed)
            out[x] = packed
            return 0

        lax.fori_loop(0, plan.x, plane, 0)

    specs, operands = [], []
    for (count, _, _), array in zip(plan.groups, arrays):
        block = (count, plan.x, plan.y, LANES)
        specs.append(pl.BlockSpec(block, lambda i: (0, 0, 0, 0)))
        specs.append(pl.BlockSpec(block, lambda i: (0, 0, 0, plan.tiles - 1)))
        operands += [array, array]
    return pl.pallas_call(
        kernel,
        grid=(1,),
        in_specs=specs,
        out_specs=pl.BlockSpec((plan.x, plan.y, LANES), lambda i: (0, 0, 0)),
        out_shape=jax.ShapeDtypeStruct((plan.x, plan.y, LANES), jnp.float32),
        compiler_params=pltpu.CompilerParams(vmem_limit_bytes=VMEM_BYTES),
        name="pack_lanes",
    )(*operands)


def exchange_lanes(plan, packed):
    lane = lane_index((1, 1, LANES))
    is_low = functools.reduce(
        jnp.logical_or,
        [(lane >= start - low) & (lane < start) for _, _, low, _, _, _, start in plan.fields],
    )
    count = lax.axis_size("bz")
    if count == 2:
        got = lax.ppermute(packed, "bz", [(0, 1), (1, 0)])
        return jnp.where(is_low == (lax.axis_index("bz") == 1), got, 0.0)
    return jnp.where(is_low, from_behind(packed, "bz"), from_ahead(packed, "bz"))


def fold_planes(plan, planes):
    count = round_up(planes.shape[0], plan.tiles)
    planes = jnp.pad(planes, ((0, count - planes.shape[0]), (0, 0), (0, 0)))
    return jnp.concatenate([planes[t :: plan.tiles] for t in range(plan.tiles)], axis=-1)


def exchange_planes(plan, arrays, packed):
    up, down = [], []
    for (count, low, high), array in zip(plan.groups, arrays):
        up.append(array[:, plan.x - low :].reshape(count * low, plan.y, plan.z))
        down.append(array[:, :high].reshape(count * high, plan.y, plan.z))
    up.append(fold_planes(plan, packed[plan.x - plan.low :]))
    down.append(fold_planes(plan, packed[: plan.high]))
    return (
        from_behind(jnp.concatenate(up, axis=0), "bx"),
        from_ahead(jnp.concatenate(down, axis=0), "bx"),
    )


def pack_rows(plan, arrays, packed, below, above):
    groups = len(plan.groups)

    def kernel(*refs):
        own = refs[: 2 * groups]
        packed_first, packed_last, below_first, below_last, above_first, above_last = refs[
            2 * groups : 2 * groups + 6
        ]
        up, down = refs[-2:]
        up[...] = jnp.zeros(up.shape, jnp.float32)
        down[...] = jnp.zeros(down.shape, jnp.float32)

        def put(plane, field, first, last):
            _, _, low, high, low_at, high_at, _ = field
            up[plane, low_at : low_at + low, :] = last[ROWS - low : ROWS, :]
            down[plane, high_at : high_at + high, :] = first[0:high, :]

        def put_packed(plane, first, last, at):
            for k in range(plan.low):
                row, lanes = plan.folded(k, plan.packed_low_at)
                source = ROWS - plan.low + k
                up[plane, row : row + 1, lanes : lanes + LANES] = last[
                    source : source + 1, at : at + LANES
                ]
            for k in range(plan.high):
                row, lanes = plan.folded(k, plan.packed_high_at)
                down[plane, row : row + 1, lanes : lanes + LANES] = first[
                    k : k + 1, at : at + LANES
                ]

        def own_plane(x, _):
            for field in plan.fields:
                group, component = field[:2]
                put(plan.low + x, field, own[2 * group].at[component, x], own[2 * group + 1].at[component, x])
            put_packed(plan.low + x, packed_first.at[x], packed_last.at[x], 0)
            return 0

        lax.fori_loop(0, plan.x, own_plane, 0)
        for k in range(plan.low):
            for field in plan.fields:
                _, _, low, _, low_at, _, _ = field
                skipped = plan.low - low
                if k >= skipped:
                    source = low_at + k - skipped
                    put(k, field, below_first.at[source], below_last.at[source])
            source, lanes = plan.folded(k, plan.packed_low_at)
            put_packed(k, below_first.at[source], below_last.at[source], lanes)
        for k in range(plan.high):
            for field in plan.fields:
                _, _, _, high, _, high_at, _ = field
                if k < high:
                    source = high_at + k
                    put(plan.low + plan.x + k, field, above_first.at[source], above_last.at[source])
            source, lanes = plan.folded(k, plan.packed_high_at)
            put_packed(plan.low + plan.x + k, above_first.at[source], above_last.at[source], lanes)

    last = plan.y // ROWS - 1
    specs, operands = [], []
    for (count, _, _), array in zip(plan.groups, arrays):
        block = (count, plan.x, ROWS, plan.z)
        specs.append(pl.BlockSpec(block, lambda i: (0, 0, 0, 0)))
        specs.append(pl.BlockSpec(block, lambda i: (0, 0, last, 0)))
        operands += [array, array]
    for array in (packed, below, above):
        block = (array.shape[0], ROWS, array.shape[2])
        specs.append(pl.BlockSpec(block, lambda i: (0, 0, 0)))
        specs.append(pl.BlockSpec(block, lambda i: (0, last, 0)))
        operands += [array, array]
    shapes = [
        (plan.planes, round_up(rows, ROWS), plan.z) for rows in (plan.low_rows, plan.high_rows)
    ]
    return pl.pallas_call(
        kernel,
        grid=(1,),
        in_specs=specs,
        out_specs=[pl.BlockSpec(shape, lambda i: (0, 0, 0)) for shape in shapes],
        out_shape=[jax.ShapeDtypeStruct(shape, jnp.float32) for shape in shapes],
        compiler_params=pltpu.CompilerParams(vmem_limit_bytes=VMEM_BYTES),
        name="pack_rows",
    )(*operands)


def exchange(plan, arrays):
    packed = exchange_lanes(plan, pack_lanes(plan, arrays))
    below, above = exchange_planes(plan, arrays, packed)
    up, down = pack_rows(plan, arrays, packed, below, above)
    return packed, below, above, from_behind(up, "by"), from_ahead(down, "by")


def assemble(plan, arrays, messages, extended, packed_ext, semaphores):
    packed, below, above, left, right = messages
    copies = []

    def copy(source, target):
        copies.append(
            pltpu.make_async_copy(source, target, semaphores.at[len(copies)])
        )
        copies[-1].start()

    own_rows = pl.ds(ROWS, plan.y)
    own_planes = pl.ds(plan.low, plan.x)
    for group, component, low, high, low_at, high_at, _ in plan.fields:
        target = extended[group].at[component]
        for t in range(plan.tiles):
            lanes = pl.ds(t * LANES, LANES)
            copy(arrays[group].at[component, :, :, lanes], target.at[own_planes, t, own_rows, :])
            copy(
                below.at[pl.ds(low_at, low), :, lanes],
                target.at[pl.ds(plan.low - low, low), t, own_rows, :],
            )
            copy(
                above.at[pl.ds(high_at, high), :, lanes],
                target.at[pl.ds(plan.low + plan.x, high), t, own_rows, :],
            )
    copy(packed, packed_ext.at[own_planes, own_rows, :])
    for k in range(plan.low):
        source, lanes = plan.folded(k, plan.packed_low_at)
        copy(below.at[source, :, pl.ds(lanes, LANES)], packed_ext.at[k, own_rows, :])
    for k in range(plan.high):
        source, lanes = plan.folded(k, plan.packed_high_at)
        copy(
            above.at[source, :, pl.ds(lanes, LANES)],
            packed_ext.at[plan.low + plan.x + k, own_rows, :],
        )
    for one in copies:
        one.wait()

    top = ROWS + plan.y

    def plane(i, _):
        for group, component, low, high, low_at, high_at, _ in plan.fields:
            target = extended[group]
            for t in range(plan.tiles):
                lanes = slice(t * LANES, (t + 1) * LANES)
                target[component, i, t, ROWS - low : ROWS, :] = left[i, low_at : low_at + low, lanes]
                target[component, i, t, top : top + high, :] = right[
                    i, high_at : high_at + high, lanes
                ]
        for k in range(plan.low):
            row, lanes = plan.folded(k, plan.packed_low_at)
            to = ROWS - plan.low + k
            packed_ext[i, to : to + 1, :] = left[i, row : row + 1, lanes : lanes + LANES]
        for k in range(plan.high):
            row, lanes = plan.folded(k, plan.packed_high_at)
            packed_ext[i, top + k : top + k + 1, :] = right[i, row : row + 1, lanes : lanes + LANES]
        tile = packed_ext[i]
        for group, component, _, _, _, _, start in plan.fields:
            extended[group][component, i, plan.tiles] = pltpu.roll(tile, (LANES - start) % LANES, 1)
        return 0

    lax.fori_loop(0, plan.planes, plane, 0)


def assemble_copies(plan):
    return len(plan.fields) * plan.tiles * 3 + 1 + plan.low + plan.high


def load(ref, index, row):
    return [ref[(*index, t, pl.ds(row, ROWS), slice(None))] for t in range(ref.shape[-3])]


def store(ref, index, row, tiles):
    for t, tile in enumerate(tiles):
        ref[(*index, t, pl.ds(row, ROWS), slice(None))] = tile


def each(function, *tiles):
    return [function(*one) for one in zip(*tiles)]


def add(first, second):
    return each(lambda a, b: a + b, first, second)


def subtract(first, second):
    return each(lambda a, b: a - b, first, second)


def lane_below(tiles):
    lane = lane_index((ROWS, LANES))
    rolled = [pltpu.roll(tile, 1, 1) for tile in tiles]
    return [jnp.where(lane == 0, rolled[t - 1], rolled[t]) for t in range(len(tiles))]


def lane_above(tiles):
    lane = lane_index((ROWS, LANES))
    rolled = [pltpu.roll(tile, LANES - 1, 1) for tile in tiles]
    count = len(tiles)
    return [
        jnp.where(lane == LANES - 1, rolled[(t + 1) % count], rolled[t]) for t in range(count)
    ]


def chunks(first, last, body):
    count = -(-(last - first + 1) // ROWS)

    def one(j, _):
        body(jnp.minimum(first + j * ROWS, last - ROWS + 1))
        return 0

    lax.fori_loop(0, count, one, 0)


class Inside:
    def __init__(self, plan, flags):
        self.plan = plan
        self.flags = flags

    def tiles(self, row, scale):
        plan, flags = self.plan, self.flags
        rows = row + lax.broadcasted_iota(jnp.int32, (ROWS, LANES), 0)
        keep = jnp.where(rows < ROWS, flags[2], jnp.where(rows >= ROWS + plan.y, flags[3], 1.0))
        lane = lane_index((ROWS, LANES))
        edge = jnp.where(lane < LANES // 2, flags[5], flags[4])
        keep = scale * keep
        return [keep] * plan.tiles + [keep * edge]

    def plane(self, i):
        plan, flags = self.plan, self.flags
        return jnp.where(
            i < plan.low, flags[0], jnp.where(i >= plan.low + plan.x, flags[1], 1.0)
        )


def force_pass(density, energy, force, mass, inside, planes, rows):
    def chunk(row):
        keep = inside.tiles(row, 0.4 * 0.25)

        def slab(i):
            here, under = load(density, (0, i), row), load(density, (0, i), row - 1)
            p = each(lambda a, b: a * b, here, load(energy, (0, i), row))
            p_under = each(lambda a, b: a * b, under, load(energy, (0, i), row - 1))
            summed, stepped = add(p, p_under), subtract(p_under, p)
            weight = add(here, under)
            summed_z, stepped_z = lane_below(summed), lane_below(stepped)
            return (
                add(summed, summed_z),
                add(stepped, stepped_z),
                subtract(summed_z, summed),
                add(weight, lane_below(weight)),
            )

        def plane(i, before):
            now = slab(i)
            here = inside.plane(i)
            scale = [tile * here for tile in keep]
            for component in range(3):
                across = (subtract if component == 0 else add)(before[component], now[component])
                store(force, (component, i), row, each(lambda a, b: a * b, scale, across))
            store(
                mass,
                (0, i),
                row,
                each(lambda a, b: 0.125 * (a + b) + 6.0 * CONSISTENT, before[3], now[3]),
            )
            return now

        lax.fori_loop(planes[0], planes[1] + 1, plane, slab(planes[0] - 1))

    chunks(*rows, chunk)


def face_sum(ref, component, i, row, before, here, after):
    total = add(add(before, after), add(lane_below(here), lane_above(here)))
    return add(total, add(load(ref, (component, i), row - 1), load(ref, (component, i), row + 1)))


def stencil_pass(ref, planes, rows, setup, use):
    def chunk(row):
        given = setup(row)

        def plane(i, carried):
            before, here = carried
            after = [load(ref, (component, i + 1), row) for component in range(3)]
            sums = [
                face_sum(ref, component, i, row, before[component], here[component], after[component])
                for component in range(3)
            ]
            use(i, row, here, sums, given)
            return here, after

        first = [load(ref, (component, planes[0] - 1), row) for component in range(3)]
        second = [load(ref, (component, planes[0]), row) for component in range(3)]
        lax.fori_loop(planes[0], planes[1] + 1, plane, (first, second))

    chunks(*rows, chunk)


def whole_sum(tile):
    return jnp.sum(jnp.sum(tile, axis=0, keepdims=True), axis=1, keepdims=True)


def moments_kernel(plan, *refs):
    flags, density, energy, packed, below, above, left, right, out = refs[:9]
    density_ext, energy_ext, packed_ext, force, image, mass, semaphores = refs[9:]
    assemble(
        plan,
        [density, energy],
        (packed, below, above, left, right),
        [density_ext, energy_ext],
        packed_ext,
        semaphores,
    )
    inside = Inside(plan, flags)
    low, x, y = plan.low, plan.x, plan.y
    force_pass(
        density_ext,
        energy_ext,
        force,
        mass,
        inside,
        (low - 1, low + x + 1),
        (ROWS - 1, ROWS + y + 1),
    )

    def multiply(i, row, here, sums, keep):
        weight = load(mass, (0, i), row)
        scale = [tile * inside.plane(i) for tile in keep]
        for component in range(3):
            result = each(
                lambda m, a, k, s: m * a + k * s, weight, here[component], scale, sums[component]
            )
            store(image, (component, i), row, result)

    stencil_pass(
        force,
        (low, low + x),
        (ROWS, ROWS + y),
        lambda row: inside.tiles(row, CONSISTENT),
        multiply,
    )

    own = range(plan.tiles)
    nothing = jnp.zeros((ROWS, LANES), jnp.float32)

    def first_plane(n, sums):
        i, row = low + n // (y // ROWS), ROWS + (n % (y // ROWS)) * ROWS
        sums = list(sums)
        for component in range(3):
            f = load(force, (component, i), row)
            v = load(image, (component, i), row)
            for t in own:
                sums[component] = sums[component] + f[t] * f[t]
                sums[3 + component] = sums[3 + component] + f[t] * v[t]
        return tuple(sums)

    sums = lax.fori_loop(0, x * (y // ROWS), first_plane, (nothing,) * 6)
    sums = [whole_sum(one) for one in sums]
    square = sums[:3]
    shift = [
        jnp.where(square[c] > 0, sums[3 + c] / jnp.where(square[c] > 0, square[c], 1.0), 0.0)
        for c in range(3)
    ]

    def pair(component, i, row):
        f = load(force, (component, i), row)
        v = load(image, (component, i), row)
        return f, each(lambda a, b: a - shift[component] * b, v, f)

    def second_chunk(j, sums):
        row = ROWS + j * ROWS

        def plane(i, carried):
            here, sums = carried
            sums = list(sums)
            ahead = [pair(component, i + 1, row) for component in range(3)]
            weight = load(mass, (0, i), row)
            for component in range(3):
                f, w = here[component]
                f_next, w_next = ahead[component]
                f_up, w_up = pair(component, i, row + 1)
                f_high = add(add(f_next, f_up), lane_above(f))
                w_high = add(add(w_next, w_up), lane_above(w))
                for t in own:
                    at = 4 * component
                    heavy = weight[t] * w[t]
                    sums[at] = sums[at] + f[t] * w[t]
                    sums[at + 1] = sums[at + 1] + w[t] * w[t]
                    sums[at + 2] = sums[at + 2] + (
                        f[t] * heavy + CONSISTENT * (f[t] * w_high[t] + w[t] * f_high[t])
                    )
                    sums[at + 3] = sums[at + 3] + w[t] * (
                        heavy + (2.0 * CONSISTENT) * w_high[t]
                    )
            return ahead, tuple(sums)

        start = [pair(component, low, row) for component in range(3)]
        return lax.fori_loop(low, low + x, plane, (start, sums))[1]

    rest = lax.fori_loop(0, y // ROWS, second_chunk, (nothing,) * 12)
    lane = lane_index((1, LANES))
    line = jnp.zeros((1, LANES), jnp.float32)
    for c in range(3):
        values = [shift[c], square[c]] + [whole_sum(one) for one in rest[4 * c : 4 * c + 4]]
        for k, value in enumerate(values):
            line = jnp.where(lane == 3 * k + c, value, line)
    out[...] = line


def solve_weights(sums):
    rows = sums.shape[0]
    got = [sums if k == 0 else pltpu.roll(sums, LANES - 3 * k, 1) for k in range(MOMENTS)]
    c, p0, q1, q2, q3, q4 = got

    def total(value):
        return jnp.sum(value, axis=0, keepdims=True)

    norm_now = total(p0)
    alpha = norm_now / total(q1 + c * p0)
    a = 1.0 - alpha * c
    norm_next = total(a * a * p0 - 2.0 * a * alpha * q1 + alpha * alpha * q2)
    product = total(a * a * (q1 + c * p0) - a * alpha * (q3 + q2 + c * q1) + alpha * alpha * q4)
    ratio = norm_next / norm_now
    later = norm_next / (product - ratio * norm_next / alpha)
    lane = lane_index((1, LANES))

    def pick(value, component):
        return jnp.sum(jnp.where(lane == component, value, 0.0), axis=1, keepdims=True)

    on_force, on_image = alpha + later * (1.0 + ratio), -later * alpha
    return [(pick(on_force, k), pick(on_image, k)) for k in range(3)]


def step_kernel(plan, *refs):
    flags, sums, density, energy, base, velocity, free = refs[:7]
    messages = refs[7:12]
    velocity_new, accel, relaxed, density_new, energy_new = refs[12:17]
    (
        density_ext,
        energy_ext,
        moved,
        speed,
        free_ext,
        packed_ext,
        force,
        mass,
        other,
        semaphores,
        out_semaphores,
    ) = refs[17:]
    assemble(
        plan,
        [density, energy, base, velocity, free],
        messages,
        [density_ext, energy_ext, moved, speed, free_ext],
        packed_ext,
        semaphores,
    )
    inside = Inside(plan, flags)
    low, x, y = plan.low, plan.x, plan.y
    weights = solve_weights(sums[...])
    reach = SWEEPS + 1
    force_pass(
        density_ext,
        energy_ext,
        force,
        mass,
        inside,
        (low - reach, low + x + reach),
        (ROWS - reach, ROWS + y + reach),
    )

    def advance(i, row, here, sums, keep):
        weight = load(mass, (0, i), row)
        scale = [tile * inside.plane(i) for tile in keep]
        for component in range(3):
            on_force, on_image = weights[component]
            result = each(
                lambda m, a, k, s: on_force * a + on_image * (m * a + k * s),
                weight,
                here[component],
                scale,
                sums[component],
            )
            store(other, (component, i), row, result)
            at = (component, i)
            store(speed, at, row, each(lambda v, a: v + TIME_STEP * a, load(speed, at, row), result))
            store(
                moved,
                at,
                row,
                each(lambda b, a: b + (TIME_STEP * TIME_STEP) * a, load(moved, at, row), result),
            )

    reach -= 1
    advanced = round_up(y + 2 * reach + 1, ROWS)
    stencil_pass(
        force,
        (low - reach, low + x + reach),
        (ROWS - reach, ROWS - reach + advanced - 1),
        lambda row: inside.tiles(row, CONSISTENT),
        advance,
    )

    out_copies = []

    def write(source, target, component, result=None):
        for t in range(plan.tiles):
            place = target if result is None else target.at[result]
            out_copies.append(
                pltpu.make_async_copy(
                    source.at[component, pl.ds(low, x), t, pl.ds(ROWS, y), :],
                    place.at[:, :, pl.ds(t * LANES, LANES)],
                    out_semaphores.at[len(out_copies)],
                )
            )
            out_copies[-1].start()

    for component in range(3):
        write(other, accel, component, component)
    accel_copies = len(out_copies)
    for component in range(3):
        write(speed, velocity_new, component, component)

    content = mass

    def content_chunk(row):
        def slab(i):
            under = [load(speed, (component, i), row) for component in range(3)]
            over = [load(speed, (component, i), row + 1) for component in range(3)]
            along_x = add(under[0], over[0])
            along_y = subtract(over[1], under[1])
            along_z = add(under[2], over[2])
            along_x = add(along_x, lane_above(along_x))
            along_y = add(along_y, lane_above(along_y))
            along_z = subtract(lane_above(along_z), along_z)
            return along_x, add(along_y, along_z)

        def plane(i, before):
            now = slab(i + 1)
            spread = add(subtract(now[0], before[0]), add(now[1], before[1]))
            held = load(energy_ext, (0, i), row)
            lagged = each(lambda e, s: e - (0.25 * 0.4 * TIME_STEP) * (e * s), held, spread)
            store(
                content, (0, i), row, each(lambda d, e: d * e, load(density_ext, (0, i), row), lagged)
            )
            return now

        lax.fori_loop(low - 1, low + x + 1, plane, slab(low - 1))

    chunks(ROWS - 1, ROWS + y, content_chunk)

    for one in out_copies[:accel_copies]:
        one.wait()
    source, target = moved, other
    for _ in range(SWEEPS):
        reach -= 1

        def relax(i, row, here, sums, given, target=target):
            rate = load(free_ext, (0, i), row)
            for component in range(3):
                result = each(
                    lambda r, s, f: r + f * (s * (1.0 / 6.0) - r),
                    here[component],
                    sums[component],
                    rate,
                )
                store(target, (component, i), row, result)

        stencil_pass(
            source,
            (low - reach, low + x + reach),
            (ROWS - reach, ROWS + y + reach),
            lambda row: None,
            relax,
        )
        source, target = target, (force if target is other else other)
    settled, free_buffer = source, target
    for component in range(3):
        write(settled, relaxed, component, component)

    quantities = (density_ext, content)

    def remap_chunk(row):
        def shift(component, i, at):
            return subtract(
                load(settled, (component, i), at), load(moved, (component, i), at)
            )

        def slab(i):
            x_here = add(shift(0, i, row), shift(0, i, row + 1))
            y_here, y_over = shift(1, i, row), shift(1, i, row + 1)
            z_here = add(shift(2, i, row), shift(2, i, row + 1))
            return (
                add(x_here, lane_above(x_here)),
                add(y_here, lane_above(y_here)),
                add(y_over, lane_above(y_over)),
                z_here,
                [load(one, (0, i), row) for one in quantities],
            )

        def flux(speeds, upper, lower):
            return each(lambda s, u, l: s * jnp.where(s > 0, u, l), speeds, upper, lower)

        def x_flux(speeds, upper, lower):
            return [flux(speeds, u, l) for u, l in zip(upper, lower)]

        def plane(i, carried):
            now, entering = carried
            ahead = slab(i + 1)
            leaving = x_flux(ahead[0], ahead[4], now[4])
            y_here, y_over, z_here = [add(now[k], ahead[k]) for k in (1, 2, 3)]
            for k, one in enumerate(quantities):
                held = now[4][k]
                under, over = load(one, (0, i), row - 1), load(one, (0, i), row + 1)
                through_z = flux(z_here, held, lane_below(held))
                change = subtract(leaving[k], entering[k])
                change = add(change, flux(y_over, over, held))
                change = subtract(change, flux(y_here, held, under))
                change = add(change, subtract(lane_above(through_z), through_z))
                result = each(lambda q, c: q + 0.25 * c, held, change)
                store(free_buffer, (k, i), row, result[: plan.tiles])
            return ahead, leaving

        start = slab(low)
        before = [load(one, (0, low - 1), row) for one in quantities]
        lax.fori_loop(low, low + x, plane, (start, x_flux(start[0], start[4], before)))

    chunks(ROWS, ROWS + y - 1, remap_chunk)
    write(free_buffer, density_new, 0)
    write(free_buffer, energy_new, 1)
    for one in out_copies[accel_copies:]:
        one.wait()


def gather_lines(line):
    for axis in ("bz", "by", "bx"):
        count = lax.axis_size(axis)
        if count & (count - 1):
            line = lax.all_gather(line, axis, axis=0, tiled=True)
            continue
        step = 1
        while step < count:
            got = lax.ppermute(line, axis, [(i, i ^ step) for i in range(count)])
            later = (lax.axis_index(axis) // step) % 2 == 1
            line = jnp.concatenate([jnp.where(later, got, line), jnp.where(later, line, got)])
            step *= 2
    return line


def any_space():
    return pl.BlockSpec(memory_space=pl.ANY)


def in_vmem():
    return pl.BlockSpec(memory_space=pltpu.VMEM)


def in_smem():
    return pl.BlockSpec(memory_space=pltpu.SMEM)


def extended_scratch(plan, count):
    return pltpu.VMEM((count, plan.planes, plan.tiles + 1, plan.rows, LANES), jnp.float32)


def message_specs():
    return [any_space()] * 3 + [in_vmem()] * 2


def on_device(position, velocity, density, energy, pinned):
    shape = density.shape
    density, energy = density[None], energy[None]
    flags = jnp.stack(
        [
            jnp.float32(limit)
            for axis in ("bx", "by", "bz")
            for limit in (
                lax.axis_index(axis) > 0,
                lax.axis_index(axis) < lax.axis_size(axis) - 1,
            )
        ]
    )

    narrow = Plan([(1, NARROW, NARROW)] * 2, shape)
    line = pl.pallas_call(
        functools.partial(moments_kernel, narrow),
        in_specs=[in_smem()] + [any_space()] * 2 + message_specs(),
        out_specs=in_vmem(),
        out_shape=jax.ShapeDtypeStruct((1, LANES), jnp.float32),
        scratch_shapes=[
            extended_scratch(narrow, 1),
            extended_scratch(narrow, 1),
            pltpu.VMEM((narrow.planes, narrow.rows, LANES), jnp.float32),
            extended_scratch(narrow, 3),
            extended_scratch(narrow, 3),
            extended_scratch(narrow, 1),
            pltpu.SemaphoreType.DMA((assemble_copies(narrow),)),
        ],
        compiler_params=pltpu.CompilerParams(vmem_limit_bytes=VMEM_BYTES),
        name="moments",
    )(flags, density, energy, *exchange(narrow, [density, energy]))

    base = position + TIME_STEP * velocity
    free = (RELAX_RATE * (1.0 - pinned.astype(jnp.float32)))[None]
    wide = Plan(
        [
            (1, WIDE, WIDE),
            (1, WIDE, WIDE),
            (3, SWEEPS, SWEEPS + 1),
            (3, 1, 2),
            (1, SWEEPS - 1, SWEEPS),
        ],
        shape,
    )
    arrays = [density, energy, base, velocity, free]
    messages = exchange(wide, arrays)
    nodes = jax.ShapeDtypeStruct((3, *shape), jnp.float32)
    cells = jax.ShapeDtypeStruct(shape, jnp.float32)
    return pl.pallas_call(
        functools.partial(step_kernel, wide),
        in_specs=[in_smem(), in_vmem()] + [any_space()] * 5 + message_specs(),
        out_specs=[any_space()] * 5,
        out_shape=[nodes, nodes, nodes, cells, cells],
        scratch_shapes=[
            extended_scratch(wide, 1),
            extended_scratch(wide, 1),
            extended_scratch(wide, 3),
            extended_scratch(wide, 3),
            extended_scratch(wide, 1),
            pltpu.VMEM((wide.planes, wide.rows, LANES), jnp.float32),
            extended_scratch(wide, 3),
            extended_scratch(wide, 1),
            extended_scratch(wide, 3),
            pltpu.SemaphoreType.DMA((assemble_copies(wide),)),
            pltpu.SemaphoreType.DMA((11 * wide.tiles,)),
        ],
        compiler_params=pltpu.CompilerParams(vmem_limit_bytes=VMEM_BYTES),
        name="step",
    )(flags, gather_lines(line), *arrays, *messages)


def solution(mesh):
    in_specs = (
        P(None, "bx", "by", "bz"),
        P(None, "bx", "by", "bz"),
        P("bx", "by", "bz"),
        P("bx", "by", "bz"),
        P("bx", "by", "bz"),
    )
    out_specs = (
        P(None, "bx", "by", "bz"),
        P(None, "bx", "by", "bz"),
        P(None, "bx", "by", "bz"),
        P("bx", "by", "bz"),
        P("bx", "by", "bz"),
    )
    return jax.shard_map(
        on_device, mesh=mesh, in_specs=in_specs, out_specs=out_specs, check_vma=False
    )
```

```python
import functools

import jax
import jax.numpy as jnp
from jax import lax
from jax.experimental import pallas as pl
from jax.experimental.pallas import tpu as pltpu
from jax.sharding import PartitionSpec as P

SWEEPS = 3
TIME_STEP = 0.6
RELAX_RATE = 0.8
CONSISTENT = 0.2

LANES = 128
ROWS = 8
MOMENTS = 7
UNROLL = 4
POSITION, VELOCITY, PINNED = 2, 3, 4
NARROW = 2
WIDE = SWEEPS + 2
VMEM_BYTES = 62 * 2**20


class Plan:
    def __init__(self, groups, shape, starts=None):
        self.groups = groups
        self.x, self.y, self.z = shape
        self.tiles = self.z // LANES
        self.low = max(low for _, low, _ in groups)
        self.high = max(high for _, _, high in groups)
        self.planes = self.low + self.x + self.high
        self.rows = self.y + 2 * ROWS
        self.fields = []
        low_at = high_at = lane_at = 0
        for group, (count, low, high) in enumerate(groups):
            for component in range(count):
                start = lane_at + low if starts is None else starts[len(self.fields)]
                self.fields.append((group, component, low, high, low_at, high_at, start))
                low_at += low
                high_at += high
                lane_at += low + high
        assert lane_at <= LANES
        self.starts = [field[-1] for field in self.fields]
        self.packed_low_at, self.packed_high_at = low_at, high_at
        self.low_rows = low_at + -(-self.low // self.tiles)
        self.high_rows = high_at + -(-self.high // self.tiles)

    def value(self, group, component, get):
        if group == POSITION:
            return get(POSITION, component) + TIME_STEP * get(VELOCITY, component)
        if group == PINNED:
            return RELAX_RATE * (1.0 - get(PINNED, component).astype(jnp.float32))
        return get(group, component)

    def folded(self, k, at):
        return at + k // self.tiles, (k % self.tiles) * LANES


def round_up(value, step):
    return -(-value // step) * step


def from_behind(x, axis):
    count = lax.axis_size(axis)
    return lax.ppermute(x, axis, [(i, i + 1) for i in range(count - 1)])


def from_ahead(x, axis):
    count = lax.axis_size(axis)
    return lax.ppermute(x, axis, [(i + 1, i) for i in range(count - 1)])


def any_space():
    return pl.BlockSpec(memory_space=pl.ANY)


def in_vmem():
    return pl.BlockSpec(memory_space=pltpu.VMEM)


def in_smem():
    return pl.BlockSpec(memory_space=pltpu.SMEM)


def cost(microseconds):
    return pl.CostEstimate(
        flops=0, bytes_accessed=int(microseconds * 3.0e6), transcendentals=0
    )


def lane_index(shape):
    return lax.broadcasted_iota(jnp.int32, shape, len(shape) - 1)


def pack_lanes(plan, arrays):
    half = LANES // 2

    def kernel(*refs):
        out = refs[-1]
        lane = lane_index((plan.y, LANES))
        in_low_half = lane < half

        def plane(x, _):
            def edge(group, component):
                first, last = refs[2 * group], refs[2 * group + 1]
                return jnp.where(in_low_half, first[component, x], last[component, x])

            packed = jnp.zeros((plan.y, LANES), jnp.float32)
            for group, component, low, high, _, _, start in plan.fields:
                moved = pltpu.roll(plan.value(group, component, edge), start, 1)
                packed = jnp.where((lane >= start - low) & (lane < start + high), moved, packed)
            out[x] = packed
            return 0

        lax.fori_loop(0, plan.x, plane, 0)

    specs, operands = [], []
    for (count, _, _), array in zip(plan.groups, arrays):
        block = (count, plan.x, plan.y, LANES)
        specs.append(pl.BlockSpec(block, lambda i: (0, 0, 0, 0)))
        specs.append(pl.BlockSpec(block, lambda i: (0, 0, 0, plan.tiles - 1)))
        operands += [array, array]
    return pl.pallas_call(
        kernel,
        grid=(1,),
        in_specs=specs,
        out_specs=pl.BlockSpec((plan.x, plan.y, LANES), lambda i: (0, 0, 0)),
        out_shape=jax.ShapeDtypeStruct((plan.x, plan.y, LANES), jnp.float32),
        compiler_params=pltpu.CompilerParams(vmem_limit_bytes=VMEM_BYTES),
        cost_estimate=cost(6),
        name="pack_lanes",
    )(*operands)


def exchange_lanes(plan, packed):
    lane = lane_index((1, 1, LANES))
    is_low = functools.reduce(
        jnp.logical_or,
        [(lane >= start - low) & (lane < start) for _, _, low, _, _, _, start in plan.fields],
    )
    count = lax.axis_size("bz")
    if count == 2:
        got = lax.ppermute(packed, "bz", [(0, 1), (1, 0)])
        return jnp.where(is_low == (lax.axis_index("bz") == 1), got, 0.0)
    return jnp.where(is_low, from_behind(packed, "bz"), from_ahead(packed, "bz"))


def pack_planes(plan, arrays, packed):
    sizes = [plan.low_rows, plan.high_rows]
    needed = [
        max(low if to_low else high for _, low, high in plan.groups) for to_low in (True, False)
    ]
    depths = [(low, high) for _, low, high in plan.groups]
    if len(depths) > VELOCITY:
        depths[VELOCITY] = depths[POSITION]

    def kernel(*refs):
        groups = len(plan.groups)
        own, packed_ref, outs = refs[:groups], refs[groups], refs[groups + 1 : groups + 3]
        edges, semaphores = refs[groups + 3 : -1], refs[-1]
        copies = []

        def copy(source, target):
            copies.append(pltpu.make_async_copy(source, target, semaphores.at[len(copies)]))
            copies[-1].start()

        for side, out in enumerate(outs):
            for group, array in enumerate(own):
                depth = depths[group][side]
                planes = pl.ds(plan.x - depth, depth) if side == 0 else pl.ds(0, depth)
                copy(array.at[:, planes], edges[2 * group + side])
            first = plan.x - needed[0] if side == 0 else 0
            at = (plan.packed_low_at, plan.packed_high_at)[side]
            for k in range(needed[side]):
                row, lanes = plan.folded(k, at)
                copy(packed_ref.at[first + k], out.at[row, :, pl.ds(lanes, LANES)])
        for one in copies:
            one.wait()
        for side, out in enumerate(outs):
            for field in plan.fields:
                group, component = field[:2]
                depth, at = field[2 + side], field[4 + side]

                def get(argument, part):
                    held = edges[2 * argument + side]
                    skip = depths[argument][0] - depth if side == 0 else 0
                    return held[part, skip : skip + depth]

                out[at : at + depth] = plan.value(group, component, get)

    shapes = [(size, plan.y, plan.z) for size in sizes]
    scratch = [
        pltpu.VMEM((array.shape[0], depth, plan.y, plan.z), array.dtype)
        for array, pair in zip(arrays, depths)
        for depth in pair
    ]
    count = 2 * len(arrays) + sum(needed)
    return pl.pallas_call(
        kernel,
        in_specs=[any_space()] * (len(arrays) + 1),
        out_specs=[in_vmem()] * 2,
        out_shape=[jax.ShapeDtypeStruct(shape, jnp.float32) for shape in shapes],
        scratch_shapes=scratch + [pltpu.SemaphoreType.DMA((count,))],
        compiler_params=pltpu.CompilerParams(vmem_limit_bytes=VMEM_BYTES),
        cost_estimate=cost(3),
        name="pack_planes",
    )(*arrays, packed)


def row_shapes(plan, planes):
    return [(planes, round_up(rows, ROWS), plan.z) for rows in (plan.low_rows, plan.high_rows)]


def pack_rows(plan, arrays, packed, below, above, own, halo):
    groups = len(plan.groups)

    def kernel(*refs):
        refs = list(refs)
        up, down = refs[-2:]
        up[...] = jnp.zeros(up.shape, jnp.float32)
        down[...] = jnp.zeros(down.shape, jnp.float32)

        def put(plane, field, first, last):
            _, _, low, high, low_at, high_at, _ = field
            up[plane, low_at : low_at + low, :] = last[ROWS - low : ROWS, :]
            down[plane, high_at : high_at + high, :] = first[0:high, :]

        def put_packed(plane, first, last, at):
            for k in range(plan.low):
                row, lanes = plan.folded(k, plan.packed_low_at)
                source = ROWS - plan.low + k
                up[plane, row : row + 1, lanes : lanes + LANES] = last[
                    source : source + 1, at : at + LANES
                ]
            for k in range(plan.high):
                row, lanes = plan.folded(k, plan.packed_high_at)
                down[plane, row : row + 1, lanes : lanes + LANES] = first[
                    k : k + 1, at : at + LANES
                ]

        base = 0
        if own:
            blocks = refs[: 2 * groups + 2]
            del refs[: 2 * groups + 2]
            base = plan.x

            def own_plane(x, _):
                for field in plan.fields:
                    first, last = [
                        plan.value(
                            *field[:2],
                            lambda argument, part: blocks[2 * argument + side][part, x],
                        )
                        for side in range(2)
                    ]
                    put(x, field, first, last)
                put_packed(x, blocks[-2].at[x], blocks[-1].at[x], 0)
                return 0

            lax.fori_loop(0, plan.x, own_plane, 0)
        if halo:
            below_first, below_last, above_first, above_last = refs[:4]
            for k in range(plan.low):
                for field in plan.fields:
                    _, _, low, _, low_at, _, _ = field
                    skipped = plan.low - low
                    if k >= skipped:
                        source = low_at + k - skipped
                        put(base + k, field, below_first.at[source], below_last.at[source])
                source, lanes = plan.folded(k, plan.packed_low_at)
                put_packed(base + k, below_first.at[source], below_last.at[source], lanes)
            base += plan.low
            for k in range(plan.high):
                for field in plan.fields:
                    _, _, _, high, _, high_at, _ = field
                    if k < high:
                        source = high_at + k
                        put(base + k, field, above_first.at[source], above_last.at[source])
                source, lanes = plan.folded(k, plan.packed_high_at)
                put_packed(base + k, above_first.at[source], above_last.at[source], lanes)

    last = plan.y // ROWS - 1
    specs, operands = [], []
    if own:
        for array in arrays:
            block = (array.shape[0], plan.x, ROWS, plan.z)
            specs.append(pl.BlockSpec(block, lambda i: (0, 0, 0, 0)))
            specs.append(pl.BlockSpec(block, lambda i: (0, 0, last, 0)))
            operands += [array, array]
    for array in ([packed] if own else []) + ([below, above] if halo else []):
        block = (array.shape[0], ROWS, array.shape[2])
        specs.append(pl.BlockSpec(block, lambda i: (0, 0, 0)))
        specs.append(pl.BlockSpec(block, lambda i: (0, last, 0)))
        operands += [array, array]
    shapes = row_shapes(plan, plan.x * own + (plan.low + plan.high) * halo)
    return pl.pallas_call(
        kernel,
        grid=(1,),
        in_specs=specs,
        out_specs=[pl.BlockSpec(shape, lambda i: (0, 0, 0)) for shape in shapes],
        out_shape=[jax.ShapeDtypeStruct(shape, jnp.float32) for shape in shapes],
        compiler_params=pltpu.CompilerParams(vmem_limit_bytes=VMEM_BYTES),
        cost_estimate=cost(4),
        name="pack_rows",
    )(*operands)


def exchange(axis, pair):
    return [from_behind(pair[0], axis), from_ahead(pair[1], axis)]


def assemble(plan, arrays, messages, extended, packed_ext, pinned_own, semaphores):
    packed, below, above = messages[:3]
    if len(messages) == 5:
        sides = [(messages[3], messages[3], plan.x), (messages[4], messages[4], plan.x)]
    else:
        sides = [(messages[3], messages[5], 0), (messages[4], messages[6], 0)]
    copies = []

    def copy(source, target):
        copies.append(
            pltpu.make_async_copy(source, target, semaphores.at[len(copies)])
        )
        copies[-1].start()

    own_rows = pl.ds(ROWS, plan.y)
    own_planes = pl.ds(plan.low, plan.x)
    for group, component, low, high, low_at, high_at, _ in plan.fields:
        target = extended[group].at[component]
        for t in range(plan.tiles):
            lanes = pl.ds(t * LANES, LANES)
            place = target.at[own_planes, t, own_rows, :]
            if group == PINNED:
                place = pinned_own.at[:, t]
            copy(arrays[group].at[component, :, :, lanes], place)
            copy(
                below.at[pl.ds(low_at, low), :, lanes],
                target.at[pl.ds(plan.low - low, low), t, own_rows, :],
            )
            copy(
                above.at[pl.ds(high_at, high), :, lanes],
                target.at[pl.ds(plan.low + plan.x, high), t, own_rows, :],
            )
    copy(packed, packed_ext.at[own_planes, own_rows, :])
    for k in range(plan.low):
        source, lanes = plan.folded(k, plan.packed_low_at)
        copy(below.at[source, :, pl.ds(lanes, LANES)], packed_ext.at[k, own_rows, :])
    for k in range(plan.high):
        source, lanes = plan.folded(k, plan.packed_high_at)
        copy(
            above.at[source, :, pl.ds(lanes, LANES)],
            packed_ext.at[plan.low + plan.x + k, own_rows, :],
        )
    for one in copies:
        one.wait()

    top = ROWS + plan.y

    def fill(i, left, right, at):
        for group, component, low, high, low_at, high_at, _ in plan.fields:
            target = extended[group]
            for t in range(plan.tiles):
                lanes = slice(t * LANES, (t + 1) * LANES)
                target[component, i, t, ROWS - low : ROWS, :] = left[at, low_at : low_at + low, lanes]
                target[component, i, t, top : top + high, :] = right[
                    at, high_at : high_at + high, lanes
                ]
        for k in range(plan.low):
            row, lanes = plan.folded(k, plan.packed_low_at)
            to = ROWS - plan.low + k
            packed_ext[i, to : to + 1, :] = left[at, row : row + 1, lanes : lanes + LANES]
        for k in range(plan.high):
            row, lanes = plan.folded(k, plan.packed_high_at)
            packed_ext[i, top + k : top + k + 1, :] = right[at, row : row + 1, lanes : lanes + LANES]
        tile = packed_ext[i]
        for group, component, _, _, _, _, start in plan.fields:
            extended[group][component, i, plan.tiles] = pltpu.roll(tile, (LANES - start) % LANES, 1)

    def own_plane(x, _):
        i = plan.low + x
        if pinned_own is not None:
            for t in range(plan.tiles):
                at = (i, t, slice(ROWS, top))

                def get(argument, component):
                    if argument == PINNED:
                        return pinned_own[x, t]
                    return extended[argument][(component, *at)]

                for group, component in [(POSITION, c) for c in range(3)] + [(PINNED, 0)]:
                    extended[group][(component, *at)] = plan.value(group, component, get)
        fill(i, sides[0][0], sides[1][0], x)
        return 0

    def low_plane(k, _):
        fill(k, sides[0][1], sides[1][1], sides[0][2] + k)
        return 0

    def high_plane(k, _):
        at = sides[0][2] + plan.low + k
        fill(plan.low + plan.x + k, sides[0][1], sides[1][1], at)
        return 0

    lax.fori_loop(0, plan.x, own_plane, 0)
    lax.fori_loop(0, plan.low, low_plane, 0)
    lax.fori_loop(0, plan.high, high_plane, 0)


def assemble_copies(plan):
    return len(plan.fields) * plan.tiles * 3 + 1 + plan.low + plan.high


def plane_loop(first, last, body, carried):
    def turn(i, carried, count):
        pending = []
        for k in range(count):
            carried, stores = body(i + k, carried)
            pending += stores
        for one in pending:
            store(*one)
        return carried

    count = last - first + 1
    carried = lax.fori_loop(
        0, count // UNROLL, lambda j, c: turn(first + j * UNROLL, c, UNROLL), carried
    )
    rest = count % UNROLL
    return turn(last + 1 - rest, carried, rest) if rest else carried


def load(ref, index, row):
    return [ref[(*index, t, pl.ds(row, ROWS), slice(None))] for t in range(ref.shape[-3])]


def store(ref, index, row, tiles):
    for t, tile in enumerate(tiles):
        ref[(*index, t, pl.ds(row, ROWS), slice(None))] = tile


def each(function, *tiles):
    return [function(*one) for one in zip(*tiles)]


def add(first, second):
    return each(lambda a, b: a + b, first, second)


def subtract(first, second):
    return each(lambda a, b: a - b, first, second)


def lane_below(tiles):
    lane = lane_index((ROWS, LANES))
    rolled = [pltpu.roll(tile, 1, 1) for tile in tiles]
    return [jnp.where(lane == 0, rolled[t - 1], rolled[t]) for t in range(len(tiles))]


def lane_above(tiles):
    lane = lane_index((ROWS, LANES))
    rolled = [pltpu.roll(tile, LANES - 1, 1) for tile in tiles]
    count = len(tiles)
    return [
        jnp.where(lane == LANES - 1, rolled[(t + 1) % count], rolled[t]) for t in range(count)
    ]


def chunks(first, last, body):
    count = -(-(last - first + 1) // ROWS)

    def one(j, _):
        body(jnp.minimum(first + j * ROWS, last - ROWS + 1))
        return 0

    lax.fori_loop(0, count, one, 0)


class Inside:
    def __init__(self, plan, flags):
        self.plan = plan
        self.flags = flags

    def tiles(self, row, scale):
        plan, flags = self.plan, self.flags
        rows = row + lax.broadcasted_iota(jnp.int32, (ROWS, LANES), 0)
        keep = jnp.where(rows < ROWS, flags[2], jnp.where(rows >= ROWS + plan.y, flags[3], 1.0))
        lane = lane_index((ROWS, LANES))
        edge = jnp.where(lane < LANES // 2, flags[5], flags[4])
        keep = scale * keep
        return [keep] * plan.tiles + [keep * edge]

    def plane(self, i):
        plan, flags = self.plan, self.flags
        return jnp.where(
            i < plan.low, flags[0], jnp.where(i >= plan.low + plan.x, flags[1], 1.0)
        )


def force_pass(density, energy, force, mass, inside, planes, rows):
    def chunk(row):
        keep = inside.tiles(row, 0.4 * 0.25)

        def slab(i):
            here, under = load(density, (0, i), row), load(density, (0, i), row - 1)
            p = each(lambda a, b: a * b, here, load(energy, (0, i), row))
            p_under = each(lambda a, b: a * b, under, load(energy, (0, i), row - 1))
            summed, stepped = add(p, p_under), subtract(p_under, p)
            weight = add(here, under)
            summed_z, stepped_z = lane_below(summed), lane_below(stepped)
            return (
                add(summed, summed_z),
                add(stepped, stepped_z),
                subtract(summed_z, summed),
                add(weight, lane_below(weight)),
            )

        def plane(i, before):
            now = slab(i)
            here = inside.plane(i)
            scale = [tile * here for tile in keep]
            stores = []
            for component in range(3):
                across = (subtract if component == 0 else add)(before[component], now[component])
                result = each(lambda a, b: a * b, scale, across)
                stores.append((force, (component, i), row, result))
            result = each(lambda a, b: 0.125 * (a + b) + 6.0 * CONSISTENT, before[3], now[3])
            stores.append((mass, (0, i), row, result))
            return now, stores

        plane_loop(*planes, plane, slab(planes[0] - 1))

    chunks(*rows, chunk)


def face_sum(ref, component, i, row, before, here, after):
    total = add(add(before, after), add(lane_below(here), lane_above(here)))
    return add(total, add(load(ref, (component, i), row - 1), load(ref, (component, i), row + 1)))


def stencil_pass(ref, planes, rows, setup, use):
    def chunk(row):
        given = setup(row)

        def plane(i, carried):
            before, here = carried
            after = [load(ref, (component, i + 1), row) for component in range(3)]
            sums = [
                face_sum(ref, component, i, row, before[component], here[component], after[component])
                for component in range(3)
            ]
            return (here, after), use(i, row, here, sums, given)

        first = [load(ref, (component, planes[0] - 1), row) for component in range(3)]
        second = [load(ref, (component, planes[0]), row) for component in range(3)]
        plane_loop(*planes, plane, (first, second))

    chunks(*rows, chunk)


def whole_sum(tile):
    return jnp.sum(jnp.sum(tile, axis=0, keepdims=True), axis=1, keepdims=True)


def moments_kernel(plan, *refs):
    flags, density, energy = refs[:3]
    messages, out = refs[3:8], refs[8]
    density_ext, energy_ext, packed_ext, force, image, mass, semaphores = refs[9:]
    assemble(
        plan,
        [density, energy],
        messages,
        [density_ext, energy_ext],
        packed_ext,
        None,
        semaphores,
    )
    inside = Inside(plan, flags)
    low, x, y = plan.low, plan.x, plan.y
    force_pass(
        density_ext,
        energy_ext,
        force,
        mass,
        inside,
        (low - 1, low + x + 1),
        (ROWS - 1, ROWS + y + 1),
    )

    def multiply(i, row, here, sums, keep):
        weight = load(mass, (0, i), row)
        scale = [tile * inside.plane(i) for tile in keep]
        stores = []
        for component in range(3):
            result = each(
                lambda m, a, k, s: m * a + k * s, weight, here[component], scale, sums[component]
            )
            stores.append((image, (component, i), row, result))
        return stores

    stencil_pass(
        force,
        (low, low + x),
        (ROWS, ROWS + y),
        lambda row: inside.tiles(row, CONSISTENT),
        multiply,
    )

    own = range(plan.tiles)
    nothing = jnp.zeros((ROWS, LANES), jnp.float32)

    def first_chunk(j, sums):
        row = ROWS + j * ROWS

        def plane(i, sums):
            sums = list(sums)
            for component in range(3):
                f = load(force, (component, i), row)
                v = load(image, (component, i), row)
                for t in own:
                    sums[component] = sums[component] + f[t] * f[t]
                    sums[3 + component] = sums[3 + component] + f[t] * v[t]
            return tuple(sums), []

        return plane_loop(low, low + x - 1, plane, sums)

    sums = lax.fori_loop(0, y // ROWS, first_chunk, (nothing,) * 6)
    sums = [whole_sum(one) for one in sums]
    square = sums[:3]
    shift = [
        jnp.where(square[c] > 0, sums[3 + c] / jnp.where(square[c] > 0, square[c], 1.0), 0.0)
        for c in range(3)
    ]

    def pair(component, i, row):
        f = load(force, (component, i), row)
        v = load(image, (component, i), row)
        return f, each(lambda a, b: a - shift[component] * b, v, f)

    def second_chunk(j, sums):
        row = ROWS + j * ROWS

        def plane(i, carried):
            here, sums = carried
            sums = list(sums)
            ahead = [pair(component, i + 1, row) for component in range(3)]
            weight = load(mass, (0, i), row)
            for component in range(3):
                f, w = here[component]
                f_next, w_next = ahead[component]
                f_up, w_up = pair(component, i, row + 1)
                f_high = add(add(f_next, f_up), lane_above(f))
                w_high = add(add(w_next, w_up), lane_above(w))
                for t in own:
                    at = 5 * component
                    heavy = weight[t] * w[t]
                    sums[at] = sums[at] + f[t] * w[t]
                    sums[at + 1] = sums[at + 1] + w[t] * w[t]
                    sums[at + 2] = sums[at + 2] + (
                        f[t] * heavy + CONSISTENT * (f[t] * w_high[t] + w[t] * f_high[t])
                    )
                    sums[at + 3] = sums[at + 3] + w[t] * (
                        heavy + (2.0 * CONSISTENT) * w_high[t]
                    )
                    sums[at + 4] = sums[at + 4] + f[t] * (
                        weight[t] * f[t] + (2.0 * CONSISTENT) * f_high[t]
                    )
            return (ahead, tuple(sums)), []

        start = [pair(component, low, row) for component in range(3)]
        return plane_loop(low, low + x - 1, plane, (start, sums))[1]

    rest = lax.fori_loop(0, y // ROWS, second_chunk, (nothing,) * 15)
    lane = lane_index((1, LANES))
    line = jnp.zeros((1, LANES), jnp.float32)
    for c in range(3):
        values = [shift[c], square[c]] + [whole_sum(one) for one in rest[5 * c : 5 * c + 5]]
        for k, value in enumerate(values):
            line = jnp.where(lane == 3 * k + c, value, line)
    out[...] = line


def solve_weights(sums):
    got = [sums if k == 0 else pltpu.roll(sums, LANES - 3 * k, 1) for k in range(MOMENTS)]
    c, p0, q1, q2, q3, q4, q5 = got

    def total(value):
        return jnp.sum(value, axis=0, keepdims=True)

    norm_now = total(p0)
    alpha = norm_now / total(q1 + c * p0)
    a = 1.0 - alpha * c
    norm_next = total(a * a * p0 - 2.0 * a * alpha * q1 + alpha * alpha * q2)
    product = total(a * a * q5 - 2.0 * a * alpha * q3 + alpha * alpha * q4)
    ratio = norm_next / norm_now
    later = norm_next / (product - ratio * norm_next / alpha)
    lane = lane_index((1, LANES))

    def pick(value, component):
        return jnp.sum(jnp.where(lane == component, value, 0.0), axis=1, keepdims=True)

    on_force, on_image = alpha + later * (1.0 + ratio), -later * alpha
    return [(pick(on_force, k), pick(on_image, k)) for k in range(3)]


def step_kernel(plan, *refs):
    flags, sums, density, energy, position, velocity, pinned = refs[:7]
    messages = refs[7:14]
    velocity_new, accel, relaxed, density_new, energy_new = refs[14:19]
    (
        density_ext,
        energy_ext,
        moved,
        speed,
        free_ext,
        packed_ext,
        pinned_own,
        force,
        mass,
        other,
        semaphores,
        out_semaphores,
    ) = refs[19:]
    assemble(
        plan,
        [density, energy, position, velocity, pinned],
        messages,
        [density_ext, energy_ext, moved, speed, free_ext],
        packed_ext,
        pinned_own,
        semaphores,
    )
    inside = Inside(plan, flags)
    low, x, y = plan.low, plan.x, plan.y
    weights = solve_weights(sums[...])
    reach = SWEEPS + 1
    force_pass(
        density_ext,
        energy_ext,
        force,
        mass,
        inside,
        (low - reach, low + x + reach),
        (ROWS - reach, ROWS + y + reach),
    )

    def advance(i, row, here, sums, keep):
        weight = load(mass, (0, i), row)
        scale = [tile * inside.plane(i) for tile in keep]
        stores = []
        for component in range(3):
            on_force, on_image = weights[component]
            result = each(
                lambda m, a, k, s: on_force * a + on_image * (m * a + k * s),
                weight,
                here[component],
                scale,
                sums[component],
            )
            at = (component, i)
            faster = each(lambda v, a: v + TIME_STEP * a, load(speed, at, row), result)
            further = each(
                lambda b, a: b + (TIME_STEP * TIME_STEP) * a, load(moved, at, row), result
            )
            stores += [
                (other, at, row, result),
                (speed, at, row, faster),
                (moved, at, row, further),
            ]
        return stores

    reach -= 1
    advanced = round_up(y + 2 * reach + 1, ROWS)
    stencil_pass(
        force,
        (low - reach, low + x + reach),
        (ROWS - reach, ROWS - reach + advanced - 1),
        lambda row: inside.tiles(row, CONSISTENT),
        advance,
    )

    out_copies = []

    def write(source, target, component, result=None):
        for t in range(plan.tiles):
            place = target if result is None else target.at[result]
            out_copies.append(
                pltpu.make_async_copy(
                    source.at[component, pl.ds(low, x), t, pl.ds(ROWS, y), :],
                    place.at[:, :, pl.ds(t * LANES, LANES)],
                    out_semaphores.at[len(out_copies)],
                )
            )
            out_copies[-1].start()

    for component in range(3):
        write(other, accel, component, component)
    accel_copies = len(out_copies)
    for component in range(3):
        write(speed, velocity_new, component, component)

    content = mass

    def content_chunk(row):
        def slab(i):
            under = [load(speed, (component, i), row) for component in range(3)]
            over = [load(speed, (component, i), row + 1) for component in range(3)]
            along_x = add(under[0], over[0])
            along_y = subtract(over[1], under[1])
            along_z = add(under[2], over[2])
            along_x = add(along_x, lane_above(along_x))
            along_y = add(along_y, lane_above(along_y))
            along_z = subtract(lane_above(along_z), along_z)
            return along_x, add(along_y, along_z)

        def plane(i, before):
            now = slab(i + 1)
            spread = add(subtract(now[0], before[0]), add(now[1], before[1]))
            held = load(energy_ext, (0, i), row)
            lagged = each(lambda e, s: e - (0.25 * 0.4 * TIME_STEP) * (e * s), held, spread)
            result = each(lambda d, e: d * e, load(density_ext, (0, i), row), lagged)
            return now, [(content, (0, i), row, result)]

        plane_loop(low - 1, low + x, plane, slab(low - 1))

    chunks(ROWS - 1, ROWS + y, content_chunk)

    for one in out_copies[:accel_copies]:
        one.wait()
    source, target = moved, other
    for _ in range(SWEEPS):
        reach -= 1

        def relax(i, row, here, sums, given, target=target):
            rate = load(free_ext, (0, i), row)
            stores = []
            for component in range(3):
                result = each(
                    lambda r, s, f: r + f * (s * (1.0 / 6.0) - r),
                    here[component],
                    sums[component],
                    rate,
                )
                stores.append((target, (component, i), row, result))
            return stores

        stencil_pass(
            source,
            (low - reach, low + x + reach),
            (ROWS - reach, ROWS + y + reach),
            lambda row: None,
            relax,
        )
        source, target = target, (force if target is other else other)
    settled, free_buffer = source, target
    for component in range(3):
        write(settled, relaxed, component, component)

    quantities = (density_ext, content)

    def remap_chunk(row):
        def shift(component, i, at):
            return subtract(
                load(settled, (component, i), at), load(moved, (component, i), at)
            )

        def slab(i):
            x_here = add(shift(0, i, row), shift(0, i, row + 1))
            y_here, y_over = shift(1, i, row), shift(1, i, row + 1)
            z_here = add(shift(2, i, row), shift(2, i, row + 1))
            return (
                add(x_here, lane_above(x_here)),
                add(y_here, lane_above(y_here)),
                add(y_over, lane_above(y_over)),
                z_here,
                [load(one, (0, i), row) for one in quantities],
            )

        def flux(speeds, upper, lower):
            return each(lambda s, u, l: s * jnp.where(s > 0, u, l), speeds, upper, lower)

        def x_flux(speeds, upper, lower):
            return [flux(speeds, u, l) for u, l in zip(upper, lower)]

        def plane(i, carried):
            now, entering = carried
            ahead = slab(i + 1)
            leaving = x_flux(ahead[0], ahead[4], now[4])
            y_here, y_over, z_here = [add(now[k], ahead[k]) for k in (1, 2, 3)]
            stores = []
            for k, one in enumerate(quantities):
                held = now[4][k]
                under, over = load(one, (0, i), row - 1), load(one, (0, i), row + 1)
                through_z = flux(z_here, held, lane_below(held))
                change = subtract(leaving[k], entering[k])
                change = add(change, flux(y_over, over, held))
                change = subtract(change, flux(y_here, held, under))
                change = add(change, subtract(lane_above(through_z), through_z))
                result = each(lambda q, c: q + 0.25 * c, held, change)
                stores.append((free_buffer, (k, i), row, result[: plan.tiles]))
            return (ahead, leaving), stores

        start = slab(low)
        before = [load(one, (0, low - 1), row) for one in quantities]
        plane_loop(low, low + x - 1, plane, (start, x_flux(start[0], start[4], before)))

    chunks(ROWS, ROWS + y - 1, remap_chunk)
    write(free_buffer, density_new, 0)
    write(free_buffer, energy_new, 1)
    for one in out_copies[accel_copies:]:
        one.wait()


def gather_lines(line, axes):
    for axis in axes:
        count = lax.axis_size(axis)
        if count & (count - 1):
            line = lax.all_gather(line, axis, axis=0, tiled=True)
            continue
        step = 1
        while step < count:
            got = lax.ppermute(line, axis, [(i, i ^ step) for i in range(count)])
            later = (lax.axis_index(axis) // step) % 2 == 1
            line = jnp.concatenate([jnp.where(later, got, line), jnp.where(later, line, got)])
            step *= 2
    return line


def extended_scratch(plan, count):
    return pltpu.VMEM((count, plan.planes, plan.tiles + 1, plan.rows, LANES), jnp.float32)


def message_specs(rows):
    return [any_space()] * 3 + [in_vmem()] * rows


def on_device(position, velocity, density, energy, pinned):
    shape = density.shape
    arrays = [density[None], energy[None], position, velocity, pinned[None]]
    flags = jnp.stack(
        [
            jnp.float32(limit)
            for axis in ("bx", "by", "bz")
            for limit in (
                lax.axis_index(axis) > 0,
                lax.axis_index(axis) < lax.axis_size(axis) - 1,
            )
        ]
    )
    wide = Plan(
        [
            (1, WIDE, WIDE),
            (1, WIDE, WIDE),
            (3, SWEEPS, SWEEPS + 1),
            (3, 1, 2),
            (1, SWEEPS - 1, SWEEPS),
        ],
        shape,
    )
    narrow = Plan([(1, NARROW, NARROW)] * 2, shape, wide.starts)

    packed = exchange_lanes(wide, pack_lanes(wide, arrays))
    planes = exchange("bx", pack_planes(narrow, arrays[:2], packed))
    wide_planes = pack_planes(wide, arrays, packed)
    wide_rows = pack_rows(wide, arrays, packed, None, None, True, False)
    planes, wide_planes = lax.optimization_barrier((planes, wide_planes))
    rows = exchange("by", pack_rows(narrow, arrays[:2], packed, *planes, True, True))
    wide_planes = exchange("bx", wide_planes)
    rows, wide_rows = lax.optimization_barrier((rows, wide_rows))
    wide_rows = exchange("by", wide_rows)

    line = pl.pallas_call(
        functools.partial(moments_kernel, narrow),
        in_specs=[in_smem()] + [any_space()] * 2 + message_specs(2),
        out_specs=in_vmem(),
        out_shape=jax.ShapeDtypeStruct((1, LANES), jnp.float32),
        scratch_shapes=[
            extended_scratch(narrow, 1),
            extended_scratch(narrow, 1),
            pltpu.VMEM((narrow.planes, narrow.rows, LANES), jnp.float32),
            extended_scratch(narrow, 3),
            extended_scratch(narrow, 3),
            extended_scratch(narrow, 1),
            pltpu.SemaphoreType.DMA((assemble_copies(narrow),)),
        ],
        compiler_params=pltpu.CompilerParams(vmem_limit_bytes=VMEM_BYTES),
        cost_estimate=cost(30),
        name="moments",
    )(flags, *arrays[:2], packed, *planes, *rows)

    line, wide_rows = lax.optimization_barrier((line, wide_rows))
    lines = gather_lines(line, ("bz", "by"))
    lines, wide_planes = lax.optimization_barrier((lines, wide_planes))
    corners = exchange("by", pack_rows(wide, None, None, *wide_planes, False, True))
    messages = [packed, *wide_planes, *wide_rows, *corners]
    nodes = jax.ShapeDtypeStruct((3, *shape), jnp.float32)
    cells = jax.ShapeDtypeStruct(shape, jnp.float32)
    return pl.pallas_call(
        functools.partial(step_kernel, wide),
        in_specs=[in_smem(), in_vmem()] + [any_space()] * 5 + message_specs(4),
        out_specs=[any_space()] * 5,
        out_shape=[nodes, nodes, nodes, cells, cells],
        scratch_shapes=[
            extended_scratch(wide, 1),
            extended_scratch(wide, 1),
            extended_scratch(wide, 3),
            extended_scratch(wide, 3),
            extended_scratch(wide, 1),
            pltpu.VMEM((wide.planes, wide.rows, LANES), jnp.float32),
            pltpu.VMEM((wide.x, wide.tiles, wide.y, LANES), jnp.int32),
            extended_scratch(wide, 3),
            extended_scratch(wide, 1),
            extended_scratch(wide, 3),
            pltpu.SemaphoreType.DMA((assemble_copies(wide),)),
            pltpu.SemaphoreType.DMA((11 * wide.tiles,)),
        ],
        compiler_params=pltpu.CompilerParams(vmem_limit_bytes=VMEM_BYTES),
        cost_estimate=cost(60),
        name="step",
    )(flags, gather_lines(lines, ("bx",)), *arrays, *messages)


def solution(mesh):
    in_specs = (
        P(None, "bx", "by", "bz"),
        P(None, "bx", "by", "bz"),
        P("bx", "by", "bz"),
        P("bx", "by", "bz"),
        P("bx", "by", "bz"),
    )
    out_specs = (
        P(None, "bx", "by", "bz"),
        P(None, "bx", "by", "bz"),
        P(None, "bx", "by", "bz"),
        P("bx", "by", "bz"),
        P("bx", "by", "bz"),
    )
    return jax.shard_map(
        on_device, mesh=mesh, in_specs=in_specs, out_specs=out_specs, check_vma=False
    )
```

```python
import functools
from typing import NamedTuple

import jax
import jax.numpy as jnp
from jax import lax
from jax.experimental import pallas as pl
from jax.experimental.pallas import tpu as pltpu
from jax.sharding import PartitionSpec as P

SWEEPS = 3
TIME_STEP = 0.6
RELAX_RATE = 0.8
CONSISTENT = 0.2

LANES = 128
ROWS = 8
MOMENTS = 7
UNROLL = 6
POSITION, VELOCITY, PINNED = 2, 3, 4
NARROW = 2
WIDE = SWEEPS + 2
VMEM_BYTES = 62 * 2**20


class Field(NamedTuple):
    group: int
    component: int
    low: int
    high: int
    skip: int
    low_at: int
    high_at: int
    full_low_at: int
    full_high_at: int
    start: int


class Plan:
    def __init__(self, groups, shape, inner=None, starts=None, cut=None):
        self.groups = groups
        self.inner = inner
        self.x, self.y, self.z = shape
        self.tiles = self.z // LANES
        self.low = max(low for _, low, _ in groups)
        self.high = max(high for _, _, high in groups)
        self.planes = self.low + self.x + self.high
        self.rows = self.y + 2 * ROWS
        self.fields = []
        at = [0] * 4
        lane_at = 0
        for group, (count, low, high) in enumerate(groups):
            skip = 0 if inner is None or group >= len(inner.groups) else inner.low
            for component in range(count):
                start = lane_at + low if starts is None else starts[len(self.fields)]
                self.fields.append(Field(group, component, low, high, skip, *at, start))
                for k, size in enumerate((low - skip, high - skip, low, high)):
                    at[k] += size
                lane_at += low + high
        assert lane_at <= LANES
        self.starts = [field.start for field in self.fields]
        self.packed_at = at
        depths = (self.low, self.high) * 2
        self.sizes = [one + -(-depth // self.tiles) for one, depth in zip(at, depths)]
        cuts = [] if cut is None else [(self.fields[cut].low_at, self.fields[cut].high_at)]
        self.parts = []
        for side in range(2):
            ends = [0, *(one[side] for one in cuts), self.sizes[side]]
            self.parts.append([b - a for a, b in zip(ends, ends[1:])])

    def value(self, group, component, get):
        if group == POSITION:
            return get(POSITION, component) + TIME_STEP * get(VELOCITY, component)
        if group == PINNED:
            return RELAX_RATE * (1.0 - get(PINNED, component).astype(jnp.float32))
        return get(group, component)

    def folded(self, k, at):
        return at + k // self.tiles, (k % self.tiles) * LANES


def round_up(value, step):
    return -(-value // step) * step


def from_behind(x, axis):
    count = lax.axis_size(axis)
    return lax.ppermute(x, axis, [(i, i + 1) for i in range(count - 1)])


def from_ahead(x, axis):
    count = lax.axis_size(axis)
    return lax.ppermute(x, axis, [(i + 1, i) for i in range(count - 1)])


def any_space():
    return pl.BlockSpec(memory_space=pl.ANY)


def in_vmem():
    return pl.BlockSpec(memory_space=pltpu.VMEM)


def in_smem():
    return pl.BlockSpec(memory_space=pltpu.SMEM)


def cost(microseconds):
    return pl.CostEstimate(
        flops=0, bytes_accessed=int(microseconds * 3.0e6), transcendentals=0
    )


def lane_index(shape):
    return lax.broadcasted_iota(jnp.int32, shape, len(shape) - 1)


def pack_lanes(plan, arrays):
    half = LANES // 2

    def kernel(*refs):
        out = refs[-1]
        lane = lane_index((plan.y, LANES))
        in_low_half = lane < half

        def plane(x, _):
            def edge(group, component):
                first, last = refs[2 * group], refs[2 * group + 1]
                return jnp.where(in_low_half, first[component, x], last[component, x])

            packed = jnp.zeros((plan.y, LANES), jnp.float32)
            for group, component, low, high, *_, start in plan.fields:
                moved = pltpu.roll(plan.value(group, component, edge), start, 1)
                packed = jnp.where((lane >= start - low) & (lane < start + high), moved, packed)
            out[x] = packed
            return 0

        for x in range(planes):
            plane(x, 0)

    planes = 4 if plan.x % 4 == 0 else 1
    specs, operands = [], []
    for (count, _, _), array in zip(plan.groups, arrays):
        block = (count, planes, plan.y, LANES)
        specs.append(pl.BlockSpec(block, lambda i: (0, i, 0, 0)))
        specs.append(pl.BlockSpec(block, lambda i: (0, i, 0, plan.tiles - 1)))
        operands += [array, array]
    return pl.pallas_call(
        kernel,
        grid=(plan.x // planes,),
        in_specs=specs,
        out_specs=pl.BlockSpec((planes, plan.y, LANES), lambda i: (i, 0, 0)),
        out_shape=jax.ShapeDtypeStruct((plan.x, plan.y, LANES), jnp.float32),
        compiler_params=pltpu.CompilerParams(vmem_limit_bytes=VMEM_BYTES),
        cost_estimate=cost(0.5),
        name="pack_lanes",
    )(*operands)


def exchange_lanes(plan, packed):
    lane = lane_index((1, 1, LANES))
    is_low = functools.reduce(
        jnp.logical_or,
        [(lane >= start - low) & (lane < start) for _, _, low, *_, start in plan.fields],
    )
    count = lax.axis_size("bz")
    if count == 2:
        got = lax.ppermute(packed, "bz", [(0, 1), (1, 0)])
        return jnp.where(is_low == (lax.axis_index("bz") == 1), got, 0.0)
    return jnp.where(is_low, from_behind(packed, "bz"), from_ahead(packed, "bz"))


def part_of(parts, at):
    for part in parts:
        if at < part.shape[0]:
            return part, at
        at -= part.shape[0]


def pack_planes(plan, arrays, packed):
    needed = [
        max(low if to_low else high for _, low, high in plan.groups) for to_low in (True, False)
    ]
    depths = [(low, high) for _, low, high in plan.groups]
    if len(depths) > VELOCITY:
        depths[VELOCITY] = depths[POSITION]

    def kernel(*refs):
        groups = len(plan.groups)
        own, packed_ref = refs[:groups], refs[groups]
        count = len(plan.parts[0])
        outs = refs[groups + 1 : groups + 1 + count], refs[groups + 1 + count : groups + 1 + 2 * count]
        edges, semaphores = refs[groups + 1 + 2 * count : -1], refs[-1]
        copies = []

        def copy(source, target):
            copies.append(pltpu.make_async_copy(source, target, semaphores.at[len(copies)]))
            copies[-1].start()

        for side, out in enumerate(outs):
            for group, array in enumerate(own):
                depth = depths[group][side]
                planes = pl.ds(plan.x - depth, depth) if side == 0 else pl.ds(0, depth)
                copy(array.at[:, planes], edges[2 * group + side])
            first = plan.x - needed[0] if side == 0 else 0
            at = plan.packed_at[side]
            for k in range(needed[side]):
                row, lanes = plan.folded(k, at)
                part, row = part_of(out, row)
                copy(packed_ref.at[first + k], part.at[row, :, pl.ds(lanes, LANES)])
        for one in copies:
            one.wait()
        for side, out in enumerate(outs):
            for field in plan.fields:
                at = (field.low_at, field.high_at)[side]
                depth = (field.low, field.high)[side] - field.skip

                def get(argument, part):
                    held = edges[2 * argument + side]
                    first = depths[argument][0] - field.low if side == 0 else field.skip
                    return held[part, first : first + depth]

                part, at = part_of(out, at)
                part[at : at + depth] = plan.value(field.group, field.component, get)

    shapes = [(size, plan.y, plan.z) for side in plan.parts for size in side]
    scratch = [
        pltpu.VMEM((array.shape[0], depth, plan.y, plan.z), array.dtype)
        for array, pair in zip(arrays, depths)
        for depth in pair
    ]
    count = 2 * len(arrays) + sum(needed)
    outs = pl.pallas_call(
        kernel,
        in_specs=[any_space()] * (len(arrays) + 1),
        out_specs=[in_vmem()] * len(shapes),
        out_shape=[jax.ShapeDtypeStruct(shape, jnp.float32) for shape in shapes],
        scratch_shapes=scratch + [pltpu.SemaphoreType.DMA((count,))],
        compiler_params=pltpu.CompilerParams(vmem_limit_bytes=VMEM_BYTES),
        cost_estimate=cost(0.5),
        name="pack_planes",
    )(*arrays, packed)
    return list(zip(outs[: len(plan.parts[0])], outs[len(plan.parts[0]) :]))


def pack_rows(plan, arrays, packed, own, planes=(), inner_planes=()):
    groups = len(plan.groups)
    sizes, packed_at = plan.sizes[2:], plan.packed_at[2:]
    if own:
        sizes, packed_at = plan.sizes[:2], plan.packed_at[:2]

    def kernel(*refs):
        refs = list(refs)
        up, down = refs[-2:]
        up[...] = jnp.zeros(up.shape, jnp.float32)
        down[...] = jnp.zeros(down.shape, jnp.float32)

        def put(plane, field, first, last):
            low_at, high_at, skip = field.full_low_at, field.full_high_at, 0
            if own:
                low_at, high_at, skip = field.low_at, field.high_at, field.skip
            low, high = field.low - skip, field.high - skip
            up[plane, low_at : low_at + low, :] = last[ROWS - field.low : ROWS - skip, :]
            down[plane, high_at : high_at + high, :] = first[skip : field.high, :]

        def put_packed(plane, first, last, at):
            for k in range(plan.low):
                row, lanes = plan.folded(k, packed_at[0])
                source = ROWS - plan.low + k
                up[plane, row : row + 1, lanes : lanes + LANES] = last[
                    source : source + 1, at : at + LANES
                ]
            for k in range(plan.high):
                row, lanes = plan.folded(k, packed_at[1])
                down[plane, row : row + 1, lanes : lanes + LANES] = first[
                    k : k + 1, at : at + LANES
                ]

        base = 0
        if own:
            blocks = refs[: 2 * groups + 2]
            del refs[: 2 * groups + 2]
            base = plan.x

            def own_plane(x, _):
                for field in plan.fields:
                    first, last = [
                        plan.value(
                            *field[:2],
                            lambda argument, part: blocks[2 * argument + side][part, x],
                        )
                        for side in range(2)
                    ]
                    put(x, field, first, last)
                put_packed(x, blocks[-2].at[x], blocks[-1].at[x], 0)
                return 0

            lax.fori_loop(0, plan.x, own_plane, 0)
        if planes:
            count = len(plan.parts[0])
            pairs = [tuple(refs[2 * k : 2 * k + 2]) for k in range(2 * count + 2)]
            if plan.inner is None:
                pairs = pairs[: 2 * count]
            sides = [pairs[:count], pairs[count : 2 * count]]
            inner_sides = [pairs[2 * count : 2 * count + 1], pairs[2 * count + 1 :]]

            def find(parts, at):
                part, at = part_of([first for first, _ in parts], at)
                pair = next(pair for pair in parts if pair[0] is part)
                return [ref.at[at] for ref in pair]

            for side in range(2):
                for k in range((plan.low, plan.high)[side]):
                    for field in plan.fields:
                        depth, at = (field.low, field.low_at) if side == 0 else (field.high, field.high_at)
                        j = plan.low - k if side == 0 else k + 1
                        if j > depth:
                            continue
                        if j > field.skip:
                            source = at + (depth - j if side == 0 else j - 1 - field.skip)
                            parts = sides[side]
                        else:
                            other = plan.inner.fields[field.group]
                            source = other.low_at + other.low - j if side == 0 else other.high_at + j - 1
                            parts = inner_sides[side]
                        put(base + k, field, *find(parts, source))
                    source, lanes = plan.folded(k, plan.packed_at[side])
                    put_packed(base + k, *find(sides[side], source), lanes)
                base += plan.low

    last = plan.y // ROWS - 1
    specs, operands = [], []
    if own:
        for array in arrays:
            block = (array.shape[0], plan.x, ROWS, plan.z)
            specs.append(pl.BlockSpec(block, lambda i: (0, 0, 0, 0)))
            specs.append(pl.BlockSpec(block, lambda i: (0, 0, last, 0)))
            operands += [array, array]
    for array in ([packed] if own else []) + [*planes, *inner_planes]:
        block = (array.shape[0], ROWS, array.shape[2])
        specs.append(pl.BlockSpec(block, lambda i: (0, 0, 0)))
        specs.append(pl.BlockSpec(block, lambda i: (0, last, 0)))
        operands += [array, array]
    count = plan.x * own + (plan.low + plan.high) * bool(planes)
    shapes = [(count, round_up(size, ROWS), plan.z) for size in sizes]
    return pl.pallas_call(
        kernel,
        grid=(1,),
        in_specs=specs,
        out_specs=[pl.BlockSpec(shape, lambda i: (0, 0, 0)) for shape in shapes],
        out_shape=[jax.ShapeDtypeStruct(shape, jnp.float32) for shape in shapes],
        compiler_params=pltpu.CompilerParams(vmem_limit_bytes=VMEM_BYTES),
        cost_estimate=cost(0.5),
        name="pack_rows",
    )(*operands)


def exchange(axis, pair):
    return [from_behind(pair[0], axis), from_ahead(pair[1], axis)]


def assemble(plan, arrays, messages, inner, extended, packed_ext, pinned_own, semaphores):
    count = len(plan.parts[0])
    packed, below, above = messages[0], messages[1 : 1 + count], messages[1 + count : 1 + 2 * count]
    rest = messages[1 + 2 * count :]
    if len(rest) == 2:
        sides = [(rest[0], rest[0], plan.x), (rest[1], rest[1], plan.x)]
    else:
        sides = [(rest[0], rest[2], 0), (rest[1], rest[3], 0)]
    copies = []

    def copy(source, target):
        copies.append(
            pltpu.make_async_copy(source, target, semaphores.at[len(copies)])
        )
        copies[-1].start()

    own_rows = pl.ds(ROWS, plan.y)
    own_planes = pl.ds(plan.low, plan.x)
    for field in plan.fields:
        group, component, low, high, skip = field[:5]
        target = extended[group].at[component]
        after = plan.low + plan.x
        for t in range(plan.tiles):
            lanes = pl.ds(t * LANES, LANES)

            def planes(source, at, first, count):
                if count:
                    source, at = part_of(source, at)
                    copy(
                        source.at[pl.ds(at, count), :, lanes],
                        target.at[pl.ds(first, count), t, own_rows, :],
                    )

            place = target.at[own_planes, t, own_rows, :]
            if group == PINNED:
                place = pinned_own.at[:, t]
            copy(arrays[group].at[component, :, :, lanes], place)
            planes(below, field.low_at, plan.low - low, low - skip)
            planes(above, field.high_at, after + skip, high - skip)
            if skip:
                other = plan.inner.fields[group]
                planes(inner[:1], other.low_at, plan.low - skip, skip)
                planes(inner[1:2], other.high_at, after, skip)
    large = len(copies)
    copy(packed, packed_ext.at[own_planes, own_rows, :])
    for k in range(plan.low):
        source, lanes = plan.folded(k, plan.packed_at[0])
        part, source = part_of(below, source)
        copy(part.at[source, :, pl.ds(lanes, LANES)], packed_ext.at[k, own_rows, :])
    for k in range(plan.high):
        source, lanes = plan.folded(k, plan.packed_at[1])
        part, source = part_of(above, source)
        copy(
            part.at[source, :, pl.ds(lanes, LANES)],
            packed_ext.at[plan.low + plan.x + k, own_rows, :],
        )
    for one in copies[large:]:
        one.wait()

    top = ROWS + plan.y

    def fill(i, left, right, at, own):
        def rows(field, first, source, source_at, count):
            if count:
                for t in range(plan.tiles):
                    extended[field.group][field.component, i, t, first : first + count, :] = source[
                        at, source_at : source_at + count, t * LANES : (t + 1) * LANES
                    ]

        packed_at = plan.packed_at[:2] if own else plan.packed_at[2:]
        for field in plan.fields:
            low, high, skip = field.low, field.high, field.skip
            if own:
                rows(field, ROWS - low, left, field.low_at, low - skip)
                rows(field, top + skip, right, field.high_at, high - skip)
                if skip:
                    other = plan.inner.fields[field.group]
                    rows(field, ROWS - skip, inner[2], other.low_at, skip)
                    rows(field, top, inner[3], other.high_at, skip)
            else:
                rows(field, ROWS - low, left, field.full_low_at, low)
                rows(field, top, right, field.full_high_at, high)
        for k in range(plan.low):
            row, lanes = plan.folded(k, packed_at[0])
            to = ROWS - plan.low + k
            packed_ext[i, to : to + 1, :] = left[at, row : row + 1, lanes : lanes + LANES]
        for k in range(plan.high):
            row, lanes = plan.folded(k, packed_at[1])
            packed_ext[i, top + k : top + k + 1, :] = right[at, row : row + 1, lanes : lanes + LANES]
        tile = packed_ext[i]
        for field in plan.fields:
            extended[field.group][field.component, i, plan.tiles] = pltpu.roll(
                tile, (LANES - field.start) % LANES, 1
            )

    def own_plane(x, _):
        fill(plan.low + x, sides[0][0], sides[1][0], x, True)
        return 0

    def finish_plane(x, _):
        i = plan.low + x
        for t in range(plan.tiles):
            at = (i, t, slice(ROWS, top))

            def get(argument, component):
                if argument == PINNED:
                    return pinned_own[x, t]
                return extended[argument][(component, *at)]

            for group, component in [(POSITION, c) for c in range(3)] + [(PINNED, 0)]:
                extended[group][(component, *at)] = plan.value(group, component, get)
        return 0

    def low_plane(k, _):
        fill(k, sides[0][1], sides[1][1], sides[0][2] + k, False)
        return 0

    def high_plane(k, _):
        at = sides[0][2] + plan.low + k
        fill(plan.low + plan.x + k, sides[0][1], sides[1][1], at, False)
        return 0

    lax.fori_loop(0, plan.x, own_plane, 0)
    lax.fori_loop(0, plan.low, low_plane, 0)
    lax.fori_loop(0, plan.high, high_plane, 0)
    for one in copies[:large]:
        one.wait()
    if pinned_own is not None:
        lax.fori_loop(0, plan.x, finish_plane, 0)


def assemble_copies(plan):
    skipping = sum(field.skip > 0 for field in plan.fields)
    return (3 * len(plan.fields) + 2 * skipping) * plan.tiles + 1 + plan.low + plan.high


def plane_loop(first, last, body, carried):
    def turn(i, carried, count):
        pending = []
        for k in range(count):
            carried, stores = body(i + k, carried)
            pending += stores
        for one in pending:
            store(*one)
        return carried

    count = last - first + 1
    carried = lax.fori_loop(
        0, count // UNROLL, lambda j, c: turn(first + j * UNROLL, c, UNROLL), carried
    )
    rest = count % UNROLL
    return turn(last + 1 - rest, carried, rest) if rest else carried


def load(ref, index, row):
    return [ref[(*index, t, pl.ds(row, ROWS), slice(None))] for t in range(ref.shape[-3])]


def store(ref, index, row, tiles):
    for t, tile in enumerate(tiles):
        ref[(*index, t, pl.ds(row, ROWS), slice(None))] = tile


def each(function, *tiles):
    return [function(*one) for one in zip(*tiles)]


def add(first, second):
    return each(lambda a, b: a + b, first, second)


def subtract(first, second):
    return each(lambda a, b: a - b, first, second)


def lane_below(tiles):
    lane = lane_index((ROWS, LANES))
    rolled = [pltpu.roll(tile, 1, 1) for tile in tiles]
    return [jnp.where(lane == 0, rolled[t - 1], rolled[t]) for t in range(len(tiles))]


def lane_above(tiles):
    lane = lane_index((ROWS, LANES))
    rolled = [pltpu.roll(tile, LANES - 1, 1) for tile in tiles]
    count = len(tiles)
    return [
        jnp.where(lane == LANES - 1, rolled[(t + 1) % count], rolled[t]) for t in range(count)
    ]


def chunks(first, last, body):
    count = -(-(last - first + 1) // ROWS)

    def one(j, _):
        body(jnp.minimum(first + j * ROWS, last - ROWS + 1))
        return 0

    lax.fori_loop(0, count, one, 0)


class Inside:
    def __init__(self, plan, flags):
        self.plan = plan
        self.flags = flags

    def tiles(self, row, scale):
        plan, flags = self.plan, self.flags
        rows = row + lax.broadcasted_iota(jnp.int32, (ROWS, LANES), 0)
        keep = jnp.where(rows < ROWS, flags[2], jnp.where(rows >= ROWS + plan.y, flags[3], 1.0))
        lane = lane_index((ROWS, LANES))
        edge = jnp.where(lane < LANES // 2, flags[5], flags[4])
        keep = scale * keep
        return [keep] * plan.tiles + [keep * edge]

    def plane(self, i):
        plan, flags = self.plan, self.flags
        return jnp.where(
            i < plan.low, flags[0], jnp.where(i >= plan.low + plan.x, flags[1], 1.0)
        )


def force_pass(density, energy, force, mass, inside, planes, rows):
    def chunk(row):
        keep = inside.tiles(row, 0.4 * 0.25)

        def slab(i):
            here, under = load(density, (0, i), row), load(density, (0, i), row - 1)
            p = each(lambda a, b: a * b, here, load(energy, (0, i), row))
            p_under = each(lambda a, b: a * b, under, load(energy, (0, i), row - 1))
            summed, stepped = add(p, p_under), subtract(p_under, p)
            weight = add(here, under)
            summed_z, stepped_z = lane_below(summed), lane_below(stepped)
            return (
                add(summed, summed_z),
                add(stepped, stepped_z),
                subtract(summed_z, summed),
                add(weight, lane_below(weight)),
            )

        def plane(i, before):
            now = slab(i)
            here = inside.plane(i)
            scale = [tile * here for tile in keep]
            stores = []
            for component in range(3):
                across = (subtract if component == 0 else add)(before[component], now[component])
                result = each(lambda a, b: a * b, scale, across)
                stores.append((force, (component, i), row, result))
            result = each(lambda a, b: 0.125 * (a + b) + 6.0 * CONSISTENT, before[3], now[3])
            stores.append((mass, (0, i), row, result))
            return now, stores

        plane_loop(*planes, plane, slab(planes[0] - 1))

    chunks(*rows, chunk)


def face_sum(ref, component, i, row, before, here, after):
    total = add(add(before, after), add(lane_below(here), lane_above(here)))
    return add(total, add(load(ref, (component, i), row - 1), load(ref, (component, i), row + 1)))


def stencil_pass(ref, planes, rows, setup, use):
    def chunk(row):
        given = setup(row)

        def plane(i, carried):
            before, here = carried
            after = [load(ref, (component, i + 1), row) for component in range(3)]
            sums = [
                face_sum(ref, component, i, row, before[component], here[component], after[component])
                for component in range(3)
            ]
            return (here, after), use(i, row, here, sums, given)

        first = [load(ref, (component, planes[0] - 1), row) for component in range(3)]
        second = [load(ref, (component, planes[0]), row) for component in range(3)]
        plane_loop(*planes, plane, (first, second))

    chunks(*rows, chunk)


def whole_sum(tile):
    return jnp.sum(jnp.sum(tile, axis=0, keepdims=True), axis=1, keepdims=True)


def moments_kernel(plan, *refs):
    flags, density, energy = refs[:3]
    messages, out = refs[3:8], refs[8]
    density_ext, energy_ext, packed_ext, force, image, mass, semaphores = refs[9:]
    assemble(
        plan,
        [density, energy],
        messages,
        None,
        [density_ext, energy_ext],
        packed_ext,
        None,
        semaphores,
    )
    inside = Inside(plan, flags)
    low, x, y = plan.low, plan.x, plan.y
    force_pass(
        density_ext,
        energy_ext,
        force,
        mass,
        inside,
        (low - 1, low + x + 1),
        (ROWS - 1, ROWS + y + 1),
    )

    def multiply(i, row, here, sums, keep):
        weight = load(mass, (0, i), row)
        scale = [tile * inside.plane(i) for tile in keep]
        stores = []
        for component in range(3):
            result = each(
                lambda m, a, k, s: m * a + k * s, weight, here[component], scale, sums[component]
            )
            stores.append((image, (component, i), row, result))
        return stores

    stencil_pass(
        force,
        (low, low + x),
        (ROWS, ROWS + y),
        lambda row: inside.tiles(row, CONSISTENT),
        multiply,
    )

    own = range(plan.tiles)
    nothing = jnp.zeros((ROWS, LANES), jnp.float32)

    def first_chunk(j, sums):
        row = ROWS + j * ROWS

        def plane(i, sums):
            sums = list(sums)
            for component in range(3):
                f = load(force, (component, i), row)
                v = load(image, (component, i), row)
                for t in own:
                    sums[component] = sums[component] + f[t] * f[t]
                    sums[3 + component] = sums[3 + component] + f[t] * v[t]
            return tuple(sums), []

        return plane_loop(low, low + x - 1, plane, sums)

    sums = lax.fori_loop(0, y // ROWS, first_chunk, (nothing,) * 6)
    sums = [whole_sum(one) for one in sums]
    square = sums[:3]
    shift = [
        jnp.where(square[c] > 0, sums[3 + c] / jnp.where(square[c] > 0, square[c], 1.0), 0.0)
        for c in range(3)
    ]

    def pair(component, i, row):
        f = load(force, (component, i), row)
        v = load(image, (component, i), row)
        return f, each(lambda a, b: a - shift[component] * b, v, f)

    def second_chunk(j, sums):
        row = ROWS + j * ROWS

        def plane(i, carried):
            here, sums = carried
            sums = list(sums)
            ahead = [pair(component, i + 1, row) for component in range(3)]
            weight = load(mass, (0, i), row)
            for component in range(3):
                f, w = here[component]
                f_next, w_next = ahead[component]
                f_up, w_up = pair(component, i, row + 1)
                f_high = add(add(f_next, f_up), lane_above(f))
                w_high = add(add(w_next, w_up), lane_above(w))
                for t in own:
                    at = 5 * component
                    heavy = weight[t] * w[t]
                    sums[at] = sums[at] + f[t] * w[t]
                    sums[at + 1] = sums[at + 1] + w[t] * w[t]
                    sums[at + 2] = sums[at + 2] + (
                        f[t] * heavy + CONSISTENT * (f[t] * w_high[t] + w[t] * f_high[t])
                    )
                    sums[at + 3] = sums[at + 3] + w[t] * (
                        heavy + (2.0 * CONSISTENT) * w_high[t]
                    )
                    sums[at + 4] = sums[at + 4] + f[t] * (
                        weight[t] * f[t] + (2.0 * CONSISTENT) * f_high[t]
                    )
            return (ahead, tuple(sums)), []

        start = [pair(component, low, row) for component in range(3)]
        return plane_loop(low, low + x - 1, plane, (start, sums))[1]

    rest = lax.fori_loop(0, y // ROWS, second_chunk, (nothing,) * 15)
    lane = lane_index((1, LANES))
    line = jnp.zeros((1, LANES), jnp.float32)
    for c in range(3):
        values = [shift[c], square[c]] + [whole_sum(one) for one in rest[5 * c : 5 * c + 5]]
        for k, value in enumerate(values):
            line = jnp.where(lane == 3 * k + c, value, line)
    out[...] = line


def solve_weights(sums):
    got = [sums if k == 0 else pltpu.roll(sums, LANES - 3 * k, 1) for k in range(MOMENTS)]
    c, p0, q1, q2, q3, q4, q5 = got

    def total(value):
        return jnp.sum(value, axis=0, keepdims=True)

    norm_now = total(p0)
    alpha = norm_now / total(q1 + c * p0)
    a = 1.0 - alpha * c
    norm_next = total(a * a * p0 - 2.0 * a * alpha * q1 + alpha * alpha * q2)
    product = total(a * a * q5 - 2.0 * a * alpha * q3 + alpha * alpha * q4)
    ratio = norm_next / norm_now
    later = norm_next / (product - ratio * norm_next / alpha)
    lane = lane_index((1, LANES))

    def pick(value, component):
        return jnp.sum(jnp.where(lane == component, value, 0.0), axis=1, keepdims=True)

    on_force, on_image = alpha + later * (1.0 + ratio), -later * alpha
    return [(pick(on_force, k), pick(on_image, k)) for k in range(3)]


def step_kernel(plan, *refs):
    flags, sums, density, energy, position, velocity, pinned = refs[:7]
    messages, inner = refs[7:16], refs[16:20]
    velocity_new, accel, relaxed, density_new, energy_new = refs[20:25]
    (
        density_ext,
        energy_ext,
        moved,
        speed,
        free_ext,
        packed_ext,
        pinned_own,
        force,
        mass,
        other,
        semaphores,
        out_semaphores,
    ) = refs[25:]
    assemble(
        plan,
        [density, energy, position, velocity, pinned],
        messages,
        inner,
        [density_ext, energy_ext, moved, speed, free_ext],
        packed_ext,
        pinned_own,
        semaphores,
    )
    inside = Inside(plan, flags)
    low, x, y = plan.low, plan.x, plan.y
    weights = solve_weights(sums[...])
    reach = SWEEPS + 1
    force_pass(
        density_ext,
        energy_ext,
        force,
        mass,
        inside,
        (low - reach, low + x + reach),
        (ROWS - reach, ROWS + y + reach),
    )

    def advance(i, row, here, sums, keep):
        weight = load(mass, (0, i), row)
        scale = [tile * inside.plane(i) for tile in keep]
        stores = []
        for component in range(3):
            on_force, on_image = weights[component]
            result = each(
                lambda m, a, k, s: on_force * a + on_image * (m * a + k * s),
                weight,
                here[component],
                scale,
                sums[component],
            )
            at = (component, i)
            faster = each(lambda v, a: v + TIME_STEP * a, load(speed, at, row), result)
            further = each(
                lambda b, a: b + (TIME_STEP * TIME_STEP) * a, load(moved, at, row), result
            )
            stores += [
                (other, at, row, result),
                (speed, at, row, faster),
                (moved, at, row, further),
            ]
        return stores

    reach -= 1
    advanced = round_up(y + 2 * reach + 1, ROWS)
    stencil_pass(
        force,
        (low - reach, low + x + reach),
        (ROWS - reach, ROWS - reach + advanced - 1),
        lambda row: inside.tiles(row, CONSISTENT),
        advance,
    )

    out_copies = []

    def write(source, target, component, result=None):
        for t in range(plan.tiles):
            place = target if result is None else target.at[result]
            out_copies.append(
                pltpu.make_async_copy(
                    source.at[component, pl.ds(low, x), t, pl.ds(ROWS, y), :],
                    place.at[:, :, pl.ds(t * LANES, LANES)],
                    out_semaphores.at[len(out_copies)],
                )
            )
            out_copies[-1].start()

    for component in range(3):
        write(other, accel, component, component)
    accel_copies = len(out_copies)
    for component in range(3):
        write(speed, velocity_new, component, component)

    content = mass

    def content_chunk(row):
        def slab(i):
            under = [load(speed, (component, i), row) for component in range(3)]
            over = [load(speed, (component, i), row + 1) for component in range(3)]
            along_x = add(under[0], over[0])
            along_y = subtract(over[1], under[1])
            along_z = add(under[2], over[2])
            along_x = add(along_x, lane_above(along_x))
            along_y = add(along_y, lane_above(along_y))
            along_z = subtract(lane_above(along_z), along_z)
            return along_x, add(along_y, along_z)

        def plane(i, before):
            now = slab(i + 1)
            spread = add(subtract(now[0], before[0]), add(now[1], before[1]))
            held = load(energy_ext, (0, i), row)
            lagged = each(lambda e, s: e - (0.25 * 0.4 * TIME_STEP) * (e * s), held, spread)
            result = each(lambda d, e: d * e, load(density_ext, (0, i), row), lagged)
            return now, [(content, (0, i), row, result)]

        plane_loop(low - 1, low + x, plane, slab(low - 1))

    chunks(ROWS - 1, ROWS + y, content_chunk)

    for one in out_copies[:accel_copies]:
        one.wait()
    source, target = moved, other
    for _ in range(SWEEPS):
        reach -= 1

        def relax(i, row, here, sums, given, target=target):
            rate = load(free_ext, (0, i), row)
            stores = []
            for component in range(3):
                result = each(
                    lambda r, s, f: r + f * (s * (1.0 / 6.0) - r),
                    here[component],
                    sums[component],
                    rate,
                )
                stores.append((target, (component, i), row, result))
            return stores

        stencil_pass(
            source,
            (low - reach, low + x + reach),
            (ROWS - reach, ROWS + y + reach),
            lambda row: None,
            relax,
        )
        source, target = target, (force if target is other else other)
    settled, free_buffer = source, target
    for component in range(3):
        write(settled, relaxed, component, component)

    quantities = (density_ext, content)

    def remap_chunk(row):
        def shift(component, i, at):
            return subtract(
                load(settled, (component, i), at), load(moved, (component, i), at)
            )

        def slab(i):
            x_here = add(shift(0, i, row), shift(0, i, row + 1))
            y_here, y_over = shift(1, i, row), shift(1, i, row + 1)
            z_here = add(shift(2, i, row), shift(2, i, row + 1))
            return (
                add(x_here, lane_above(x_here)),
                add(y_here, lane_above(y_here)),
                add(y_over, lane_above(y_over)),
                z_here,
                [load(one, (0, i), row) for one in quantities],
            )

        def flux(speeds, upper, lower):
            return each(lambda s, u, l: s * jnp.where(s > 0, u, l), speeds, upper, lower)

        def x_flux(speeds, upper, lower):
            return [flux(speeds, u, l) for u, l in zip(upper, lower)]

        def plane(i, carried):
            now, entering = carried
            ahead = slab(i + 1)
            leaving = x_flux(ahead[0], ahead[4], now[4])
            y_here, y_over, z_here = [add(now[k], ahead[k]) for k in (1, 2, 3)]
            stores = []
            for k, one in enumerate(quantities):
                held = now[4][k]
                under, over = load(one, (0, i), row - 1), load(one, (0, i), row + 1)
                through_z = flux(z_here, held, lane_below(held))
                change = subtract(leaving[k], entering[k])
                change = add(change, flux(y_over, over, held))
                change = subtract(change, flux(y_here, held, under))
                change = add(change, subtract(lane_above(through_z), through_z))
                result = each(lambda q, c: q + 0.25 * c, held, change)
                stores.append((free_buffer, (k, i), row, result[: plan.tiles]))
            return (ahead, leaving), stores

        start = slab(low)
        before = [load(one, (0, low - 1), row) for one in quantities]
        plane_loop(low, low + x - 1, plane, (start, x_flux(start[0], start[4], before)))

    chunks(ROWS, ROWS + y - 1, remap_chunk)
    write(free_buffer, density_new, 0)
    write(free_buffer, energy_new, 1)
    for one in out_copies[accel_copies:]:
        one.wait()


def gather_lines(line, axes):
    for axis in axes:
        count = lax.axis_size(axis)
        if count & (count - 1):
            line = lax.all_gather(line, axis, axis=0, tiled=True)
            continue
        step = 1
        while step < count:
            got = lax.ppermute(line, axis, [(i, i ^ step) for i in range(count)])
            later = (lax.axis_index(axis) // step) % 2 == 1
            line = jnp.concatenate([jnp.where(later, got, line), jnp.where(later, line, got)])
            step *= 2
    return line


def extended_scratch(plan, count):
    return pltpu.VMEM((count, plan.planes, plan.tiles + 1, plan.rows, LANES), jnp.float32)


def message_specs(planes, rows):
    return [any_space()] * planes + [in_vmem()] * rows


def on_device(position, velocity, density, energy, pinned):
    shape = density.shape
    arrays = [density[None], energy[None], position, velocity, pinned[None]]
    flags = jnp.stack(
        [
            jnp.float32(limit)
            for axis in ("bx", "by", "bz")
            for limit in (
                lax.axis_index(axis) > 0,
                lax.axis_index(axis) < lax.axis_size(axis) - 1,
            )
        ]
    )
    groups = [
        (1, WIDE, WIDE),
        (1, WIDE, WIDE),
        (3, SWEEPS, SWEEPS + 1),
        (3, 1, 2),
        (1, SWEEPS - 1, SWEEPS),
    ]
    starts = Plan(groups, shape).starts
    narrow = Plan([(1, NARROW, NARROW)] * 2, shape, None, starts)
    wide = Plan(groups, shape, narrow, cut=3)

    packed = exchange_lanes(wide, pack_lanes(wide, arrays))
    planes = exchange("bx", *pack_planes(narrow, arrays[:2], packed))
    first_planes, last_planes = pack_planes(wide, arrays, packed)
    wide_rows = pack_rows(wide, arrays, packed, True)
    planes, first_planes = lax.optimization_barrier((planes, first_planes))
    rows = exchange("by", pack_rows(narrow, arrays[:2], packed, True, planes))
    first_planes = exchange("bx", first_planes)
    rows, first_planes, last_planes, wide_rows = lax.optimization_barrier(
        (rows, first_planes, last_planes, wide_rows)
    )
    last_planes = exchange("bx", last_planes)
    wide_rows = exchange("by", wide_rows)

    line = pl.pallas_call(
        functools.partial(moments_kernel, narrow),
        in_specs=[in_smem()] + [any_space()] * 2 + message_specs(3, 2),
        out_specs=in_vmem(),
        out_shape=jax.ShapeDtypeStruct((1, LANES), jnp.float32),
        scratch_shapes=[
            extended_scratch(narrow, 1),
            extended_scratch(narrow, 1),
            pltpu.VMEM((narrow.planes, narrow.rows, LANES), jnp.float32),
            extended_scratch(narrow, 3),
            extended_scratch(narrow, 3),
            extended_scratch(narrow, 1),
            pltpu.SemaphoreType.DMA((assemble_copies(narrow),)),
        ],
        compiler_params=pltpu.CompilerParams(vmem_limit_bytes=VMEM_BYTES),
        cost_estimate=cost(1),
        name="moments",
    )(flags, *arrays[:2], packed, *planes, *rows)

    line, wide_rows, last_planes = lax.optimization_barrier((line, wide_rows, last_planes))
    wide_planes = [pair[side] for side in range(2) for pair in (first_planes, last_planes)]
    corners = exchange("by", pack_rows(wide, None, None, False, wide_planes, planes))
    lines = gather_lines(line, ("bz", "bx"))
    lines, corners = lax.optimization_barrier((lines, corners))
    messages = [packed, *wide_planes, *wide_rows, *corners]
    nodes = jax.ShapeDtypeStruct((3, *shape), jnp.float32)
    cells = jax.ShapeDtypeStruct(shape, jnp.float32)
    return pl.pallas_call(
        functools.partial(step_kernel, wide),
        in_specs=[in_smem(), in_vmem()] + [any_space()] * 5 + message_specs(5, 4) + message_specs(2, 2),
        out_specs=[any_space()] * 5,
        out_shape=[nodes, nodes, nodes, cells, cells],
        scratch_shapes=[
            extended_scratch(wide, 1),
            extended_scratch(wide, 1),
            extended_scratch(wide, 3),
            extended_scratch(wide, 3),
            extended_scratch(wide, 1),
            pltpu.VMEM((wide.planes, wide.rows, LANES), jnp.float32),
            pltpu.VMEM((wide.x, wide.tiles, wide.y, LANES), jnp.int32),
            extended_scratch(wide, 3),
            extended_scratch(wide, 1),
            extended_scratch(wide, 3),
            pltpu.SemaphoreType.DMA((assemble_copies(wide),)),
            pltpu.SemaphoreType.DMA((11 * wide.tiles,)),
        ],
        compiler_params=pltpu.CompilerParams(vmem_limit_bytes=VMEM_BYTES),
        cost_estimate=cost(1),
        name="step",
    )(flags, gather_lines(lines, ("by",)), *arrays, *messages, *planes, *rows)


def solution(mesh):
    in_specs = (
        P(None, "bx", "by", "bz"),
        P(None, "bx", "by", "bz"),
        P("bx", "by", "bz"),
        P("bx", "by", "bz"),
        P("bx", "by", "bz"),
    )
    out_specs = (
        P(None, "bx", "by", "bz"),
        P(None, "bx", "by", "bz"),
        P(None, "bx", "by", "bz"),
        P("bx", "by", "bz"),
        P("bx", "by", "bz"),
    )
    return jax.shard_map(
        on_device, mesh=mesh, in_specs=in_specs, out_specs=out_specs, check_vma=False
    )
```

```python
import functools
from typing import NamedTuple

import jax
import jax.numpy as jnp
from jax import lax
from jax.experimental import pallas as pl
from jax.experimental.pallas import tpu as pltpu
from jax.sharding import PartitionSpec as P

SWEEPS = 3
TIME_STEP = 0.6
RELAX_RATE = 0.8
CONSISTENT = 0.2

LANES = 128
ROWS = 8
MOMENTS = 7
UNROLL = 6
POSITION, VELOCITY, PINNED = 2, 3, 4
NARROW = 2
WIDE = SWEEPS + 2
VMEM_BYTES = 62 * 2**20


class Field(NamedTuple):
    group: int
    component: int
    low: int
    high: int
    skip: int
    low_at: int
    high_at: int
    full_low_at: int
    full_high_at: int
    start: int


class Plan:
    def __init__(self, groups, shape, inner=None, starts=None, cut=None):
        self.groups = groups
        self.inner = inner
        self.x, self.y, self.z = shape
        self.tiles = self.z // LANES
        self.low = max(low for _, low, _ in groups)
        self.high = max(high for _, _, high in groups)
        self.planes = self.low + self.x + self.high
        self.rows = self.y + 2 * ROWS
        self.fields = []
        at = [0] * 4
        lane_at = 0
        for group, (count, low, high) in enumerate(groups):
            skip = 0 if inner is None or group >= len(inner.groups) else inner.low
            for component in range(count):
                start = lane_at + low if starts is None else starts[len(self.fields)]
                self.fields.append(Field(group, component, low, high, skip, *at, start))
                for k, size in enumerate((low - skip, high - skip, low, high)):
                    at[k] += size
                lane_at += low + high
        assert lane_at <= LANES
        self.starts = [field.start for field in self.fields]
        self.packed_at = at
        depths = (self.low, self.high) * 2
        self.sizes = [one + -(-depth // self.tiles) for one, depth in zip(at, depths)]
        cuts = [] if cut is None else [(self.fields[cut].low_at, self.fields[cut].high_at)]
        self.parts = []
        for side in range(2):
            ends = [0, *(one[side] for one in cuts), self.sizes[side]]
            self.parts.append([b - a for a, b in zip(ends, ends[1:])])

    def value(self, group, component, get):
        if group == POSITION:
            return get(POSITION, component) + TIME_STEP * get(VELOCITY, component)
        if group == PINNED:
            return RELAX_RATE * (1.0 - get(PINNED, component).astype(jnp.float32))
        return get(group, component)

    def folded(self, k, at):
        return at + k // self.tiles, (k % self.tiles) * LANES


def round_up(value, step):
    return -(-value // step) * step


def from_behind(x, axis):
    count = lax.axis_size(axis)
    return lax.ppermute(x, axis, [(i, i + 1) for i in range(count - 1)])


def from_ahead(x, axis):
    count = lax.axis_size(axis)
    return lax.ppermute(x, axis, [(i + 1, i) for i in range(count - 1)])


def any_space():
    return pl.BlockSpec(memory_space=pl.ANY)


def in_vmem():
    return pl.BlockSpec(memory_space=pltpu.VMEM)


def in_smem():
    return pl.BlockSpec(memory_space=pltpu.SMEM)


def cost(microseconds):
    return pl.CostEstimate(
        flops=0, bytes_accessed=int(microseconds * 3.0e6), transcendentals=0
    )


def lane_index(shape):
    return lax.broadcasted_iota(jnp.int32, shape, len(shape) - 1)


def pack_lanes(plan, arrays):
    half = LANES // 2

    def kernel(*refs):
        out = refs[-1]
        lane = lane_index((plan.y, LANES))
        in_low_half = lane < half

        def plane(x, _):
            def edge(group, component):
                first, last = refs[2 * group], refs[2 * group + 1]
                return jnp.where(in_low_half, first[component, x], last[component, x])

            packed = jnp.zeros((plan.y, LANES), jnp.float32)
            for group, component, low, high, *_, start in plan.fields:
                moved = pltpu.roll(plan.value(group, component, edge), start, 1)
                packed = jnp.where((lane >= start - low) & (lane < start + high), moved, packed)
            out[x] = packed
            return 0

        for x in range(planes):
            plane(x, 0)

    planes = 4 if plan.x % 4 == 0 else 1
    specs, operands = [], []
    for (count, _, _), array in zip(plan.groups, arrays):
        block = (count, planes, plan.y, LANES)
        specs.append(pl.BlockSpec(block, lambda i: (0, i, 0, 0)))
        specs.append(pl.BlockSpec(block, lambda i: (0, i, 0, plan.tiles - 1)))
        operands += [array, array]
    return pl.pallas_call(
        kernel,
        grid=(plan.x // planes,),
        in_specs=specs,
        out_specs=pl.BlockSpec((planes, plan.y, LANES), lambda i: (i, 0, 0)),
        out_shape=jax.ShapeDtypeStruct((plan.x, plan.y, LANES), jnp.float32),
        compiler_params=pltpu.CompilerParams(vmem_limit_bytes=VMEM_BYTES),
        cost_estimate=cost(0.5),
        name="pack_lanes",
    )(*operands)


def exchange_lanes(plan, packed):
    lane = lane_index((1, 1, LANES))
    is_low = functools.reduce(
        jnp.logical_or,
        [(lane >= start - low) & (lane < start) for _, _, low, *_, start in plan.fields],
    )
    count = lax.axis_size("bz")
    if count == 2:
        got = lax.ppermute(packed, "bz", [(0, 1), (1, 0)])
        return jnp.where(is_low == (lax.axis_index("bz") == 1), got, 0.0)
    return jnp.where(is_low, from_behind(packed, "bz"), from_ahead(packed, "bz"))


def part_of(parts, at):
    for part in parts:
        if at < part.shape[0]:
            return part, at
        at -= part.shape[0]


def pack_planes(plan, flags, arrays, packed):
    needed = [
        max(low if to_low else high for _, low, high in plan.groups) for to_low in (True, False)
    ]
    depths = [(low, high) for _, low, high in plan.groups]
    if len(depths) > VELOCITY:
        depths[VELOCITY] = depths[POSITION]

    def kernel(*refs):
        groups = len(plan.groups)
        edge, refs = refs[0], refs[1:]
        own, packed_ref = refs[:groups], refs[groups]
        count = len(plan.parts[0])
        outs = refs[groups + 1 : groups + 1 + count], refs[groups + 1 + count : groups + 1 + 2 * count]
        edges, semaphores = refs[groups + 1 + 2 * count : -1], refs[-1]
        copies = []

        def copy(source, target):
            copies.append(pltpu.make_async_copy(source, target, semaphores.at[len(copies)]))
            copies[-1].start()

        for side, out in enumerate(outs):
            for group, array in enumerate(own):
                depth = depths[group][side]
                planes = pl.ds(plan.x - depth, depth) if side == 0 else pl.ds(0, depth)
                copy(array.at[:, planes], edges[2 * group + side])
            first = plan.x - needed[0] if side == 0 else 0
            at = plan.packed_at[side]
            for k in range(needed[side]):
                row, lanes = plan.folded(k, at)
                part, row = part_of(out, row)
                copy(packed_ref.at[first + k], part.at[row, :, pl.ds(lanes, LANES)])
        for one in copies:
            one.wait()
        for side, out in enumerate(outs):
            for field in plan.fields:
                at = (field.low_at, field.high_at)[side]
                depth = (field.low, field.high)[side] - field.skip

                def get(argument, part):
                    held = edges[2 * argument + side]
                    first = depths[argument][0] - field.low if side == 0 else field.skip
                    return held[part, first : first + depth]

                part, at = part_of(out, at)
                part[at : at + depth] = plan.value(field.group, field.component, get)

        for side, parts in enumerate(outs):

            @pl.when(edge[1 - side] == 0.0)
            def _(parts=parts):
                for part in parts:
                    part[...] = jnp.zeros(part.shape, jnp.float32)

    shapes = [(size, plan.y, plan.z) for side in plan.parts for size in side]
    scratch = [
        pltpu.VMEM((array.shape[0], depth, plan.y, plan.z), array.dtype)
        for array, pair in zip(arrays, depths)
        for depth in pair
    ]
    count = 2 * len(arrays) + sum(needed)
    outs = pl.pallas_call(
        kernel,
        in_specs=[in_smem()] + [any_space()] * (len(arrays) + 1),
        out_specs=[in_vmem()] * len(shapes),
        out_shape=[jax.ShapeDtypeStruct(shape, jnp.float32) for shape in shapes],
        scratch_shapes=scratch + [pltpu.SemaphoreType.DMA((count,))],
        compiler_params=pltpu.CompilerParams(vmem_limit_bytes=VMEM_BYTES),
        cost_estimate=cost(0.5),
        name="pack_planes",
    )(flags, *arrays, packed)
    return list(zip(outs[: len(plan.parts[0])], outs[len(plan.parts[0]) :]))


def pack_rows(plan, flags, arrays, packed, own, planes=(), inner_planes=()):
    groups = len(plan.groups)
    sizes, packed_at = plan.sizes[2:], plan.packed_at[2:]
    if own:
        sizes, packed_at = plan.sizes[:2], plan.packed_at[:2]

    def kernel(flags, *refs):
        for parity in range(2):
            up, down = refs[-2:] if parity == 0 else refs[:-3:-1]
            pl.when(flags[6] == parity)(functools.partial(pack, flags, list(refs[:-2]), up, down))

    def pack(flags, refs, up, down):
        up[...] = jnp.zeros(up.shape, jnp.float32)
        down[...] = jnp.zeros(down.shape, jnp.float32)

        def put(plane, field, first, last):
            low_at, high_at, skip = field.full_low_at, field.full_high_at, 0
            if own:
                low_at, high_at, skip = field.low_at, field.high_at, field.skip
            low, high = field.low - skip, field.high - skip
            up[plane, low_at : low_at + low, :] = last[ROWS - field.low : ROWS - skip, :]
            down[plane, high_at : high_at + high, :] = first[skip : field.high, :]

        def put_packed(plane, first, last, at):
            for k in range(plan.low):
                row, lanes = plan.folded(k, packed_at[0])
                source = ROWS - plan.low + k
                up[plane, row : row + 1, lanes : lanes + LANES] = last[
                    source : source + 1, at : at + LANES
                ]
            for k in range(plan.high):
                row, lanes = plan.folded(k, packed_at[1])
                down[plane, row : row + 1, lanes : lanes + LANES] = first[
                    k : k + 1, at : at + LANES
                ]

        base = 0
        if own:
            blocks = refs[: 2 * groups + 2]
            del refs[: 2 * groups + 2]
            base = plan.x

            def own_plane(x, _):
                for field in plan.fields:
                    first, last = [
                        plan.value(
                            *field[:2],
                            lambda argument, part: blocks[2 * argument + side][part, x],
                        )
                        for side in range(2)
                    ]
                    put(x, field, first, last)
                put_packed(x, blocks[-2].at[x], blocks[-1].at[x], 0)
                return 0

            lax.fori_loop(0, plan.x, own_plane, 0)
        if planes:
            count = len(plan.parts[0])
            pairs = [tuple(refs[2 * k : 2 * k + 2]) for k in range(2 * count + 2)]
            if plan.inner is None:
                pairs = pairs[: 2 * count]
            sides = [pairs[:count], pairs[count : 2 * count]]
            inner_sides = [pairs[2 * count : 2 * count + 1], pairs[2 * count + 1 :]]

            def find(parts, at):
                part, at = part_of([first for first, _ in parts], at)
                pair = next(pair for pair in parts if pair[0] is part)
                return [ref.at[at] for ref in pair]

            for side in range(2):
                for k in range((plan.low, plan.high)[side]):
                    for field in plan.fields:
                        depth, at = (field.low, field.low_at) if side == 0 else (field.high, field.high_at)
                        j = plan.low - k if side == 0 else k + 1
                        if j > depth:
                            continue
                        if j > field.skip:
                            source = at + (depth - j if side == 0 else j - 1 - field.skip)
                            parts = sides[side]
                        else:
                            other = plan.inner.fields[field.group]
                            source = other.low_at + other.low - j if side == 0 else other.high_at + j - 1
                            parts = inner_sides[side]
                        put(base + k, field, *find(parts, source))
                    source, lanes = plan.folded(k, plan.packed_at[side])
                    put_packed(base + k, *find(sides[side], source), lanes)
                base += plan.low

        @pl.when(flags[3] == 0.0)
        def _():
            up[...] = jnp.zeros(up.shape, jnp.float32)

        @pl.when(flags[2] == 0.0)
        def _():
            down[...] = jnp.zeros(down.shape, jnp.float32)

    last = plan.y // ROWS - 1
    specs, operands = [in_smem()], [flags]
    if own:
        for array in arrays:
            block = (array.shape[0], plan.x, ROWS, plan.z)
            specs.append(pl.BlockSpec(block, lambda i: (0, 0, 0, 0)))
            specs.append(pl.BlockSpec(block, lambda i: (0, 0, last, 0)))
            operands += [array, array]
    for array in ([packed] if own else []) + [*planes, *inner_planes]:
        block = (array.shape[0], ROWS, array.shape[2])
        specs.append(pl.BlockSpec(block, lambda i: (0, 0, 0)))
        specs.append(pl.BlockSpec(block, lambda i: (0, last, 0)))
        operands += [array, array]
    count = plan.x * own + (plan.low + plan.high) * bool(planes)
    shapes = [(count, round_up(max(sizes), ROWS), plan.z)] * 2
    return pl.pallas_call(
        kernel,
        grid=(1,),
        in_specs=specs,
        out_specs=[pl.BlockSpec(shape, lambda i: (0, 0, 0)) for shape in shapes],
        out_shape=[jax.ShapeDtypeStruct(shape, jnp.float32) for shape in shapes],
        compiler_params=pltpu.CompilerParams(vmem_limit_bytes=VMEM_BYTES),
        cost_estimate=cost(0.5),
        name="pack_rows",
    )(*operands)


def exchange_planes(pair):
    count = lax.axis_size("bx")
    return [
        lax.ppermute(one, "bx", [(i, (i + step) % count) for i in range(count)])
        for one, step in zip(pair, (1, -1))
    ]


def exchange_rows(pair):
    count = lax.axis_size("by")
    got = []
    for parity, one in enumerate(pair):
        partner = list(range(count))
        for i in range(parity, count - 1, 2):
            partner[i], partner[i + 1] = i + 1, i
        got.append(lax.ppermute(one, "by", list(enumerate(partner))))
    return got


def assemble(plan, flags, arrays, messages, inner, extended, packed_ext, pinned_own, semaphores):
    count = len(plan.parts[0])
    packed, below, above = messages[0], messages[1 : 1 + count], messages[1 + count : 1 + 2 * count]
    rest = messages[1 + 2 * count :]
    own_messages, halo_messages, halo_at = rest[:2], rest[-2:], plan.x if len(rest) == 2 else 0
    copies = []

    def copy(source, target):
        copies.append(
            pltpu.make_async_copy(source, target, semaphores.at[len(copies)])
        )
        copies[-1].start()

    own_rows = pl.ds(ROWS, plan.y)
    own_planes = pl.ds(plan.low, plan.x)
    for field in plan.fields:
        group, component, low, high, skip = field[:5]
        target = extended[group].at[component]
        after = plan.low + plan.x
        for t in range(plan.tiles):
            lanes = pl.ds(t * LANES, LANES)

            def planes(source, at, first, count):
                if count:
                    source, at = part_of(source, at)
                    copy(
                        source.at[pl.ds(at, count), :, lanes],
                        target.at[pl.ds(first, count), t, own_rows, :],
                    )

            place = target.at[own_planes, t, own_rows, :]
            if group == PINNED:
                place = pinned_own.at[:, t]
            copy(arrays[group].at[component, :, :, lanes], place)
            planes(below, field.low_at, plan.low - low, low - skip)
            planes(above, field.high_at, after + skip, high - skip)
            if skip:
                other = plan.inner.fields[group]
                planes(inner[:1], other.low_at, plan.low - skip, skip)
                planes(inner[1:2], other.high_at, after, skip)
    large = len(copies)
    copy(packed, packed_ext.at[own_planes, own_rows, :])
    for k in range(plan.low):
        source, lanes = plan.folded(k, plan.packed_at[0])
        part, source = part_of(below, source)
        copy(part.at[source, :, pl.ds(lanes, LANES)], packed_ext.at[k, own_rows, :])
    for k in range(plan.high):
        source, lanes = plan.folded(k, plan.packed_at[1])
        part, source = part_of(above, source)
        copy(
            part.at[source, :, pl.ds(lanes, LANES)],
            packed_ext.at[plan.low + plan.x + k, own_rows, :],
        )
    for one in copies[large:]:
        one.wait()

    top = ROWS + plan.y

    def fill(i, left, right, inner_left, inner_right, at, own):
        def rows(field, first, source, source_at, count):
            if count:
                for t in range(plan.tiles):
                    extended[field.group][field.component, i, t, first : first + count, :] = source[
                        at, source_at : source_at + count, t * LANES : (t + 1) * LANES
                    ]

        packed_at = plan.packed_at[:2] if own else plan.packed_at[2:]
        for field in plan.fields:
            low, high, skip = field.low, field.high, field.skip
            if own:
                rows(field, ROWS - low, left, field.low_at, low - skip)
                rows(field, top + skip, right, field.high_at, high - skip)
                if skip:
                    other = plan.inner.fields[field.group]
                    rows(field, ROWS - skip, inner_left, other.low_at, skip)
                    rows(field, top, inner_right, other.high_at, skip)
            else:
                rows(field, ROWS - low, left, field.full_low_at, low)
                rows(field, top, right, field.full_high_at, high)
        for k in range(plan.low):
            row, lanes = plan.folded(k, packed_at[0])
            to = ROWS - plan.low + k
            packed_ext[i, to : to + 1, :] = left[at, row : row + 1, lanes : lanes + LANES]
        for k in range(plan.high):
            row, lanes = plan.folded(k, packed_at[1])
            packed_ext[i, top + k : top + k + 1, :] = right[at, row : row + 1, lanes : lanes + LANES]
        tile = packed_ext[i]
        for field in plan.fields:
            extended[field.group][field.component, i, plan.tiles] = pltpu.roll(
                tile, (LANES - field.start) % LANES, 1
            )

    def fill_all(parity):
        def ordered(pair):
            return pair[::-1] if parity == 0 else pair

        own, halo = ordered(own_messages), ordered(halo_messages)
        inner_rows = (None, None) if inner is None else ordered(inner[2:4])

        def own_plane(x, _):
            fill(plan.low + x, *own, *inner_rows, x, True)
            return 0

        def low_plane(k, _):
            fill(k, *halo, None, None, halo_at + k, False)
            return 0

        def high_plane(k, _):
            fill(plan.low + plan.x + k, *halo, None, None, halo_at + plan.low + k, False)
            return 0

        lax.fori_loop(0, plan.x, own_plane, 0)
        lax.fori_loop(0, plan.low, low_plane, 0)
        lax.fori_loop(0, plan.high, high_plane, 0)

    def finish_plane(x, _):
        i = plan.low + x
        for t in range(plan.tiles):
            at = (i, t, slice(ROWS, top))

            def get(argument, component):
                if argument == PINNED:
                    return pinned_own[x, t]
                return extended[argument][(component, *at)]

            for group, component in [(POSITION, c) for c in range(3)] + [(PINNED, 0)]:
                extended[group][(component, *at)] = plan.value(group, component, get)
        return 0

    for parity in range(2):
        pl.when(flags[6] == parity)(functools.partial(fill_all, parity))
    for one in copies[:large]:
        one.wait()
    if pinned_own is not None:
        lax.fori_loop(0, plan.x, finish_plane, 0)


def assemble_copies(plan):
    skipping = sum(field.skip > 0 for field in plan.fields)
    return (3 * len(plan.fields) + 2 * skipping) * plan.tiles + 1 + plan.low + plan.high


def plane_loop(first, last, body, carried):
    def turn(i, carried, count):
        pending = []
        for k in range(count):
            carried, stores = body(i + k, carried)
            pending += stores
        for one in pending:
            store(*one)
        return carried

    count = last - first + 1
    carried = lax.fori_loop(
        0, count // UNROLL, lambda j, c: turn(first + j * UNROLL, c, UNROLL), carried
    )
    rest = count % UNROLL
    return turn(last + 1 - rest, carried, rest) if rest else carried


def load(ref, index, row):
    return [ref[(*index, t, pl.ds(row, ROWS), slice(None))] for t in range(ref.shape[-3])]


def store(ref, index, row, tiles):
    for t, tile in enumerate(tiles):
        ref[(*index, t, pl.ds(row, ROWS), slice(None))] = tile


def each(function, *tiles):
    return [function(*one) for one in zip(*tiles)]


def add(first, second):
    return each(lambda a, b: a + b, first, second)


def subtract(first, second):
    return each(lambda a, b: a - b, first, second)


def lane_below(tiles):
    lane = lane_index((ROWS, LANES))
    rolled = [pltpu.roll(tile, 1, 1) for tile in tiles]
    return [jnp.where(lane == 0, rolled[t - 1], rolled[t]) for t in range(len(tiles))]


def lane_above(tiles):
    lane = lane_index((ROWS, LANES))
    rolled = [pltpu.roll(tile, LANES - 1, 1) for tile in tiles]
    count = len(tiles)
    return [
        jnp.where(lane == LANES - 1, rolled[(t + 1) % count], rolled[t]) for t in range(count)
    ]


def chunks(first, last, body):
    count = -(-(last - first + 1) // ROWS)

    def one(j, _):
        body(jnp.minimum(first + j * ROWS, last - ROWS + 1))
        return 0

    lax.fori_loop(0, count, one, 0)


class Inside:
    def __init__(self, plan, flags):
        self.plan = plan
        self.flags = flags

    def tiles(self, row, scale):
        plan, flags = self.plan, self.flags
        rows = row + lax.broadcasted_iota(jnp.int32, (ROWS, LANES), 0)
        keep = jnp.where(rows < ROWS, flags[2], jnp.where(rows >= ROWS + plan.y, flags[3], 1.0))
        lane = lane_index((ROWS, LANES))
        edge = jnp.where(lane < LANES // 2, flags[5], flags[4])
        keep = scale * keep
        return [keep] * plan.tiles + [keep * edge]

    def plane(self, i):
        plan, flags = self.plan, self.flags
        return jnp.where(
            i < plan.low, flags[0], jnp.where(i >= plan.low + plan.x, flags[1], 1.0)
        )


def force_pass(density, energy, force, mass, inside, planes, rows):
    def chunk(row):
        keep = inside.tiles(row, 0.4 * 0.25)

        def slab(i):
            here, under = load(density, (0, i), row), load(density, (0, i), row - 1)
            p = each(lambda a, b: a * b, here, load(energy, (0, i), row))
            p_under = each(lambda a, b: a * b, under, load(energy, (0, i), row - 1))
            summed, stepped = add(p, p_under), subtract(p_under, p)
            weight = add(here, under)
            summed_z, stepped_z = lane_below(summed), lane_below(stepped)
            return (
                add(summed, summed_z),
                add(stepped, stepped_z),
                subtract(summed_z, summed),
                add(weight, lane_below(weight)),
            )

        def plane(i, before):
            now = slab(i)
            here = inside.plane(i)
            scale = [tile * here for tile in keep]
            stores = []
            for component in range(3):
                across = (subtract if component == 0 else add)(before[component], now[component])
                result = each(lambda a, b: a * b, scale, across)
                stores.append((force, (component, i), row, result))
            result = each(lambda a, b: 0.125 * (a + b) + 6.0 * CONSISTENT, before[3], now[3])
            stores.append((mass, (0, i), row, result))
            return now, stores

        plane_loop(*planes, plane, slab(planes[0] - 1))

    chunks(*rows, chunk)


def face_sum(ref, component, i, row, before, here, after):
    total = add(add(before, after), add(lane_below(here), lane_above(here)))
    return add(total, add(load(ref, (component, i), row - 1), load(ref, (component, i), row + 1)))


def stencil_pass(ref, planes, rows, setup, use):
    def chunk(row):
        given = setup(row)

        def plane(i, carried):
            before, here = carried
            after = [load(ref, (component, i + 1), row) for component in range(3)]
            sums = [
                face_sum(ref, component, i, row, before[component], here[component], after[component])
                for component in range(3)
            ]
            return (here, after), use(i, row, here, sums, given)

        first = [load(ref, (component, planes[0] - 1), row) for component in range(3)]
        second = [load(ref, (component, planes[0]), row) for component in range(3)]
        plane_loop(*planes, plane, (first, second))

    chunks(*rows, chunk)


def whole_sum(tile):
    return jnp.sum(jnp.sum(tile, axis=0, keepdims=True), axis=1, keepdims=True)


def moments_kernel(plan, *refs):
    flags, density, energy = refs[:3]
    messages, out = refs[3:8], refs[8]
    density_ext, energy_ext, packed_ext, force, image, mass, semaphores = refs[9:]
    assemble(
        plan,
        flags,
        [density, energy],
        messages,
        None,
        [density_ext, energy_ext],
        packed_ext,
        None,
        semaphores,
    )
    inside = Inside(plan, flags)
    low, x, y = plan.low, plan.x, plan.y
    force_pass(
        density_ext,
        energy_ext,
        force,
        mass,
        inside,
        (low - 1, low + x + 1),
        (ROWS - 1, ROWS + y + 1),
    )

    def multiply(i, row, here, sums, keep):
        weight = load(mass, (0, i), row)
        scale = [tile * inside.plane(i) for tile in keep]
        stores = []
        for component in range(3):
            result = each(
                lambda m, a, k, s: m * a + k * s, weight, here[component], scale, sums[component]
            )
            stores.append((image, (component, i), row, result))
        return stores

    stencil_pass(
        force,
        (low, low + x),
        (ROWS, ROWS + y),
        lambda row: inside.tiles(row, CONSISTENT),
        multiply,
    )

    own = range(plan.tiles)
    nothing = jnp.zeros((ROWS, LANES), jnp.float32)

    def first_chunk(j, sums):
        row = ROWS + j * ROWS

        def plane(i, sums):
            sums = list(sums)
            for component in range(3):
                f = load(force, (component, i), row)
                v = load(image, (component, i), row)
                for t in own:
                    sums[component] = sums[component] + f[t] * f[t]
                    sums[3 + component] = sums[3 + component] + f[t] * v[t]
            return tuple(sums), []

        return plane_loop(low, low + x - 1, plane, sums)

    sums = lax.fori_loop(0, y // ROWS, first_chunk, (nothing,) * 6)
    sums = [whole_sum(one) for one in sums]
    square = sums[:3]
    shift = [
        jnp.where(square[c] > 0, sums[3 + c] / jnp.where(square[c] > 0, square[c], 1.0), 0.0)
        for c in range(3)
    ]

    def pair(component, i, row):
        f = load(force, (component, i), row)
        v = load(image, (component, i), row)
        return f, each(lambda a, b: a - shift[component] * b, v, f)

    def second_chunk(j, sums):
        row = ROWS + j * ROWS

        def plane(i, carried):
            here, sums = carried
            sums = list(sums)
            ahead = [pair(component, i + 1, row) for component in range(3)]
            weight = load(mass, (0, i), row)
            for component in range(3):
                f, w = here[component]
                f_next, w_next = ahead[component]
                f_up, w_up = pair(component, i, row + 1)
                f_high = add(add(f_next, f_up), lane_above(f))
                w_high = add(add(w_next, w_up), lane_above(w))
                for t in own:
                    at = 5 * component
                    heavy = weight[t] * w[t]
                    sums[at] = sums[at] + f[t] * w[t]
                    sums[at + 1] = sums[at + 1] + w[t] * w[t]
                    sums[at + 2] = sums[at + 2] + (
                        f[t] * heavy + CONSISTENT * (f[t] * w_high[t] + w[t] * f_high[t])
                    )
                    sums[at + 3] = sums[at + 3] + w[t] * (
                        heavy + (2.0 * CONSISTENT) * w_high[t]
                    )
                    sums[at + 4] = sums[at + 4] + f[t] * (
                        weight[t] * f[t] + (2.0 * CONSISTENT) * f_high[t]
                    )
            return (ahead, tuple(sums)), []

        start = [pair(component, low, row) for component in range(3)]
        return plane_loop(low, low + x - 1, plane, (start, sums))[1]

    rest = lax.fori_loop(0, y // ROWS, second_chunk, (nothing,) * 15)
    lane = lane_index((1, LANES))
    line = jnp.zeros((1, LANES), jnp.float32)
    for c in range(3):
        values = [shift[c], square[c]] + [whole_sum(one) for one in rest[5 * c : 5 * c + 5]]
        for k, value in enumerate(values):
            line = jnp.where(lane == 3 * k + c, value, line)
    out[...] = line


def solve_weights(sums):
    got = [sums if k == 0 else pltpu.roll(sums, LANES - 3 * k, 1) for k in range(MOMENTS)]
    c, p0, q1, q2, q3, q4, q5 = got

    def total(value):
        return jnp.sum(value, axis=0, keepdims=True)

    norm_now = total(p0)
    alpha = norm_now / total(q1 + c * p0)
    a = 1.0 - alpha * c
    norm_next = total(a * a * p0 - 2.0 * a * alpha * q1 + alpha * alpha * q2)
    product = total(a * a * q5 - 2.0 * a * alpha * q3 + alpha * alpha * q4)
    ratio = norm_next / norm_now
    later = norm_next / (product - ratio * norm_next / alpha)
    lane = lane_index((1, LANES))

    def pick(value, component):
        return jnp.sum(jnp.where(lane == component, value, 0.0), axis=1, keepdims=True)

    on_force, on_image = alpha + later * (1.0 + ratio), -later * alpha
    return [(pick(on_force, k), pick(on_image, k)) for k in range(3)]


def step_kernel(plan, *refs):
    flags, sums, density, energy, position, velocity, pinned = refs[:7]
    messages, inner = refs[7:16], refs[16:20]
    velocity_new, accel, relaxed, density_new, energy_new = refs[20:25]
    (
        density_ext,
        energy_ext,
        moved,
        speed,
        free_ext,
        packed_ext,
        pinned_own,
        force,
        mass,
        other,
        semaphores,
        out_semaphores,
    ) = refs[25:]
    assemble(
        plan,
        flags,
        [density, energy, position, velocity, pinned],
        messages,
        inner,
        [density_ext, energy_ext, moved, speed, free_ext],
        packed_ext,
        pinned_own,
        semaphores,
    )
    inside = Inside(plan, flags)
    low, x, y = plan.low, plan.x, plan.y
    weights = solve_weights(sums[...])
    reach = SWEEPS + 1
    force_pass(
        density_ext,
        energy_ext,
        force,
        mass,
        inside,
        (low - reach, low + x + reach),
        (ROWS - reach, ROWS + y + reach),
    )

    def advance(i, row, here, sums, keep):
        weight = load(mass, (0, i), row)
        scale = [tile * inside.plane(i) for tile in keep]
        stores = []
        for component in range(3):
            on_force, on_image = weights[component]
            result = each(
                lambda m, a, k, s: on_force * a + on_image * (m * a + k * s),
                weight,
                here[component],
                scale,
                sums[component],
            )
            at = (component, i)
            faster = each(lambda v, a: v + TIME_STEP * a, load(speed, at, row), result)
            further = each(
                lambda b, a: b + (TIME_STEP * TIME_STEP) * a, load(moved, at, row), result
            )
            stores += [
                (other, at, row, result),
                (speed, at, row, faster),
                (moved, at, row, further),
            ]
        return stores

    reach -= 1
    advanced = round_up(y + 2 * reach + 1, ROWS)
    stencil_pass(
        force,
        (low - reach, low + x + reach),
        (ROWS - reach, ROWS - reach + advanced - 1),
        lambda row: inside.tiles(row, CONSISTENT),
        advance,
    )

    out_copies = []

    def write(source, target, component, result=None):
        for t in range(plan.tiles):
            place = target if result is None else target.at[result]
            out_copies.append(
                pltpu.make_async_copy(
                    source.at[component, pl.ds(low, x), t, pl.ds(ROWS, y), :],
                    place.at[:, :, pl.ds(t * LANES, LANES)],
                    out_semaphores.at[len(out_copies)],
                )
            )
            out_copies[-1].start()

    for component in range(3):
        write(other, accel, component, component)
    accel_copies = len(out_copies)
    for component in range(3):
        write(speed, velocity_new, component, component)

    content = mass

    def content_chunk(row):
        def slab(i):
            under = [load(speed, (component, i), row) for component in range(3)]
            over = [load(speed, (component, i), row + 1) for component in range(3)]
            along_x = add(under[0], over[0])
            along_y = subtract(over[1], under[1])
            along_z = add(under[2], over[2])
            along_x = add(along_x, lane_above(along_x))
            along_y = add(along_y, lane_above(along_y))
            along_z = subtract(lane_above(along_z), along_z)
            return along_x, add(along_y, along_z)

        def plane(i, before):
            now = slab(i + 1)
            spread = add(subtract(now[0], before[0]), add(now[1], before[1]))
            held = load(energy_ext, (0, i), row)
            lagged = each(lambda e, s: e - (0.25 * 0.4 * TIME_STEP) * (e * s), held, spread)
            result = each(lambda d, e: d * e, load(density_ext, (0, i), row), lagged)
            return now, [(content, (0, i), row, result)]

        plane_loop(low - 1, low + x, plane, slab(low - 1))

    chunks(ROWS - 1, ROWS + y, content_chunk)

    for one in out_copies[:accel_copies]:
        one.wait()
    source, target = moved, other
    for _ in range(SWEEPS):
        reach -= 1

        def relax(i, row, here, sums, given, target=target):
            rate = load(free_ext, (0, i), row)
            stores = []
            for component in range(3):
                result = each(
                    lambda r, s, f: r + f * (s * (1.0 / 6.0) - r),
                    here[component],
                    sums[component],
                    rate,
                )
                stores.append((target, (component, i), row, result))
            return stores

        stencil_pass(
            source,
            (low - reach, low + x + reach),
            (ROWS - reach, ROWS + y + reach),
            lambda row: None,
            relax,
        )
        source, target = target, (force if target is other else other)
    settled, free_buffer = source, target
    for component in range(3):
        write(settled, relaxed, component, component)

    quantities = (density_ext, content)

    def remap_chunk(row):
        def shift(component, i, at):
            return subtract(
                load(settled, (component, i), at), load(moved, (component, i), at)
            )

        def slab(i):
            x_here = add(shift(0, i, row), shift(0, i, row + 1))
            y_here, y_over = shift(1, i, row), shift(1, i, row + 1)
            z_here = add(shift(2, i, row), shift(2, i, row + 1))
            return (
                add(x_here, lane_above(x_here)),
                add(y_here, lane_above(y_here)),
                add(y_over, lane_above(y_over)),
                z_here,
                [load(one, (0, i), row) for one in quantities],
            )

        def flux(speeds, upper, lower):
            return each(lambda s, u, l: s * jnp.where(s > 0, u, l), speeds, upper, lower)

        def x_flux(speeds, upper, lower):
            return [flux(speeds, u, l) for u, l in zip(upper, lower)]

        def plane(i, carried):
            now, entering = carried
            ahead = slab(i + 1)
            leaving = x_flux(ahead[0], ahead[4], now[4])
            y_here, y_over, z_here = [add(now[k], ahead[k]) for k in (1, 2, 3)]
            stores = []
            for k, one in enumerate(quantities):
                held = now[4][k]
                under, over = load(one, (0, i), row - 1), load(one, (0, i), row + 1)
                through_z = flux(z_here, held, lane_below(held))
                change = subtract(leaving[k], entering[k])
                change = add(change, flux(y_over, over, held))
                change = subtract(change, flux(y_here, held, under))
                change = add(change, subtract(lane_above(through_z), through_z))
                result = each(lambda q, c: q + 0.25 * c, held, change)
                stores.append((free_buffer, (k, i), row, result[: plan.tiles]))
            return (ahead, leaving), stores

        start = slab(low)
        before = [load(one, (0, low - 1), row) for one in quantities]
        plane_loop(low, low + x - 1, plane, (start, x_flux(start[0], start[4], before)))

    chunks(ROWS, ROWS + y - 1, remap_chunk)
    write(free_buffer, density_new, 0)
    write(free_buffer, energy_new, 1)
    for one in out_copies[accel_copies:]:
        one.wait()


def gather_lines(line, axes):
    for axis in axes:
        count = lax.axis_size(axis)
        if count & (count - 1):
            line = lax.all_gather(line, axis, axis=0, tiled=True)
            continue
        step = 1
        while step < count:
            got = lax.ppermute(line, axis, [(i, i ^ step) for i in range(count)])
            later = (lax.axis_index(axis) // step) % 2 == 1
            line = jnp.concatenate([jnp.where(later, got, line), jnp.where(later, line, got)])
            step *= 2
    return line


def extended_scratch(plan, count):
    return pltpu.VMEM((count, plan.planes, plan.tiles + 1, plan.rows, LANES), jnp.float32)


def message_specs(planes, rows):
    return [any_space()] * planes + [in_vmem()] * rows


def on_device(position, velocity, density, energy, pinned):
    shape = density.shape
    arrays = [density[None], energy[None], position, velocity, pinned[None]]
    flags = jnp.stack(
        [
            jnp.float32(limit)
            for axis in ("bx", "by", "bz")
            for limit in (
                lax.axis_index(axis) > 0,
                lax.axis_index(axis) < lax.axis_size(axis) - 1,
            )
        ]
        + [(lax.axis_index("by") % 2).astype(jnp.float32)]
    )
    groups = [
        (1, WIDE, WIDE),
        (1, WIDE, WIDE),
        (3, SWEEPS, SWEEPS + 1),
        (3, 1, 2),
        (1, SWEEPS - 1, SWEEPS),
    ]
    narrow = Plan([(1, NARROW, NARROW)] * 2, shape)
    wide = Plan(groups, shape, narrow, cut=5)
    cells = arrays[:2]

    packed = exchange_lanes(narrow, pack_lanes(narrow, cells))
    planes = exchange_planes(*pack_planes(narrow, flags, cells, packed))
    wide_lanes = pack_lanes(wide, arrays)
    planes, wide_lanes = lax.optimization_barrier((planes, wide_lanes))
    wide_packed = exchange_lanes(wide, wide_lanes)
    rows = exchange_rows(pack_rows(narrow, flags, cells, packed, True, planes))

    first_planes, last_planes = pack_planes(wide, flags, arrays, wide_packed)
    wide_rows = pack_rows(wide, flags, arrays, wide_packed, True)
    rows, first_planes, last_planes, wide_rows = lax.optimization_barrier(
        (rows, first_planes, last_planes, wide_rows)
    )
    first_planes = exchange_planes(first_planes)
    last_planes = exchange_planes(last_planes)
    wide_rows = exchange_rows(wide_rows)

    line = pl.pallas_call(
        functools.partial(moments_kernel, narrow),
        in_specs=[in_smem()] + [any_space()] * 2 + message_specs(3, 2),
        out_specs=in_vmem(),
        out_shape=jax.ShapeDtypeStruct((1, LANES), jnp.float32),
        scratch_shapes=[
            extended_scratch(narrow, 1),
            extended_scratch(narrow, 1),
            pltpu.VMEM((narrow.planes, narrow.rows, LANES), jnp.float32),
            extended_scratch(narrow, 3),
            extended_scratch(narrow, 3),
            extended_scratch(narrow, 1),
            pltpu.SemaphoreType.DMA((assemble_copies(narrow),)),
        ],
        compiler_params=pltpu.CompilerParams(vmem_limit_bytes=VMEM_BYTES),
        cost_estimate=cost(1),
        name="moments",
    )(flags, *cells, packed, *planes, *rows)

    line, wide_rows, first_planes = lax.optimization_barrier((line, wide_rows, first_planes))
    lines = gather_lines(line, ("bz", "by"))
    lines, last_planes = lax.optimization_barrier((lines, last_planes))
    wide_planes = [pair[side] for side in range(2) for pair in (first_planes, last_planes)]
    corners = exchange_rows(pack_rows(wide, flags, None, None, False, wide_planes, planes))
    messages = [wide_packed, *wide_planes, *wide_rows, *corners]
    nodes = jax.ShapeDtypeStruct((3, *shape), jnp.float32)
    cell = jax.ShapeDtypeStruct(shape, jnp.float32)
    return pl.pallas_call(
        functools.partial(step_kernel, wide),
        in_specs=[in_smem(), in_vmem()] + [any_space()] * 5 + message_specs(5, 4) + message_specs(2, 2),
        out_specs=[any_space()] * 5,
        out_shape=[nodes, nodes, nodes, cell, cell],
        scratch_shapes=[
            extended_scratch(wide, 1),
            extended_scratch(wide, 1),
            extended_scratch(wide, 3),
            extended_scratch(wide, 3),
            extended_scratch(wide, 1),
            pltpu.VMEM((wide.planes, wide.rows, LANES), jnp.float32),
            pltpu.VMEM((wide.x, wide.tiles, wide.y, LANES), jnp.int32),
            extended_scratch(wide, 3),
            extended_scratch(wide, 1),
            extended_scratch(wide, 3),
            pltpu.SemaphoreType.DMA((assemble_copies(wide),)),
            pltpu.SemaphoreType.DMA((11 * wide.tiles,)),
        ],
        compiler_params=pltpu.CompilerParams(vmem_limit_bytes=VMEM_BYTES),
        cost_estimate=cost(1),
        name="step",
    )(flags, gather_lines(lines, ("bx",)), *arrays, *messages, *planes, *rows)


def solution(mesh):
    in_specs = (
        P(None, "bx", "by", "bz"),
        P(None, "bx", "by", "bz"),
        P("bx", "by", "bz"),
        P("bx", "by", "bz"),
        P("bx", "by", "bz"),
    )
    out_specs = (
        P(None, "bx", "by", "bz"),
        P(None, "bx", "by", "bz"),
        P(None, "bx", "by", "bz"),
        P("bx", "by", "bz"),
        P("bx", "by", "bz"),
    )
    return jax.shard_map(
        on_device, mesh=mesh, in_specs=in_specs, out_specs=out_specs, check_vma=False
    )
```

```python
import functools
import math
from typing import NamedTuple

import jax
import jax.numpy as jnp
from jax import lax
from jax.experimental import pallas as pl
from jax.experimental.pallas import tpu as pltpu
from jax.sharding import PartitionSpec as P

SWEEPS = 3
TIME_STEP = 0.6
RELAX_RATE = 0.8
CONSISTENT = 0.2

LANES = 128
ROWS = 8
MOMENTS = 7
UNROLL = 6
POSITION, VELOCITY, PINNED = 2, 3, 4
NARROW = 2
WIDE = SWEEPS + 2
VMEM_BYTES = 62 * 2**20


class Field(NamedTuple):
    group: int
    component: int
    low: int
    high: int
    skip: int
    low_at: int
    high_at: int
    full_low_at: int
    full_high_at: int
    start: int


class Plan:
    def __init__(self, groups, shape, inner=None, starts=None, cut=None):
        self.groups = groups
        self.inner = inner
        self.x, self.y, self.z = shape
        self.tiles = self.z // LANES
        self.low = max(low for _, low, _ in groups)
        self.high = max(high for _, _, high in groups)
        self.planes = self.low + self.x + self.high
        self.rows = self.y + 2 * ROWS
        self.fields = []
        at = [0] * 4
        lane_at = 0
        for group, (count, low, high) in enumerate(groups):
            skip = 0 if inner is None or group >= len(inner.groups) else inner.low
            for component in range(count):
                start = lane_at + low if starts is None else starts[len(self.fields)]
                self.fields.append(Field(group, component, low, high, skip, *at, start))
                for k, size in enumerate((low - skip, high - skip, low, high)):
                    at[k] += size
                lane_at += low + high
        assert lane_at <= LANES
        self.starts = [field.start for field in self.fields]
        self.packed_at = at
        depths = (self.low, self.high) * 2
        self.sizes = [one + -(-depth // self.tiles) for one, depth in zip(at, depths)]
        cuts = [] if cut is None else [(self.fields[cut].low_at, self.fields[cut].high_at)]
        self.parts = []
        for side in range(2):
            ends = [0, *(one[side] for one in cuts), self.sizes[side]]
            self.parts.append([b - a for a, b in zip(ends, ends[1:])])

    def value(self, group, component, get):
        if group == POSITION:
            return get(POSITION, component) + TIME_STEP * get(VELOCITY, component)
        if group == PINNED:
            return RELAX_RATE * (1.0 - get(PINNED, component).astype(jnp.float32))
        return get(group, component)

    def folded(self, k, at):
        return at + k // self.tiles, (k % self.tiles) * LANES


def round_up(value, step):
    return -(-value // step) * step


def from_behind(x, axis):
    count = lax.axis_size(axis)
    return lax.ppermute(x, axis, [(i, i + 1) for i in range(count - 1)])


def from_ahead(x, axis):
    count = lax.axis_size(axis)
    return lax.ppermute(x, axis, [(i + 1, i) for i in range(count - 1)])


def any_space():
    return pl.BlockSpec(memory_space=pl.ANY)


def in_vmem():
    return pl.BlockSpec(memory_space=pltpu.VMEM)


def in_smem():
    return pl.BlockSpec(memory_space=pltpu.SMEM)


def cost(microseconds):
    return pl.CostEstimate(
        flops=0, bytes_accessed=int(microseconds * 3.0e6), transcendentals=0
    )


def lane_index(shape):
    return lax.broadcasted_iota(jnp.int32, shape, len(shape) - 1)


def pack_lanes(plan, arrays):
    half = LANES // 2

    def kernel(*refs):
        out = refs[-1]
        lane = lane_index((plan.y, LANES))
        in_low_half = lane < half

        def plane(x, _):
            def edge(group, component):
                first, last = refs[2 * group], refs[2 * group + 1]
                return jnp.where(in_low_half, first[component, x], last[component, x])

            packed = jnp.zeros((plan.y, LANES), jnp.float32)
            for group, component, low, high, *_, start in plan.fields:
                moved = pltpu.roll(plan.value(group, component, edge), start, 1)
                packed = jnp.where((lane >= start - low) & (lane < start + high), moved, packed)
            out[x] = packed
            return 0

        for x in range(planes):
            plane(x, 0)

    planes = next(n for n in (16 if len(arrays) == 2 else 8, 4, 1) if plan.x % n == 0)
    specs, operands = [], []
    for (count, _, _), array in zip(plan.groups, arrays):
        block = (count, planes, plan.y, LANES)
        specs.append(pl.BlockSpec(block, lambda i: (0, i, 0, 0)))
        specs.append(pl.BlockSpec(block, lambda i: (0, i, 0, plan.tiles - 1)))
        operands += [array, array]
    return pl.pallas_call(
        kernel,
        grid=(plan.x // planes,),
        in_specs=specs,
        out_specs=pl.BlockSpec((planes, plan.y, LANES), lambda i: (i, 0, 0)),
        out_shape=jax.ShapeDtypeStruct((plan.x, plan.y, LANES), jnp.float32),
        compiler_params=pltpu.CompilerParams(vmem_limit_bytes=VMEM_BYTES),
        cost_estimate=cost(0.5),
        name="pack_lanes",
    )(*operands)


def exchange_lanes(plan, packed):
    lane = lane_index((1, 1, LANES))
    is_low = functools.reduce(
        jnp.logical_or,
        [(lane >= start - low) & (lane < start) for _, _, low, *_, start in plan.fields],
    )
    count = lax.axis_size("bz")
    if count == 2:
        got = lax.ppermute(packed, "bz", [(0, 1), (1, 0)])
        return jnp.where(is_low == (lax.axis_index("bz") == 1), got, 0.0)
    return jnp.where(is_low, from_behind(packed, "bz"), from_ahead(packed, "bz"))


def part_of(parts, at):
    for part in parts:
        if at < part.shape[0]:
            return part, at
        at -= part.shape[0]


def pack_planes(plan, flags, arrays, packed):
    needed = [
        max(low if to_low else high for _, low, high in plan.groups) for to_low in (True, False)
    ]
    depths = [(low, high) for _, low, high in plan.groups]
    if len(depths) > VELOCITY:
        depths[VELOCITY] = depths[POSITION]

    def kernel(*refs):
        groups = len(plan.groups)
        edge, refs = refs[0], refs[1:]
        own, packed_ref = refs[:groups], refs[groups]
        count = len(plan.parts[0])
        outs = refs[groups + 1 : groups + 1 + count], refs[groups + 1 + count : groups + 1 + 2 * count]
        edges, semaphores = refs[groups + 1 + 2 * count : -1], refs[-1]
        copies = []

        def copy(source, target):
            copies.append(pltpu.make_async_copy(source, target, semaphores.at[len(copies)]))
            copies[-1].start()

        for side, out in enumerate(outs):
            for group, array in enumerate(own):
                depth = depths[group][side]
                planes = pl.ds(plan.x - depth, depth) if side == 0 else pl.ds(0, depth)
                copy(array.at[:, planes], edges[2 * group + side])
            first = plan.x - needed[0] if side == 0 else 0
            at = plan.packed_at[side]
            for k in range(needed[side]):
                row, lanes = plan.folded(k, at)
                part, row = part_of(out, row)
                copy(packed_ref.at[first + k], part.at[row, :, pl.ds(lanes, LANES)])
        for one in copies:
            one.wait()
        for side, out in enumerate(outs):
            for field in plan.fields:
                at = (field.low_at, field.high_at)[side]
                depth = (field.low, field.high)[side] - field.skip

                def get(argument, part):
                    held = edges[2 * argument + side]
                    first = depths[argument][0] - field.low if side == 0 else field.skip
                    return held[part, first : first + depth]

                part, at = part_of(out, at)
                part[at : at + depth] = plan.value(field.group, field.component, get)

        for side, parts in enumerate(outs):

            @pl.when(edge[1 - side] == 0.0)
            def _(parts=parts):
                for part in parts:
                    part[...] = jnp.zeros(part.shape, jnp.float32)

    shapes = [(size, plan.y, plan.z) for side in plan.parts for size in side]
    scratch = [
        pltpu.VMEM((array.shape[0], depth, plan.y, plan.z), array.dtype)
        for array, pair in zip(arrays, depths)
        for depth in pair
    ]
    count = 2 * len(arrays) + sum(needed)
    outs = pl.pallas_call(
        kernel,
        in_specs=[in_smem()] + [any_space()] * (len(arrays) + 1),
        out_specs=[in_vmem()] * len(shapes),
        out_shape=[jax.ShapeDtypeStruct(shape, jnp.float32) for shape in shapes],
        scratch_shapes=scratch + [pltpu.SemaphoreType.DMA((count,))],
        compiler_params=pltpu.CompilerParams(vmem_limit_bytes=VMEM_BYTES),
        cost_estimate=cost(0.5),
        name="pack_planes",
    )(flags, *arrays, packed)
    return list(zip(outs[: len(plan.parts[0])], outs[len(plan.parts[0]) :]))


def pack_rows(plan, flags, arrays, packed, own, planes=(), inner_planes=()):
    groups = len(plan.groups)
    sizes, packed_at = plan.sizes[2:], plan.packed_at[2:]
    if own:
        sizes, packed_at = plan.sizes[:2], plan.packed_at[:2]

    def kernel(flags, *refs):
        for parity in range(2):
            up, down = refs[-2:] if parity == 0 else refs[:-3:-1]
            pl.when(flags[6] == parity)(functools.partial(pack, flags, list(refs[:-2]), up, down))

    def pack(flags, refs, up, down):
        up[...] = jnp.zeros(up.shape, jnp.float32)
        down[...] = jnp.zeros(down.shape, jnp.float32)

        def put(plane, field, first, last):
            low_at, high_at, skip = field.full_low_at, field.full_high_at, 0
            if own:
                low_at, high_at, skip = field.low_at, field.high_at, field.skip
            low, high = field.low - skip, field.high - skip
            up[plane, low_at : low_at + low, :] = last[ROWS - field.low : ROWS - skip, :]
            down[plane, high_at : high_at + high, :] = first[skip : field.high, :]

        def put_packed(plane, first, last, at):
            for k in range(plan.low):
                row, lanes = plan.folded(k, packed_at[0])
                source = ROWS - plan.low + k
                up[plane, row : row + 1, lanes : lanes + LANES] = last[
                    source : source + 1, at : at + LANES
                ]
            for k in range(plan.high):
                row, lanes = plan.folded(k, packed_at[1])
                down[plane, row : row + 1, lanes : lanes + LANES] = first[
                    k : k + 1, at : at + LANES
                ]

        base = 0
        if own:
            blocks = refs[: 2 * groups + 2]
            del refs[: 2 * groups + 2]
            base = plan.x

            def own_plane(x, _):
                for field in plan.fields:
                    first, last = [
                        plan.value(
                            *field[:2],
                            lambda argument, part: blocks[2 * argument + side][part, x],
                        )
                        for side in range(2)
                    ]
                    put(x, field, first, last)
                put_packed(x, blocks[-2].at[x], blocks[-1].at[x], 0)
                return 0

            lax.fori_loop(0, plan.x, own_plane, 0)
        if planes:
            count = len(plan.parts[0])
            pairs = [tuple(refs[2 * k : 2 * k + 2]) for k in range(2 * count + 2)]
            if plan.inner is None:
                pairs = pairs[: 2 * count]
            sides = [pairs[:count], pairs[count : 2 * count]]
            inner_sides = [pairs[2 * count : 2 * count + 1], pairs[2 * count + 1 :]]

            def find(parts, at):
                part, at = part_of([first for first, _ in parts], at)
                pair = next(pair for pair in parts if pair[0] is part)
                return [ref.at[at] for ref in pair]

            for side in range(2):
                for k in range((plan.low, plan.high)[side]):
                    for field in plan.fields:
                        depth, at = (field.low, field.low_at) if side == 0 else (field.high, field.high_at)
                        j = plan.low - k if side == 0 else k + 1
                        if j > depth:
                            continue
                        if j > field.skip:
                            source = at + (depth - j if side == 0 else j - 1 - field.skip)
                            parts = sides[side]
                        else:
                            other = plan.inner.fields[field.group]
                            source = other.low_at + other.low - j if side == 0 else other.high_at + j - 1
                            parts = inner_sides[side]
                        put(base + k, field, *find(parts, source))
                    source, lanes = plan.folded(k, plan.packed_at[side])
                    put_packed(base + k, *find(sides[side], source), lanes)
                base += plan.low

        @pl.when(flags[3] == 0.0)
        def _():
            up[...] = jnp.zeros(up.shape, jnp.float32)

        @pl.when(flags[2] == 0.0)
        def _():
            down[...] = jnp.zeros(down.shape, jnp.float32)

    last = plan.y // ROWS - 1
    specs, operands = [in_smem()], [flags]
    if own:
        for array in arrays:
            block = (array.shape[0], plan.x, ROWS, plan.z)
            specs.append(pl.BlockSpec(block, lambda i: (0, 0, 0, 0)))
            specs.append(pl.BlockSpec(block, lambda i: (0, 0, last, 0)))
            operands += [array, array]
    for array in ([packed] if own else []) + [*planes, *inner_planes]:
        block = (array.shape[0], ROWS, array.shape[2])
        specs.append(pl.BlockSpec(block, lambda i: (0, 0, 0)))
        specs.append(pl.BlockSpec(block, lambda i: (0, last, 0)))
        operands += [array, array]
    count = plan.x * own + (plan.low + plan.high) * bool(planes)
    shapes = [(count, round_up(max(sizes), ROWS), plan.z)] * 2
    return pl.pallas_call(
        kernel,
        grid=(1,),
        in_specs=specs,
        out_specs=[pl.BlockSpec(shape, lambda i: (0, 0, 0)) for shape in shapes],
        out_shape=[jax.ShapeDtypeStruct(shape, jnp.float32) for shape in shapes],
        compiler_params=pltpu.CompilerParams(vmem_limit_bytes=VMEM_BYTES),
        cost_estimate=cost(0.5),
        name="pack_rows",
    )(*operands)


def exchange_planes(pair):
    count = lax.axis_size("bx")
    return [
        lax.ppermute(one, "bx", [(i, (i + step) % count) for i in range(count)])
        for one, step in zip(pair, (1, -1))
    ]


def exchange_rows(pair):
    count = lax.axis_size("by")
    got = []
    for parity, one in enumerate(pair):
        partner = list(range(count))
        for i in range(parity, count - 1, 2):
            partner[i], partner[i + 1] = i + 1, i
        got.append(lax.ppermute(one, "by", list(enumerate(partner))))
    return got


def assemble(plan, flags, arrays, messages, inner, extended, packed_ext, pinned_own, semaphores):
    count = len(plan.parts[0])
    packed, below, above = messages[0], messages[1 : 1 + count], messages[1 + count : 1 + 2 * count]
    rest = messages[1 + 2 * count :]
    own_messages, halo_messages, halo_at = rest[:2], rest[-2:], plan.x if len(rest) == 2 else 0
    copies = []

    def copy(source, target):
        copies.append(
            pltpu.make_async_copy(source, target, semaphores.at[len(copies)])
        )
        copies[-1].start()

    own_rows = pl.ds(ROWS, plan.y)
    own_planes = pl.ds(plan.low, plan.x)
    for field in plan.fields:
        group, component, low, high, skip = field[:5]
        target = extended[group].at[component]
        after = plan.low + plan.x
        for t in range(plan.tiles):
            lanes = pl.ds(t * LANES, LANES)

            def planes(source, at, first, count):
                if count:
                    source, at = part_of(source, at)
                    copy(
                        source.at[pl.ds(at, count), :, lanes],
                        target.at[pl.ds(first, count), t, own_rows, :],
                    )

            place = target.at[own_planes, t, own_rows, :]
            if group == PINNED:
                place = pinned_own.at[:, t]
            copy(arrays[group].at[component, :, :, lanes], place)
            planes(below, field.low_at, plan.low - low, low - skip)
            planes(above, field.high_at, after + skip, high - skip)
            if skip:
                other = plan.inner.fields[group]
                planes(inner[:1], other.low_at, plan.low - skip, skip)
                planes(inner[1:2], other.high_at, after, skip)
    large = len(copies)
    copy(packed, packed_ext.at[own_planes, own_rows, :])
    for k in range(plan.low):
        source, lanes = plan.folded(k, plan.packed_at[0])
        part, source = part_of(below, source)
        copy(part.at[source, :, pl.ds(lanes, LANES)], packed_ext.at[k, own_rows, :])
    for k in range(plan.high):
        source, lanes = plan.folded(k, plan.packed_at[1])
        part, source = part_of(above, source)
        copy(
            part.at[source, :, pl.ds(lanes, LANES)],
            packed_ext.at[plan.low + plan.x + k, own_rows, :],
        )
    for one in copies[large:]:
        one.wait()

    top = ROWS + plan.y

    def fill(i, left, right, inner_left, inner_right, at, own):
        def rows(field, first, source, source_at, count):
            if count:
                for t in range(plan.tiles):
                    extended[field.group][field.component, i, t, first : first + count, :] = source[
                        at, source_at : source_at + count, t * LANES : (t + 1) * LANES
                    ]

        packed_at = plan.packed_at[:2] if own else plan.packed_at[2:]
        for field in plan.fields:
            low, high, skip = field.low, field.high, field.skip
            if own:
                rows(field, ROWS - low, left, field.low_at, low - skip)
                rows(field, top + skip, right, field.high_at, high - skip)
                if skip:
                    other = plan.inner.fields[field.group]
                    rows(field, ROWS - skip, inner_left, other.low_at, skip)
                    rows(field, top, inner_right, other.high_at, skip)
            else:
                rows(field, ROWS - low, left, field.full_low_at, low)
                rows(field, top, right, field.full_high_at, high)
        for k in range(plan.low):
            row, lanes = plan.folded(k, packed_at[0])
            to = ROWS - plan.low + k
            packed_ext[i, to : to + 1, :] = left[at, row : row + 1, lanes : lanes + LANES]
        for k in range(plan.high):
            row, lanes = plan.folded(k, packed_at[1])
            packed_ext[i, top + k : top + k + 1, :] = right[at, row : row + 1, lanes : lanes + LANES]
        tile = packed_ext[i]
        for field in plan.fields:
            extended[field.group][field.component, i, plan.tiles] = pltpu.roll(
                tile, (LANES - field.start) % LANES, 1
            )

    def fill_all(parity):
        def ordered(pair):
            return pair[::-1] if parity == 0 else pair

        own, halo = ordered(own_messages), ordered(halo_messages)
        inner_rows = (None, None) if inner is None else ordered(inner[2:4])

        def own_plane(x, _):
            fill(plan.low + x, *own, *inner_rows, x, True)
            return 0

        def low_plane(k, _):
            fill(k, *halo, None, None, halo_at + k, False)
            return 0

        def high_plane(k, _):
            fill(plan.low + plan.x + k, *halo, None, None, halo_at + plan.low + k, False)
            return 0

        lax.fori_loop(0, plan.x, own_plane, 0)
        lax.fori_loop(0, plan.low, low_plane, 0)
        lax.fori_loop(0, plan.high, high_plane, 0)

    def finish_plane(x, _):
        i = plan.low + x
        for t in range(plan.tiles):
            at = (i, t, slice(ROWS, top))

            def get(argument, component):
                if argument == PINNED:
                    return pinned_own[x, t]
                return extended[argument][(component, *at)]

            for group, component in [(POSITION, c) for c in range(3)] + [(PINNED, 0)]:
                extended[group][(component, *at)] = plan.value(group, component, get)
        return 0

    for parity in range(2):
        pl.when(flags[6] == parity)(functools.partial(fill_all, parity))
    for one in copies[:large]:
        one.wait()
    if pinned_own is not None:
        lax.fori_loop(0, plan.x, finish_plane, 0)


def assemble_copies(plan):
    skipping = sum(field.skip > 0 for field in plan.fields)
    return (3 * len(plan.fields) + 2 * skipping) * plan.tiles + 1 + plan.low + plan.high


def plane_loop(ref, first, last, row, body, carried):
    def turn(plane, carried, count):
        here = spot(ref, plane, row)
        pending = []
        for k in range(count):
            carried, stores = body(here.at_plane(k), carried)
            pending += stores
        for one in pending:
            store(*one)
        return carried

    count = last - first + 1
    carried = lax.fori_loop(
        0, count // UNROLL, lambda j, c: turn(first + j * UNROLL, c, UNROLL), carried
    )
    rest = count % UNROLL
    return turn(last + 1 - rest, carried, rest) if rest else carried


class Spot(NamedTuple):
    base: jax.Array
    plane: jax.Array
    planes: int = 0
    rows: int = 0

    def at_plane(self, step):
        return self._replace(planes=self.planes + step)

    def at_row(self, step):
        return self._replace(rows=self.rows + step)


def spot(ref, plane, row):
    return Spot(plane * (ref.shape[-3] * ref.shape[-2]) + row, plane)


def tile_rows(ref, component, at):
    planes, tiles, rows, lanes = ref.shape[-4:]
    first = (component * planes + at.planes) * tiles * rows + at.rows
    flat = ref.reshape(math.prod(ref.shape[:-1]), lanes)
    return flat, [at.base + (first + t * rows) for t in range(tiles)]


def load(ref, component, at):
    flat, starts = tile_rows(ref, component, at)
    return [flat[pl.ds(start, ROWS), :] for start in starts]


def store(ref, component, at, tiles):
    flat, starts = tile_rows(ref, component, at)
    for start, tile in zip(starts, tiles):
        flat[pl.ds(start, ROWS), :] = tile


def each(function, *tiles):
    return [function(*one) for one in zip(*tiles)]


def add(first, second):
    return each(lambda a, b: a + b, first, second)


def subtract(first, second):
    return each(lambda a, b: a - b, first, second)


def lane_below(tiles):
    lane = lane_index((ROWS, LANES))
    rolled = [pltpu.roll(tile, 1, 1) for tile in tiles]
    return [jnp.where(lane == 0, rolled[t - 1], rolled[t]) for t in range(len(tiles))]


def lane_above(tiles):
    lane = lane_index((ROWS, LANES))
    rolled = [pltpu.roll(tile, LANES - 1, 1) for tile in tiles]
    count = len(tiles)
    return [
        jnp.where(lane == LANES - 1, rolled[(t + 1) % count], rolled[t]) for t in range(count)
    ]


def chunks(first, last, body):
    count = -(-(last - first + 1) // ROWS)

    def one(j, _):
        body(jnp.minimum(first + j * ROWS, last - ROWS + 1))
        return 0

    lax.fori_loop(0, count, one, 0)


class Inside:
    def __init__(self, plan, flags):
        self.plan = plan
        self.flags = flags

    def tiles(self, row, scale):
        plan, flags = self.plan, self.flags
        rows = row + lax.broadcasted_iota(jnp.int32, (ROWS, LANES), 0)
        keep = jnp.where(rows < ROWS, flags[2], jnp.where(rows >= ROWS + plan.y, flags[3], 1.0))
        lane = lane_index((ROWS, LANES))
        edge = jnp.where(lane < LANES // 2, flags[5], flags[4])
        keep = scale * keep
        return [keep] * plan.tiles + [keep * edge]

    def plane(self, at):
        plan, flags = self.plan, self.flags
        i = at.plane + at.planes
        return jnp.where(
            i < plan.low, flags[0], jnp.where(i >= plan.low + plan.x, flags[1], 1.0)
        )


def force_pass(density, energy, force, mass, inside, planes, rows):
    def chunk(row):
        keep = inside.tiles(row, 0.4 * 0.25)

        def slab(at):
            here, under = load(density, 0, at), load(density, 0, at.at_row(-1))
            p = each(lambda a, b: a * b, here, load(energy, 0, at))
            p_under = each(lambda a, b: a * b, under, load(energy, 0, at.at_row(-1)))
            summed, stepped = add(p, p_under), subtract(p_under, p)
            weight = add(here, under)
            summed_z, stepped_z = lane_below(summed), lane_below(stepped)
            return (
                add(summed, summed_z),
                add(stepped, stepped_z),
                subtract(summed_z, summed),
                add(weight, lane_below(weight)),
            )

        def plane(at, before):
            now = slab(at)
            here = inside.plane(at)
            scale = [tile * here for tile in keep]
            stores = []
            for component in range(3):
                across = (subtract if component == 0 else add)(before[component], now[component])
                result = each(lambda a, b: a * b, scale, across)
                stores.append((force, component, at, result))
            result = each(lambda a, b: 0.125 * (a + b) + 6.0 * CONSISTENT, before[3], now[3])
            stores.append((mass, 0, at, result))
            return now, stores

        plane_loop(density, *planes, row, plane, slab(spot(density, planes[0] - 1, row)))

    chunks(*rows, chunk)


def face_sum(ref, component, at, before, here, after):
    total = add(add(before, after), add(lane_below(here), lane_above(here)))
    sides = add(load(ref, component, at.at_row(-1)), load(ref, component, at.at_row(1)))
    return add(total, sides)


def stencil_pass(ref, planes, rows, setup, use):
    def chunk(row):
        given = setup(row)

        def plane(at, carried):
            before, here = carried
            after = [load(ref, component, at.at_plane(1)) for component in range(3)]
            sums = [
                face_sum(ref, component, at, before[component], here[component], after[component])
                for component in range(3)
            ]
            return (here, after), use(at, here, sums, given)

        start = spot(ref, planes[0], row)
        first = [load(ref, component, start.at_plane(-1)) for component in range(3)]
        second = [load(ref, component, start) for component in range(3)]
        plane_loop(ref, *planes, row, plane, (first, second))

    chunks(*rows, chunk)


def whole_sum(tile):
    return jnp.sum(jnp.sum(tile, axis=0, keepdims=True), axis=1, keepdims=True)


def moments_kernel(plan, *refs):
    flags, density, energy = refs[:3]
    messages, out = refs[3:8], refs[8]
    density_ext, energy_ext, packed_ext, force, image, mass, semaphores = refs[9:]
    assemble(
        plan,
        flags,
        [density, energy],
        messages,
        None,
        [density_ext, energy_ext],
        packed_ext,
        None,
        semaphores,
    )
    inside = Inside(plan, flags)
    low, x, y = plan.low, plan.x, plan.y
    force_pass(
        density_ext,
        energy_ext,
        force,
        mass,
        inside,
        (low - 1, low + x + 1),
        (ROWS - 1, ROWS + y + 1),
    )

    def multiply(at, here, sums, keep):
        weight = load(mass, 0, at)
        scale = [tile * inside.plane(at) for tile in keep]
        stores = []
        for component in range(3):
            result = each(
                lambda m, a, k, s: m * a + k * s, weight, here[component], scale, sums[component]
            )
            stores.append((image, component, at, result))
        return stores

    stencil_pass(
        force,
        (low, low + x),
        (ROWS, ROWS + y),
        lambda row: inside.tiles(row, CONSISTENT),
        multiply,
    )

    own = range(plan.tiles)
    nothing = jnp.zeros((ROWS, LANES), jnp.float32)

    def first_chunk(j, sums):
        row = ROWS + j * ROWS

        def plane(at, sums):
            sums = list(sums)
            for component in range(3):
                f = load(force, component, at)
                v = load(image, component, at)
                for t in own:
                    sums[component] = sums[component] + f[t] * f[t]
                    sums[3 + component] = sums[3 + component] + f[t] * v[t]
            return tuple(sums), []

        return plane_loop(force, low, low + x - 1, row, plane, sums)

    sums = lax.fori_loop(0, y // ROWS, first_chunk, (nothing,) * 6)
    sums = [whole_sum(one) for one in sums]
    square = sums[:3]
    shift = [
        jnp.where(square[c] > 0, sums[3 + c] / jnp.where(square[c] > 0, square[c], 1.0), 0.0)
        for c in range(3)
    ]

    def pair(component, at):
        f = load(force, component, at)
        v = load(image, component, at)
        return f, each(lambda a, b: a - shift[component] * b, v, f)

    def second_chunk(j, sums):
        row = ROWS + j * ROWS

        def plane(at, carried):
            here, sums = carried
            sums = list(sums)
            ahead = [pair(component, at.at_plane(1)) for component in range(3)]
            weight = load(mass, 0, at)
            for component in range(3):
                f, w = here[component]
                f_next, w_next = ahead[component]
                f_up, w_up = pair(component, at.at_row(1))
                f_high = add(add(f_next, f_up), lane_above(f))
                w_high = add(add(w_next, w_up), lane_above(w))
                for t in own:
                    k = 5 * component
                    heavy = weight[t] * w[t]
                    sums[k] = sums[k] + f[t] * w[t]
                    sums[k + 1] = sums[k + 1] + w[t] * w[t]
                    sums[k + 2] = sums[k + 2] + (
                        f[t] * heavy + CONSISTENT * (f[t] * w_high[t] + w[t] * f_high[t])
                    )
                    sums[k + 3] = sums[k + 3] + w[t] * (
                        heavy + (2.0 * CONSISTENT) * w_high[t]
                    )
                    sums[k + 4] = sums[k + 4] + f[t] * (
                        weight[t] * f[t] + (2.0 * CONSISTENT) * f_high[t]
                    )
            return (ahead, tuple(sums)), []

        start = [pair(component, spot(force, low, row)) for component in range(3)]
        return plane_loop(force, low, low + x - 1, row, plane, (start, sums))[1]

    rest = lax.fori_loop(0, y // ROWS, second_chunk, (nothing,) * 15)
    lane = lane_index((1, LANES))
    line = jnp.zeros((1, LANES), jnp.float32)
    for c in range(3):
        values = [shift[c], square[c]] + [whole_sum(one) for one in rest[5 * c : 5 * c + 5]]
        for k, value in enumerate(values):
            line = jnp.where(lane == 3 * k + c, value, line)
    out[...] = line


def solve_weights(sums):
    got = [sums if k == 0 else pltpu.roll(sums, LANES - 3 * k, 1) for k in range(MOMENTS)]
    c, p0, q1, q2, q3, q4, q5 = got

    def total(value):
        return jnp.sum(value, axis=0, keepdims=True)

    norm_now = total(p0)
    alpha = norm_now / total(q1 + c * p0)
    a = 1.0 - alpha * c
    norm_next = total(a * a * p0 - 2.0 * a * alpha * q1 + alpha * alpha * q2)
    product = total(a * a * q5 - 2.0 * a * alpha * q3 + alpha * alpha * q4)
    ratio = norm_next / norm_now
    later = norm_next / (product - ratio * norm_next / alpha)
    lane = lane_index((1, LANES))

    def pick(value, component):
        return jnp.sum(jnp.where(lane == component, value, 0.0), axis=1, keepdims=True)

    on_force, on_image = alpha + later * (1.0 + ratio), -later * alpha
    return [(pick(on_force, k), pick(on_image, k)) for k in range(3)]


def step_kernel(plan, *refs):
    flags, sums, density, energy, position, velocity, pinned = refs[:7]
    messages, inner = refs[7:16], refs[16:20]
    velocity_new, accel, relaxed, density_new, energy_new = refs[20:25]
    (
        density_ext,
        energy_ext,
        moved,
        speed,
        free_ext,
        packed_ext,
        pinned_own,
        force,
        mass,
        other,
        semaphores,
        out_semaphores,
    ) = refs[25:]
    assemble(
        plan,
        flags,
        [density, energy, position, velocity, pinned],
        messages,
        inner,
        [density_ext, energy_ext, moved, speed, free_ext],
        packed_ext,
        pinned_own,
        semaphores,
    )
    inside = Inside(plan, flags)
    low, x, y = plan.low, plan.x, plan.y
    weights = solve_weights(sums[...])
    reach = SWEEPS + 1
    force_pass(
        density_ext,
        energy_ext,
        force,
        mass,
        inside,
        (low - reach, low + x + reach),
        (ROWS - reach, ROWS + y + reach),
    )

    def advance(at, here, sums, keep):
        weight = load(mass, 0, at)
        scale = [tile * inside.plane(at) for tile in keep]
        stores = []
        for component in range(3):
            on_force, on_image = weights[component]
            result = each(
                lambda m, a, k, s: on_force * a + on_image * (m * a + k * s),
                weight,
                here[component],
                scale,
                sums[component],
            )
            faster = each(lambda v, a: v + TIME_STEP * a, load(speed, component, at), result)
            further = each(
                lambda b, a: b + (TIME_STEP * TIME_STEP) * a, load(moved, component, at), result
            )
            stores += [
                (other, component, at, result),
                (speed, component, at, faster),
                (moved, component, at, further),
            ]
        return stores

    reach -= 1
    advanced = round_up(y + 2 * reach + 1, ROWS)
    stencil_pass(
        force,
        (low - reach, low + x + reach),
        (ROWS - reach, ROWS - reach + advanced - 1),
        lambda row: inside.tiles(row, CONSISTENT),
        advance,
    )

    out_copies = []

    def write(source, target, component, result=None):
        for t in range(plan.tiles):
            place = target if result is None else target.at[result]
            out_copies.append(
                pltpu.make_async_copy(
                    source.at[component, pl.ds(low, x), t, pl.ds(ROWS, y), :],
                    place.at[:, :, pl.ds(t * LANES, LANES)],
                    out_semaphores.at[len(out_copies)],
                )
            )
            out_copies[-1].start()

    for component in range(3):
        write(other, accel, component, component)
    accel_copies = len(out_copies)
    for component in range(3):
        write(speed, velocity_new, component, component)

    content = mass

    def content_chunk(row):
        def slab(at):
            under = [load(speed, component, at) for component in range(3)]
            over = [load(speed, component, at.at_row(1)) for component in range(3)]
            along_x = add(under[0], over[0])
            along_y = subtract(over[1], under[1])
            along_z = add(under[2], over[2])
            along_x = add(along_x, lane_above(along_x))
            along_y = add(along_y, lane_above(along_y))
            along_z = subtract(lane_above(along_z), along_z)
            return along_x, add(along_y, along_z)

        def plane(at, before):
            now = slab(at.at_plane(1))
            spread = add(subtract(now[0], before[0]), add(now[1], before[1]))
            held = load(energy_ext, 0, at)
            lagged = each(lambda e, s: e - (0.25 * 0.4 * TIME_STEP) * (e * s), held, spread)
            result = each(lambda d, e: d * e, load(density_ext, 0, at), lagged)
            return now, [(content, 0, at, result)]

        plane_loop(speed, low - 1, low + x, row, plane, slab(spot(speed, low - 1, row)))

    chunks(ROWS - 1, ROWS + y, content_chunk)

    for one in out_copies[:accel_copies]:
        one.wait()
    source, target = moved, other
    for _ in range(SWEEPS):
        reach -= 1

        def relax(at, here, sums, given, target=target):
            rate = load(free_ext, 0, at)
            stores = []
            for component in range(3):
                result = each(
                    lambda r, s, f: r + f * (s * (1.0 / 6.0) - r),
                    here[component],
                    sums[component],
                    rate,
                )
                stores.append((target, component, at, result))
            return stores

        stencil_pass(
            source,
            (low - reach, low + x + reach),
            (ROWS - reach, ROWS + y + reach),
            lambda row: None,
            relax,
        )
        source, target = target, (force if target is other else other)
    settled, free_buffer = source, target
    for component in range(3):
        write(settled, relaxed, component, component)

    quantities = (density_ext, content)

    def remap_chunk(row):
        def shift(component, at):
            return subtract(load(settled, component, at), load(moved, component, at))

        def slab(at):
            over = at.at_row(1)
            x_here = add(shift(0, at), shift(0, over))
            y_here, y_over = shift(1, at), shift(1, over)
            z_here = add(shift(2, at), shift(2, over))
            return (
                add(x_here, lane_above(x_here)),
                add(y_here, lane_above(y_here)),
                add(y_over, lane_above(y_over)),
                z_here,
                [load(one, 0, at) for one in quantities],
            )

        def flux(speeds, upper, lower):
            return each(lambda s, u, l: s * jnp.where(s > 0, u, l), speeds, upper, lower)

        def x_flux(speeds, upper, lower):
            return [flux(speeds, u, l) for u, l in zip(upper, lower)]

        def plane(at, carried):
            now, entering = carried
            ahead = slab(at.at_plane(1))
            leaving = x_flux(ahead[0], ahead[4], now[4])
            y_here, y_over, z_here = [add(now[k], ahead[k]) for k in (1, 2, 3)]
            stores = []
            for k, one in enumerate(quantities):
                held = now[4][k]
                under, over = [load(one, 0, at.at_row(step)) for step in (-1, 1)]
                through_z = flux(z_here, held, lane_below(held))
                change = subtract(leaving[k], entering[k])
                change = add(change, flux(y_over, over, held))
                change = subtract(change, flux(y_here, held, under))
                change = add(change, subtract(lane_above(through_z), through_z))
                result = each(lambda q, c: q + 0.25 * c, held, change)
                stores.append((free_buffer, k, at, result[: plan.tiles]))
            return (ahead, leaving), stores

        first = spot(settled, low, row)
        start = slab(first)
        before = [load(one, 0, first.at_plane(-1)) for one in quantities]
        plane_loop(settled, low, low + x - 1, row, plane, (start, x_flux(start[0], start[4], before)))

    chunks(ROWS, ROWS + y - 1, remap_chunk)
    write(free_buffer, density_new, 0)
    write(free_buffer, energy_new, 1)
    for one in out_copies[accel_copies:]:
        one.wait()


def gather_lines(line, axes):
    for axis in axes:
        count = lax.axis_size(axis)
        if count & (count - 1):
            line = lax.all_gather(line, axis, axis=0, tiled=True)
            continue
        step = 1
        while step < count:
            got = lax.ppermute(line, axis, [(i, i ^ step) for i in range(count)])
            later = (lax.axis_index(axis) // step) % 2 == 1
            line = jnp.concatenate([jnp.where(later, got, line), jnp.where(later, line, got)])
            step *= 2
    return line


def extended_scratch(plan, count):
    return pltpu.VMEM((count, plan.planes, plan.tiles + 1, plan.rows, LANES), jnp.float32)


def message_specs(planes, rows):
    return [any_space()] * planes + [in_vmem()] * rows


def on_device(position, velocity, density, energy, pinned):
    shape = density.shape
    arrays = [density[None], energy[None], position, velocity, pinned[None]]
    flags = jnp.stack(
        [
            jnp.float32(limit)
            for axis in ("bx", "by", "bz")
            for limit in (
                lax.axis_index(axis) > 0,
                lax.axis_index(axis) < lax.axis_size(axis) - 1,
            )
        ]
        + [(lax.axis_index("by") % 2).astype(jnp.float32)]
    )
    groups = [
        (1, WIDE, WIDE),
        (1, WIDE, WIDE),
        (3, SWEEPS, SWEEPS + 1),
        (3, 1, 2),
        (1, SWEEPS - 1, SWEEPS),
    ]
    narrow = Plan([(1, NARROW, NARROW)] * 2, shape)
    wide = Plan(groups, shape, narrow, cut=8)
    cells = arrays[:2]

    packed = exchange_lanes(narrow, pack_lanes(narrow, cells))
    planes = exchange_planes(*pack_planes(narrow, flags, cells, packed))
    wide_lanes = pack_lanes(wide, arrays)
    planes, wide_lanes = lax.optimization_barrier((planes, wide_lanes))
    wide_packed = exchange_lanes(wide, wide_lanes)
    rows = exchange_rows(pack_rows(narrow, flags, cells, packed, True, planes))

    first_planes, last_planes = pack_planes(wide, flags, arrays, wide_packed)
    wide_rows = pack_rows(wide, flags, arrays, wide_packed, True)
    rows, first_planes, last_planes, wide_rows = lax.optimization_barrier(
        (rows, first_planes, last_planes, wide_rows)
    )
    first_planes = exchange_planes(first_planes)
    last_planes = exchange_planes(last_planes)
    wide_rows = exchange_rows(wide_rows)

    line = pl.pallas_call(
        functools.partial(moments_kernel, narrow),
        in_specs=[in_smem()] + [any_space()] * 2 + message_specs(3, 2),
        out_specs=in_vmem(),
        out_shape=jax.ShapeDtypeStruct((1, LANES), jnp.float32),
        scratch_shapes=[
            extended_scratch(narrow, 1),
            extended_scratch(narrow, 1),
            pltpu.VMEM((narrow.planes, narrow.rows, LANES), jnp.float32),
            extended_scratch(narrow, 3),
            extended_scratch(narrow, 3),
            extended_scratch(narrow, 1),
            pltpu.SemaphoreType.DMA((assemble_copies(narrow),)),
        ],
        compiler_params=pltpu.CompilerParams(vmem_limit_bytes=VMEM_BYTES),
        cost_estimate=cost(1),
        name="moments",
    )(flags, *cells, packed, *planes, *rows)

    line, wide_rows, first_planes = lax.optimization_barrier((line, wide_rows, first_planes))
    lines = gather_lines(line, ("bz",))
    lines, last_planes = lax.optimization_barrier((lines, last_planes))
    wide_planes = [pair[side] for side in range(2) for pair in (first_planes, last_planes)]
    corners = exchange_rows(pack_rows(wide, flags, None, None, False, wide_planes, planes))
    messages = [wide_packed, *wide_planes, *wide_rows, *corners]
    nodes = jax.ShapeDtypeStruct((3, *shape), jnp.float32)
    cell = jax.ShapeDtypeStruct(shape, jnp.float32)
    return pl.pallas_call(
        functools.partial(step_kernel, wide),
        in_specs=[in_smem(), in_vmem()] + [any_space()] * 5 + message_specs(5, 4) + message_specs(2, 2),
        out_specs=[any_space()] * 5,
        out_shape=[nodes, nodes, nodes, cell, cell],
        scratch_shapes=[
            extended_scratch(wide, 1),
            extended_scratch(wide, 1),
            extended_scratch(wide, 3),
            extended_scratch(wide, 3),
            extended_scratch(wide, 1),
            pltpu.VMEM((wide.planes, wide.rows, LANES), jnp.float32),
            pltpu.VMEM((wide.x, wide.tiles, wide.y, LANES), jnp.int32),
            extended_scratch(wide, 3),
            extended_scratch(wide, 1),
            extended_scratch(wide, 3),
            pltpu.SemaphoreType.DMA((assemble_copies(wide),)),
            pltpu.SemaphoreType.DMA((11 * wide.tiles,)),
        ],
        compiler_params=pltpu.CompilerParams(vmem_limit_bytes=VMEM_BYTES),
        cost_estimate=cost(1),
        name="step",
    )(flags, gather_lines(lines, ("bx", "by")), *arrays, *messages, *planes, *rows)


def solution(mesh):
    in_specs = (
        P(None, "bx", "by", "bz"),
        P(None, "bx", "by", "bz"),
        P("bx", "by", "bz"),
        P("bx", "by", "bz"),
        P("bx", "by", "bz"),
    )
    out_specs = (
        P(None, "bx", "by", "bz"),
        P(None, "bx", "by", "bz"),
        P(None, "bx", "by", "bz"),
        P("bx", "by", "bz"),
        P("bx", "by", "bz"),
    )
    return jax.shard_map(
        on_device, mesh=mesh, in_specs=in_specs, out_specs=out_specs, check_vma=False
    )
```

```python
import functools
import math
from typing import NamedTuple

import jax
import jax.numpy as jnp
from jax import lax
from jax.experimental import pallas as pl
from jax.experimental.pallas import tpu as pltpu
from jax.sharding import PartitionSpec as P

SWEEPS = 3
TIME_STEP = 0.6
RELAX_RATE = 0.8
CONSISTENT = 0.2

LANES = 128
ROWS = 8
MOMENTS = 7
UNROLL = 6
POSITION, VELOCITY, PINNED = 2, 3, 4
NARROW = 2
WIDE = SWEEPS + 2
VMEM_BYTES = 62 * 2**20


class Field(NamedTuple):
    group: int
    component: int
    low: int
    high: int
    skip: int
    low_at: int
    high_at: int
    full_low_at: int
    full_high_at: int
    start: int


class Plan:
    def __init__(self, groups, shape, inner=None, starts=None, cut=None):
        self.groups = groups
        self.inner = inner
        self.x, self.y, self.z = shape
        self.tiles = self.z // LANES
        self.low = max(low for _, low, _ in groups)
        self.high = max(high for _, _, high in groups)
        self.planes = self.low + self.x + self.high
        self.rows = self.y + 2 * ROWS
        self.fields = []
        at = [0] * 4
        lane_at = 0
        for group, (count, low, high) in enumerate(groups):
            skip = 0 if inner is None or group >= len(inner.groups) else inner.low
            for component in range(count):
                start = lane_at + low if starts is None else starts[len(self.fields)]
                self.fields.append(Field(group, component, low, high, skip, *at, start))
                for k, size in enumerate((low - skip, high - skip, low, high)):
                    at[k] += size
                lane_at += low + high
        assert lane_at <= LANES
        self.starts = [field.start for field in self.fields]
        self.packed_at = at
        depths = (self.low, self.high) * 2
        self.sizes = [one + -(-depth // self.tiles) for one, depth in zip(at, depths)]
        cuts = [] if cut is None else [(self.fields[cut].low_at, self.fields[cut].high_at)]
        self.parts = []
        for side in range(2):
            ends = [0, *(one[side] for one in cuts), self.sizes[side]]
            self.parts.append([b - a for a, b in zip(ends, ends[1:])])

    def value(self, group, component, get):
        if group == POSITION:
            return get(POSITION, component) + TIME_STEP * get(VELOCITY, component)
        if group == PINNED:
            return RELAX_RATE * (1.0 - get(PINNED, component).astype(jnp.float32))
        return get(group, component)

    def folded(self, k, at):
        return at + k // self.tiles, (k % self.tiles) * LANES


def round_up(value, step):
    return -(-value // step) * step


def from_behind(x, axis):
    count = lax.axis_size(axis)
    return lax.ppermute(x, axis, [(i, i + 1) for i in range(count - 1)])


def from_ahead(x, axis):
    count = lax.axis_size(axis)
    return lax.ppermute(x, axis, [(i + 1, i) for i in range(count - 1)])


def any_space():
    return pl.BlockSpec(memory_space=pl.ANY)


def in_vmem():
    return pl.BlockSpec(memory_space=pltpu.VMEM)


def in_smem():
    return pl.BlockSpec(memory_space=pltpu.SMEM)


def cost(microseconds):
    return pl.CostEstimate(
        flops=0, bytes_accessed=int(microseconds * 3.0e6), transcendentals=0
    )


def lane_index(shape):
    return lax.broadcasted_iota(jnp.int32, shape, len(shape) - 1)


def pack_lanes(plan, arrays):
    half = LANES // 2

    def kernel(*refs):
        out = refs[-1]
        lane = lane_index((plan.y, LANES))
        in_low_half = lane < half

        def plane(x, _):
            def edge(group, component):
                first, last = refs[2 * group], refs[2 * group + 1]
                return jnp.where(in_low_half, first[component, x], last[component, x])

            packed = jnp.zeros((plan.y, LANES), jnp.float32)
            for group, component, low, high, *_, start in plan.fields:
                moved = pltpu.roll(plan.value(group, component, edge), start, 1)
                packed = jnp.where((lane >= start - low) & (lane < start + high), moved, packed)
            out[x] = packed
            return 0

        for x in range(planes):
            plane(x, 0)

    planes = next(n for n in (16 if len(arrays) == 2 else 8, 4, 1) if plan.x % n == 0)
    specs, operands = [], []
    for (count, _, _), array in zip(plan.groups, arrays):
        block = (count, planes, plan.y, LANES)
        specs.append(pl.BlockSpec(block, lambda i: (0, i, 0, 0)))
        specs.append(pl.BlockSpec(block, lambda i: (0, i, 0, plan.tiles - 1)))
        operands += [array, array]
    return pl.pallas_call(
        kernel,
        grid=(plan.x // planes,),
        in_specs=specs,
        out_specs=pl.BlockSpec((planes, plan.y, LANES), lambda i: (i, 0, 0)),
        out_shape=jax.ShapeDtypeStruct((plan.x, plan.y, LANES), jnp.float32),
        compiler_params=pltpu.CompilerParams(vmem_limit_bytes=VMEM_BYTES),
        cost_estimate=cost(0.5),
        name="pack_lanes",
    )(*operands)


def exchange_lanes(plan, packed):
    lane = lane_index((1, 1, LANES))
    is_low = functools.reduce(
        jnp.logical_or,
        [(lane >= start - low) & (lane < start) for _, _, low, *_, start in plan.fields],
    )
    count = lax.axis_size("bz")
    if count == 2:
        got = lax.ppermute(packed, "bz", [(0, 1), (1, 0)])
        return jnp.where(is_low == (lax.axis_index("bz") == 1), got, 0.0)
    return jnp.where(is_low, from_behind(packed, "bz"), from_ahead(packed, "bz"))


def part_of(parts, at):
    for part in parts:
        if at < part.shape[0]:
            return part, at
        at -= part.shape[0]


def pack_planes(plan, flags, arrays, packed):
    needed = [
        max(low if to_low else high for _, low, high in plan.groups) for to_low in (True, False)
    ]
    depths = [(low, high) for _, low, high in plan.groups]
    if len(depths) > VELOCITY:
        depths[VELOCITY] = depths[POSITION]

    def kernel(*refs):
        groups = len(plan.groups)
        edge, refs = refs[0], refs[1:]
        own, packed_ref = refs[:groups], refs[groups]
        count = len(plan.parts[0])
        outs = refs[groups + 1 : groups + 1 + count], refs[groups + 1 + count : groups + 1 + 2 * count]
        edges, semaphores = refs[groups + 1 + 2 * count : -1], refs[-1]
        copies = []

        def copy(source, target):
            copies.append(pltpu.make_async_copy(source, target, semaphores.at[len(copies)]))
            copies[-1].start()

        for side, out in enumerate(outs):
            for group, array in enumerate(own):
                depth = depths[group][side]
                planes = pl.ds(plan.x - depth, depth) if side == 0 else pl.ds(0, depth)
                copy(array.at[:, planes], edges[2 * group + side])
            first = plan.x - needed[0] if side == 0 else 0
            at = plan.packed_at[side]
            for k in range(needed[side]):
                row, lanes = plan.folded(k, at)
                part, row = part_of(out, row)
                copy(packed_ref.at[first + k], part.at[row, :, pl.ds(lanes, LANES)])
        for one in copies:
            one.wait()
        for side, out in enumerate(outs):
            for field in plan.fields:
                at = (field.low_at, field.high_at)[side]
                depth = (field.low, field.high)[side] - field.skip

                def get(argument, part):
                    held = edges[2 * argument + side]
                    first = depths[argument][0] - field.low if side == 0 else field.skip
                    return held[part, first : first + depth]

                part, at = part_of(out, at)
                part[at : at + depth] = plan.value(field.group, field.component, get)

        for side, parts in enumerate(outs):

            @pl.when(edge[1 - side] == 0.0)
            def _(parts=parts):
                for part in parts:
                    part[...] = jnp.zeros(part.shape, jnp.float32)

    shapes = [(size, plan.y, plan.z) for side in plan.parts for size in side]
    scratch = [
        pltpu.VMEM((array.shape[0], depth, plan.y, plan.z), array.dtype)
        for array, pair in zip(arrays, depths)
        for depth in pair
    ]
    count = 2 * len(arrays) + sum(needed)
    outs = pl.pallas_call(
        kernel,
        in_specs=[in_smem()] + [any_space()] * (len(arrays) + 1),
        out_specs=[in_vmem()] * len(shapes),
        out_shape=[jax.ShapeDtypeStruct(shape, jnp.float32) for shape in shapes],
        scratch_shapes=scratch + [pltpu.SemaphoreType.DMA((count,))],
        compiler_params=pltpu.CompilerParams(vmem_limit_bytes=VMEM_BYTES),
        cost_estimate=cost(0.5),
        name="pack_planes",
    )(flags, *arrays, packed)
    return list(zip(outs[: len(plan.parts[0])], outs[len(plan.parts[0]) :]))


def pack_rows(plan, flags, arrays, packed, own, planes=(), inner_planes=()):
    groups = len(plan.groups)
    sizes, packed_at = plan.sizes[2:], plan.packed_at[2:]
    if own:
        sizes, packed_at = plan.sizes[:2], plan.packed_at[:2]

    def kernel(flags, *refs):
        for parity in range(2):
            up, down = refs[-2:] if parity == 0 else refs[:-3:-1]
            pl.when(flags[6] == parity)(functools.partial(pack, flags, list(refs[:-2]), up, down))

    def pack(flags, refs, up, down):
        up[...] = jnp.zeros(up.shape, jnp.float32)
        down[...] = jnp.zeros(down.shape, jnp.float32)

        def put(plane, field, first, last):
            low_at, high_at, skip = field.full_low_at, field.full_high_at, 0
            if own:
                low_at, high_at, skip = field.low_at, field.high_at, field.skip
            low, high = field.low - skip, field.high - skip
            up[plane, low_at : low_at + low, :] = last[ROWS - field.low : ROWS - skip, :]
            down[plane, high_at : high_at + high, :] = first[skip : field.high, :]

        def put_packed(plane, first, last, at):
            for k in range(plan.low):
                row, lanes = plan.folded(k, packed_at[0])
                source = ROWS - plan.low + k
                up[plane, row : row + 1, lanes : lanes + LANES] = last[
                    source : source + 1, at : at + LANES
                ]
            for k in range(plan.high):
                row, lanes = plan.folded(k, packed_at[1])
                down[plane, row : row + 1, lanes : lanes + LANES] = first[
                    k : k + 1, at : at + LANES
                ]

        base = 0
        if own:
            blocks = refs[: 2 * groups + 2]
            del refs[: 2 * groups + 2]
            base = plan.x

            def own_plane(x, _):
                for field in plan.fields:
                    first, last = [
                        plan.value(
                            *field[:2],
                            lambda argument, part: blocks[2 * argument + side][part, x],
                        )
                        for side in range(2)
                    ]
                    put(x, field, first, last)
                put_packed(x, blocks[-2].at[x], blocks[-1].at[x], 0)
                return 0

            lax.fori_loop(0, plan.x, own_plane, 0)
        if planes:
            count = len(plan.parts[0])
            pairs = [tuple(refs[2 * k : 2 * k + 2]) for k in range(2 * count + 2)]
            if plan.inner is None:
                pairs = pairs[: 2 * count]
            sides = [pairs[:count], pairs[count : 2 * count]]
            inner_sides = [pairs[2 * count : 2 * count + 1], pairs[2 * count + 1 :]]

            def find(parts, at):
                part, at = part_of([first for first, _ in parts], at)
                pair = next(pair for pair in parts if pair[0] is part)
                return [ref.at[at] for ref in pair]

            for side in range(2):
                for k in range((plan.low, plan.high)[side]):
                    for field in plan.fields:
                        depth, at = (field.low, field.low_at) if side == 0 else (field.high, field.high_at)
                        j = plan.low - k if side == 0 else k + 1
                        if j > depth:
                            continue
                        if j > field.skip:
                            source = at + (depth - j if side == 0 else j - 1 - field.skip)
                            parts = sides[side]
                        else:
                            other = plan.inner.fields[field.group]
                            source = other.low_at + other.low - j if side == 0 else other.high_at + j - 1
                            parts = inner_sides[side]
                        put(base + k, field, *find(parts, source))
                    source, lanes = plan.folded(k, plan.packed_at[side])
                    put_packed(base + k, *find(sides[side], source), lanes)
                base += plan.low

        @pl.when(flags[3] == 0.0)
        def _():
            up[...] = jnp.zeros(up.shape, jnp.float32)

        @pl.when(flags[2] == 0.0)
        def _():
            down[...] = jnp.zeros(down.shape, jnp.float32)

    last = plan.y // ROWS - 1
    specs, operands = [in_smem()], [flags]
    if own:
        for array in arrays:
            block = (array.shape[0], plan.x, ROWS, plan.z)
            specs.append(pl.BlockSpec(block, lambda i: (0, 0, 0, 0)))
            specs.append(pl.BlockSpec(block, lambda i: (0, 0, last, 0)))
            operands += [array, array]
    for array in ([packed] if own else []) + [*planes, *inner_planes]:
        block = (array.shape[0], ROWS, array.shape[2])
        specs.append(pl.BlockSpec(block, lambda i: (0, 0, 0)))
        specs.append(pl.BlockSpec(block, lambda i: (0, last, 0)))
        operands += [array, array]
    count = plan.x * own + (plan.low + plan.high) * bool(planes)
    shapes = [(count, round_up(max(sizes), ROWS), plan.z)] * 2
    return pl.pallas_call(
        kernel,
        grid=(1,),
        in_specs=specs,
        out_specs=[pl.BlockSpec(shape, lambda i: (0, 0, 0)) for shape in shapes],
        out_shape=[jax.ShapeDtypeStruct(shape, jnp.float32) for shape in shapes],
        compiler_params=pltpu.CompilerParams(vmem_limit_bytes=VMEM_BYTES),
        cost_estimate=cost(0.5),
        name="pack_rows",
    )(*operands)


def exchange_planes(pair):
    count = lax.axis_size("bx")
    return [
        lax.ppermute(one, "bx", [(i, (i + step) % count) for i in range(count)])
        for one, step in zip(pair, (1, -1))
    ]


def exchange_rows(pair, to_self=True):
    count = lax.axis_size("by")
    got = []
    for parity, one in enumerate(pair):
        partner = list(range(count))
        for i in range(parity, count - 1, 2):
            partner[i], partner[i + 1] = i + 1, i
        pairs = [(i, j) for i, j in enumerate(partner) if to_self or i != j]
        got.append(lax.ppermute(one, "by", pairs))
    return got


def assemble(plan, flags, arrays, messages, inner, extended, packed_ext, pinned_own, semaphores):
    count = len(plan.parts[0])
    packed, below, above = messages[0], messages[1 : 1 + count], messages[1 + count : 1 + 2 * count]
    rest = messages[1 + 2 * count :]
    own_messages, halo_messages, halo_at = rest[:2], rest[-2:], plan.x if len(rest) == 2 else 0
    copies = []

    def copy(source, target):
        copies.append(
            pltpu.make_async_copy(source, target, semaphores.at[len(copies)])
        )
        copies[-1].start()

    own_rows = pl.ds(ROWS, plan.y)
    own_planes = pl.ds(plan.low, plan.x)
    for field in plan.fields:
        group, component, low, high, skip = field[:5]
        target = extended[group].at[component]
        after = plan.low + plan.x
        for t in range(plan.tiles):
            lanes = pl.ds(t * LANES, LANES)

            def planes(source, at, first, count):
                if count:
                    source, at = part_of(source, at)
                    copy(
                        source.at[pl.ds(at, count), :, lanes],
                        target.at[pl.ds(first, count), t, own_rows, :],
                    )

            place = target.at[own_planes, t, own_rows, :]
            if group == PINNED:
                place = pinned_own.at[:, t]
            copy(arrays[group].at[component, :, :, lanes], place)
            planes(below, field.low_at, plan.low - low, low - skip)
            planes(above, field.high_at, after + skip, high - skip)
            if skip:
                other = plan.inner.fields[group]
                planes(inner[:1], other.low_at, plan.low - skip, skip)
                planes(inner[1:2], other.high_at, after, skip)
    large = len(copies)
    copy(packed, packed_ext.at[own_planes, own_rows, :])
    for k in range(plan.low):
        source, lanes = plan.folded(k, plan.packed_at[0])
        part, source = part_of(below, source)
        copy(part.at[source, :, pl.ds(lanes, LANES)], packed_ext.at[k, own_rows, :])
    for k in range(plan.high):
        source, lanes = plan.folded(k, plan.packed_at[1])
        part, source = part_of(above, source)
        copy(
            part.at[source, :, pl.ds(lanes, LANES)],
            packed_ext.at[plan.low + plan.x + k, own_rows, :],
        )
    for one in copies[large:]:
        one.wait()

    top = ROWS + plan.y

    def fill(i, left, right, inner_left, inner_right, at, own):
        def rows(field, first, source, source_at, count):
            if count:
                for t in range(plan.tiles):
                    extended[field.group][field.component, i, t, first : first + count, :] = source[
                        at, source_at : source_at + count, t * LANES : (t + 1) * LANES
                    ]

        packed_at = plan.packed_at[:2] if own else plan.packed_at[2:]
        for field in plan.fields:
            low, high, skip = field.low, field.high, field.skip
            if own:
                rows(field, ROWS - low, left, field.low_at, low - skip)
                rows(field, top + skip, right, field.high_at, high - skip)
                if skip:
                    other = plan.inner.fields[field.group]
                    rows(field, ROWS - skip, inner_left, other.low_at, skip)
                    rows(field, top, inner_right, other.high_at, skip)
            else:
                rows(field, ROWS - low, left, field.full_low_at, low)
                rows(field, top, right, field.full_high_at, high)
        for k in range(plan.low):
            row, lanes = plan.folded(k, packed_at[0])
            to = ROWS - plan.low + k
            packed_ext[i, to : to + 1, :] = left[at, row : row + 1, lanes : lanes + LANES]
        for k in range(plan.high):
            row, lanes = plan.folded(k, packed_at[1])
            packed_ext[i, top + k : top + k + 1, :] = right[at, row : row + 1, lanes : lanes + LANES]
        tile = packed_ext[i]
        for field in plan.fields:
            extended[field.group][field.component, i, plan.tiles] = pltpu.roll(
                tile, (LANES - field.start) % LANES, 1
            )

    def fill_all(parity):
        def ordered(pair):
            return pair[::-1] if parity == 0 else pair

        own, halo = ordered(own_messages), ordered(halo_messages)
        inner_rows = (None, None) if inner is None else ordered(inner[2:4])

        def own_plane(x, _):
            fill(plan.low + x, *own, *inner_rows, x, True)
            return 0

        def low_plane(k, _):
            fill(k, *halo, None, None, halo_at + k, False)
            return 0

        def high_plane(k, _):
            fill(plan.low + plan.x + k, *halo, None, None, halo_at + plan.low + k, False)
            return 0

        lax.fori_loop(0, plan.x, own_plane, 0)
        lax.fori_loop(0, plan.low, low_plane, 0)
        lax.fori_loop(0, plan.high, high_plane, 0)

    def finish_plane(x, _):
        i = plan.low + x
        for t in range(plan.tiles):
            at = (i, t, slice(ROWS, top))

            def get(argument, component):
                if argument == PINNED:
                    return pinned_own[x, t]
                return extended[argument][(component, *at)]

            for group, component in [(POSITION, c) for c in range(3)] + [(PINNED, 0)]:
                extended[group][(component, *at)] = plan.value(group, component, get)
        return 0

    for parity in range(2):
        pl.when(flags[6] == parity)(functools.partial(fill_all, parity))
    for one in copies[:large]:
        one.wait()
    if pinned_own is not None:
        lax.fori_loop(0, plan.x, finish_plane, 0)


def assemble_copies(plan):
    skipping = sum(field.skip > 0 for field in plan.fields)
    return (3 * len(plan.fields) + 2 * skipping) * plan.tiles + 1 + plan.low + plan.high


def plane_loop(ref, first, last, row, body, carried):
    def turn(plane, carried, count):
        here = spot(ref, plane, row)
        pending = []
        for k in range(count):
            carried, stores = body(here.at_plane(k), carried)
            pending += stores
        for one in pending:
            store(*one)
        return carried

    count = last - first + 1
    carried = lax.fori_loop(
        0, count // UNROLL, lambda j, c: turn(first + j * UNROLL, c, UNROLL), carried
    )
    rest = count % UNROLL
    return turn(last + 1 - rest, carried, rest) if rest else carried


class Spot(NamedTuple):
    base: jax.Array
    plane: jax.Array
    planes: int = 0
    rows: int = 0

    def at_plane(self, step):
        return self._replace(planes=self.planes + step)

    def at_row(self, step):
        return self._replace(rows=self.rows + step)


def spot(ref, plane, row):
    return Spot(plane * (ref.shape[-3] * ref.shape[-2]) + row, plane)


def tile_rows(ref, component, at):
    planes, tiles, rows, lanes = ref.shape[-4:]
    first = (component * planes + at.planes) * tiles * rows + at.rows
    flat = ref.reshape(math.prod(ref.shape[:-1]), lanes)
    return flat, [at.base + (first + t * rows) for t in range(tiles)]


def load(ref, component, at):
    flat, starts = tile_rows(ref, component, at)
    return [flat[pl.ds(start, ROWS), :] for start in starts]


def store(ref, component, at, tiles):
    flat, starts = tile_rows(ref, component, at)
    for start, tile in zip(starts, tiles):
        flat[pl.ds(start, ROWS), :] = tile


def each(function, *tiles):
    return [function(*one) for one in zip(*tiles)]


def add(first, second):
    return each(lambda a, b: a + b, first, second)


def subtract(first, second):
    return each(lambda a, b: a - b, first, second)


def lane_below(tiles):
    lane = lane_index((ROWS, LANES))
    rolled = [pltpu.roll(tile, 1, 1) for tile in tiles]
    return [jnp.where(lane == 0, rolled[t - 1], rolled[t]) for t in range(len(tiles))]


def lane_above(tiles):
    lane = lane_index((ROWS, LANES))
    rolled = [pltpu.roll(tile, LANES - 1, 1) for tile in tiles]
    count = len(tiles)
    return [
        jnp.where(lane == LANES - 1, rolled[(t + 1) % count], rolled[t]) for t in range(count)
    ]


def chunks(first, last, body):
    count = -(-(last - first + 1) // ROWS)

    def one(j, _):
        body(jnp.minimum(first + j * ROWS, last - ROWS + 1))
        return 0

    lax.fori_loop(0, count, one, 0)


class Inside:
    def __init__(self, plan, flags):
        self.plan = plan
        self.flags = flags

    def tiles(self, row, scale):
        plan, flags = self.plan, self.flags
        rows = row + lax.broadcasted_iota(jnp.int32, (ROWS, LANES), 0)
        keep = jnp.where(rows < ROWS, flags[2], jnp.where(rows >= ROWS + plan.y, flags[3], 1.0))
        lane = lane_index((ROWS, LANES))
        edge = jnp.where(lane < LANES // 2, flags[5], flags[4])
        keep = scale * keep
        return [keep] * plan.tiles + [keep * edge]

    def plane(self, at):
        plan, flags = self.plan, self.flags
        i = at.plane + at.planes
        return jnp.where(
            i < plan.low, flags[0], jnp.where(i >= plan.low + plan.x, flags[1], 1.0)
        )


def force_pass(density, energy, force, mass, inside, planes, rows):
    def chunk(row):
        keep = inside.tiles(row, 0.4 * 0.25)

        def slab(at):
            here, under = load(density, 0, at), load(density, 0, at.at_row(-1))
            p = each(lambda a, b: a * b, here, load(energy, 0, at))
            p_under = each(lambda a, b: a * b, under, load(energy, 0, at.at_row(-1)))
            summed, stepped = add(p, p_under), subtract(p_under, p)
            weight = add(here, under)
            summed_z, stepped_z = lane_below(summed), lane_below(stepped)
            return (
                add(summed, summed_z),
                add(stepped, stepped_z),
                subtract(summed_z, summed),
                add(weight, lane_below(weight)),
            )

        def plane(at, before):
            now = slab(at)
            here = inside.plane(at)
            scale = [tile * here for tile in keep]
            stores = []
            for component in range(3):
                across = (subtract if component == 0 else add)(before[component], now[component])
                result = each(lambda a, b: a * b, scale, across)
                stores.append((force, component, at, result))
            result = each(lambda a, b: 0.125 * (a + b) + 6.0 * CONSISTENT, before[3], now[3])
            stores.append((mass, 0, at, result))
            return now, stores

        plane_loop(density, *planes, row, plane, slab(spot(density, planes[0] - 1, row)))

    chunks(*rows, chunk)


def face_sum(ref, component, at, before, here, after):
    total = add(add(before, after), add(lane_below(here), lane_above(here)))
    sides = add(load(ref, component, at.at_row(-1)), load(ref, component, at.at_row(1)))
    return add(total, sides)


def stencil_pass(ref, planes, rows, setup, use):
    def chunk(row):
        given = setup(row)

        def plane(at, carried):
            before, here = carried
            after = [load(ref, component, at.at_plane(1)) for component in range(3)]
            sums = [
                face_sum(ref, component, at, before[component], here[component], after[component])
                for component in range(3)
            ]
            return (here, after), use(at, here, sums, given)

        start = spot(ref, planes[0], row)
        first = [load(ref, component, start.at_plane(-1)) for component in range(3)]
        second = [load(ref, component, start) for component in range(3)]
        plane_loop(ref, *planes, row, plane, (first, second))

    chunks(*rows, chunk)


def whole_sum(tile):
    return jnp.sum(jnp.sum(tile, axis=0, keepdims=True), axis=1, keepdims=True)


def moments_kernel(plan, *refs):
    flags, density, energy = refs[:3]
    messages, out = refs[3:8], refs[8]
    density_ext, energy_ext, packed_ext, force, image, mass, semaphores = refs[9:]
    assemble(
        plan,
        flags,
        [density, energy],
        messages,
        None,
        [density_ext, energy_ext],
        packed_ext,
        None,
        semaphores,
    )
    inside = Inside(plan, flags)
    low, x, y = plan.low, plan.x, plan.y
    force_pass(
        density_ext,
        energy_ext,
        force,
        mass,
        inside,
        (low - 1, low + x + 1),
        (ROWS - 1, ROWS + y + 1),
    )

    def multiply(at, here, sums, keep):
        weight = load(mass, 0, at)
        scale = [tile * inside.plane(at) for tile in keep]
        stores = []
        for component in range(3):
            result = each(
                lambda m, a, k, s: m * a + k * s, weight, here[component], scale, sums[component]
            )
            stores.append((image, component, at, result))
        return stores

    stencil_pass(
        force,
        (low, low + x),
        (ROWS, ROWS + y),
        lambda row: inside.tiles(row, CONSISTENT),
        multiply,
    )

    own = range(plan.tiles)
    nothing = jnp.zeros((ROWS, LANES), jnp.float32)

    def first_chunk(j, sums):
        row = ROWS + j * ROWS

        def plane(at, sums):
            sums = list(sums)
            for component in range(3):
                f = load(force, component, at)
                v = load(image, component, at)
                for t in own:
                    sums[component] = sums[component] + f[t] * f[t]
                    sums[3 + component] = sums[3 + component] + f[t] * v[t]
            return tuple(sums), []

        return plane_loop(force, low, low + x - 1, row, plane, sums)

    sums = lax.fori_loop(0, y // ROWS, first_chunk, (nothing,) * 6)
    sums = [whole_sum(one) for one in sums]
    square = sums[:3]
    shift = [
        jnp.where(square[c] > 0, sums[3 + c] / jnp.where(square[c] > 0, square[c], 1.0), 0.0)
        for c in range(3)
    ]

    def pair(component, at):
        f = load(force, component, at)
        v = load(image, component, at)
        return f, each(lambda a, b: a - shift[component] * b, v, f)

    def second_chunk(j, sums):
        row = ROWS + j * ROWS

        def plane(at, carried):
            here, sums = carried
            sums = list(sums)
            ahead = [pair(component, at.at_plane(1)) for component in range(3)]
            weight = load(mass, 0, at)
            for component in range(3):
                f, w = here[component]
                f_next, w_next = ahead[component]
                f_up, w_up = pair(component, at.at_row(1))
                f_high = add(add(f_next, f_up), lane_above(f))
                w_high = add(add(w_next, w_up), lane_above(w))
                for t in own:
                    k = 5 * component
                    heavy = weight[t] * w[t]
                    sums[k] = sums[k] + f[t] * w[t]
                    sums[k + 1] = sums[k + 1] + w[t] * w[t]
                    sums[k + 2] = sums[k + 2] + (
                        f[t] * heavy + CONSISTENT * (f[t] * w_high[t] + w[t] * f_high[t])
                    )
                    sums[k + 3] = sums[k + 3] + w[t] * (
                        heavy + (2.0 * CONSISTENT) * w_high[t]
                    )
                    sums[k + 4] = sums[k + 4] + f[t] * (
                        weight[t] * f[t] + (2.0 * CONSISTENT) * f_high[t]
                    )
            return (ahead, tuple(sums)), []

        start = [pair(component, spot(force, low, row)) for component in range(3)]
        return plane_loop(force, low, low + x - 1, row, plane, (start, sums))[1]

    rest = lax.fori_loop(0, y // ROWS, second_chunk, (nothing,) * 15)
    lane = lane_index((1, LANES))
    line = jnp.zeros((1, LANES), jnp.float32)
    for c in range(3):
        values = [shift[c], square[c]] + [whole_sum(one) for one in rest[5 * c : 5 * c + 5]]
        for k, value in enumerate(values):
            line = jnp.where(lane == 3 * k + c, value, line)
    out[...] = line


def solve_weights(sums):
    got = [sums if k == 0 else pltpu.roll(sums, LANES - 3 * k, 1) for k in range(MOMENTS)]
    c, p0, q1, q2, q3, q4, q5 = got

    def total(value):
        return jnp.sum(value, axis=0, keepdims=True)

    norm_now = total(p0)
    alpha = norm_now / total(q1 + c * p0)
    a = 1.0 - alpha * c
    norm_next = total(a * a * p0 - 2.0 * a * alpha * q1 + alpha * alpha * q2)
    product = total(a * a * q5 - 2.0 * a * alpha * q3 + alpha * alpha * q4)
    ratio = norm_next / norm_now
    later = norm_next / (product - ratio * norm_next / alpha)
    lane = lane_index((1, LANES))

    def pick(value, component):
        return jnp.sum(jnp.where(lane == component, value, 0.0), axis=1, keepdims=True)

    on_force, on_image = alpha + later * (1.0 + ratio), -later * alpha
    return [(pick(on_force, k), pick(on_image, k)) for k in range(3)]


def step_kernel(plan, *refs):
    flags, sums, density, energy, position, velocity, pinned = refs[:7]
    messages, inner = refs[7:14], refs[14:18]
    velocity_new, accel, relaxed, density_new, energy_new = refs[18:23]
    (
        density_ext,
        energy_ext,
        moved,
        speed,
        free_ext,
        packed_ext,
        pinned_own,
        force,
        mass,
        other,
        semaphores,
        out_semaphores,
    ) = refs[23:]
    assemble(
        plan,
        flags,
        [density, energy, position, velocity, pinned],
        messages,
        inner,
        [density_ext, energy_ext, moved, speed, free_ext],
        packed_ext,
        pinned_own,
        semaphores,
    )
    inside = Inside(plan, flags)
    low, x, y = plan.low, plan.x, plan.y
    weights = solve_weights(sums[...])
    reach = SWEEPS + 1
    force_pass(
        density_ext,
        energy_ext,
        force,
        mass,
        inside,
        (low - reach, low + x + reach),
        (ROWS - reach, ROWS + y + reach),
    )

    def advance(at, here, sums, keep):
        weight = load(mass, 0, at)
        scale = [tile * inside.plane(at) for tile in keep]
        stores = []
        for component in range(3):
            on_force, on_image = weights[component]
            result = each(
                lambda m, a, k, s: on_force * a + on_image * (m * a + k * s),
                weight,
                here[component],
                scale,
                sums[component],
            )
            faster = each(lambda v, a: v + TIME_STEP * a, load(speed, component, at), result)
            further = each(
                lambda b, a: b + (TIME_STEP * TIME_STEP) * a, load(moved, component, at), result
            )
            stores += [
                (other, component, at, result),
                (speed, component, at, faster),
                (moved, component, at, further),
            ]
        return stores

    reach -= 1
    advanced = round_up(y + 2 * reach + 1, ROWS)
    stencil_pass(
        force,
        (low - reach, low + x + reach),
        (ROWS - reach, ROWS - reach + advanced - 1),
        lambda row: inside.tiles(row, CONSISTENT),
        advance,
    )

    out_copies = []

    def write(source, target, component, result=None):
        for t in range(plan.tiles):
            place = target if result is None else target.at[result]
            out_copies.append(
                pltpu.make_async_copy(
                    source.at[component, pl.ds(low, x), t, pl.ds(ROWS, y), :],
                    place.at[:, :, pl.ds(t * LANES, LANES)],
                    out_semaphores.at[len(out_copies)],
                )
            )
            out_copies[-1].start()

    for component in range(3):
        write(other, accel, component, component)
    accel_copies = len(out_copies)
    for component in range(3):
        write(speed, velocity_new, component, component)

    content = mass

    def content_chunk(row):
        def slab(at):
            under = [load(speed, component, at) for component in range(3)]
            over = [load(speed, component, at.at_row(1)) for component in range(3)]
            along_x = add(under[0], over[0])
            along_y = subtract(over[1], under[1])
            along_z = add(under[2], over[2])
            along_x = add(along_x, lane_above(along_x))
            along_y = add(along_y, lane_above(along_y))
            along_z = subtract(lane_above(along_z), along_z)
            return along_x, add(along_y, along_z)

        def plane(at, before):
            now = slab(at.at_plane(1))
            spread = add(subtract(now[0], before[0]), add(now[1], before[1]))
            held = load(energy_ext, 0, at)
            lagged = each(lambda e, s: e - (0.25 * 0.4 * TIME_STEP) * (e * s), held, spread)
            result = each(lambda d, e: d * e, load(density_ext, 0, at), lagged)
            return now, [(content, 0, at, result)]

        plane_loop(speed, low - 1, low + x, row, plane, slab(spot(speed, low - 1, row)))

    chunks(ROWS - 1, ROWS + y, content_chunk)

    for one in out_copies[:accel_copies]:
        one.wait()
    source, target = moved, other
    for _ in range(SWEEPS):
        reach -= 1

        def relax(at, here, sums, given, target=target):
            rate = load(free_ext, 0, at)
            stores = []
            for component in range(3):
                result = each(
                    lambda r, s, f: r + f * (s * (1.0 / 6.0) - r),
                    here[component],
                    sums[component],
                    rate,
                )
                stores.append((target, component, at, result))
            return stores

        stencil_pass(
            source,
            (low - reach, low + x + reach),
            (ROWS - reach, ROWS + y + reach),
            lambda row: None,
            relax,
        )
        source, target = target, (force if target is other else other)
    settled, free_buffer = source, target
    for component in range(3):
        write(settled, relaxed, component, component)

    quantities = (density_ext, content)

    def remap_chunk(row):
        def shift(component, at):
            return subtract(load(settled, component, at), load(moved, component, at))

        def slab(at):
            over = at.at_row(1)
            x_here = add(shift(0, at), shift(0, over))
            y_here, y_over = shift(1, at), shift(1, over)
            z_here = add(shift(2, at), shift(2, over))
            return (
                add(x_here, lane_above(x_here)),
                add(y_here, lane_above(y_here)),
                add(y_over, lane_above(y_over)),
                z_here,
                [load(one, 0, at) for one in quantities],
            )

        def flux(speeds, upper, lower):
            return each(lambda s, u, l: s * jnp.where(s > 0, u, l), speeds, upper, lower)

        def x_flux(speeds, upper, lower):
            return [flux(speeds, u, l) for u, l in zip(upper, lower)]

        def plane(at, carried):
            now, entering = carried
            ahead = slab(at.at_plane(1))
            leaving = x_flux(ahead[0], ahead[4], now[4])
            y_here, y_over, z_here = [add(now[k], ahead[k]) for k in (1, 2, 3)]
            stores = []
            for k, one in enumerate(quantities):
                held = now[4][k]
                under, over = [load(one, 0, at.at_row(step)) for step in (-1, 1)]
                through_z = flux(z_here, held, lane_below(held))
                change = subtract(leaving[k], entering[k])
                change = add(change, flux(y_over, over, held))
                change = subtract(change, flux(y_here, held, under))
                change = add(change, subtract(lane_above(through_z), through_z))
                result = each(lambda q, c: q + 0.25 * c, held, change)
                stores.append((free_buffer, k, at, result[: plan.tiles]))
            return (ahead, leaving), stores

        first = spot(settled, low, row)
        start = slab(first)
        before = [load(one, 0, first.at_plane(-1)) for one in quantities]
        plane_loop(settled, low, low + x - 1, row, plane, (start, x_flux(start[0], start[4], before)))

    chunks(ROWS, ROWS + y - 1, remap_chunk)
    write(free_buffer, density_new, 0)
    write(free_buffer, energy_new, 1)
    for one in out_copies[accel_copies:]:
        one.wait()


def line_hops():
    hops = []
    for axis in ("bz", "by", "bx"):
        step = 1
        while step < lax.axis_size(axis):
            hops.append((axis, step))
            step *= 2
    return hops


def gather_lines(line, hops):
    for axis, step in hops:
        count = lax.axis_size(axis)
        assert count & (count - 1) == 0
        got = lax.ppermute(line, axis, [(i, i ^ step) for i in range(count)])
        later = (lax.axis_index(axis) // step) % 2 == 1
        line = jnp.concatenate([jnp.where(later, got, line), jnp.where(later, line, got)])
    return line


def extended_scratch(plan, count):
    return pltpu.VMEM((count, plan.planes, plan.tiles + 1, plan.rows, LANES), jnp.float32)


def message_specs(planes, rows):
    return [any_space()] * planes + [in_vmem()] * rows


def on_device(position, velocity, density, energy, pinned):
    shape = density.shape
    arrays = [density[None], energy[None], position, velocity, pinned[None]]
    flags = jnp.stack(
        [
            jnp.float32(limit)
            for axis in ("bx", "by", "bz")
            for limit in (
                lax.axis_index(axis) > 0,
                lax.axis_index(axis) < lax.axis_size(axis) - 1,
            )
        ]
        + [(lax.axis_index("by") % 2).astype(jnp.float32)]
    )
    groups = [
        (1, WIDE, WIDE),
        (1, WIDE, WIDE),
        (3, SWEEPS, SWEEPS + 1),
        (3, 1, 2),
        (1, SWEEPS - 1, SWEEPS),
    ]
    narrow = Plan([(1, NARROW, NARROW)] * 2, shape)
    wide = Plan(groups, shape, narrow, cut=None)
    cells = arrays[:2]

    packed = exchange_lanes(narrow, pack_lanes(narrow, cells))
    planes = exchange_planes(*pack_planes(narrow, flags, cells, packed))
    wide_lanes = pack_lanes(wide, arrays)
    planes, wide_lanes = lax.optimization_barrier((planes, wide_lanes))
    wide_packed = exchange_lanes(wide, wide_lanes)
    rows = exchange_rows(pack_rows(narrow, flags, cells, packed, True, planes))

    (wide_planes,) = pack_planes(wide, flags, arrays, wide_packed)
    wide_rows = pack_rows(wide, flags, arrays, wide_packed, True)
    rows, wide_planes, wide_rows = lax.optimization_barrier((rows, wide_planes, wide_rows))
    wide_planes = exchange_planes(wide_planes)
    wide_rows = exchange_rows(wide_rows, to_self=False)

    line = pl.pallas_call(
        functools.partial(moments_kernel, narrow),
        in_specs=[in_smem()] + [any_space()] * 2 + message_specs(3, 2),
        out_specs=in_vmem(),
        out_shape=jax.ShapeDtypeStruct((1, LANES), jnp.float32),
        scratch_shapes=[
            extended_scratch(narrow, 1),
            extended_scratch(narrow, 1),
            pltpu.VMEM((narrow.planes, narrow.rows, LANES), jnp.float32),
            extended_scratch(narrow, 3),
            extended_scratch(narrow, 3),
            extended_scratch(narrow, 1),
            pltpu.SemaphoreType.DMA((assemble_copies(narrow),)),
        ],
        compiler_params=pltpu.CompilerParams(vmem_limit_bytes=VMEM_BYTES),
        cost_estimate=cost(1),
        name="moments",
    )(flags, *cells, packed, *planes, *rows)

    line, wide_rows = lax.optimization_barrier((line, wide_rows))
    hops = line_hops()
    early = len(hops) - 3
    lines = gather_lines(line, hops[:early])
    lines, wide_planes = lax.optimization_barrier((lines, wide_planes))
    corners = pack_rows(wide, flags, None, None, False, wide_planes, planes)
    lines, corners = lax.optimization_barrier((lines, corners))
    corners = exchange_rows(corners)
    messages = [wide_packed, *wide_planes, *wide_rows, *corners]
    nodes = jax.ShapeDtypeStruct((3, *shape), jnp.float32)
    cell = jax.ShapeDtypeStruct(shape, jnp.float32)
    return pl.pallas_call(
        functools.partial(step_kernel, wide),
        in_specs=[in_smem(), in_vmem()] + [any_space()] * 5 + message_specs(3, 4) + message_specs(2, 2),
        out_specs=[any_space()] * 5,
        out_shape=[nodes, nodes, nodes, cell, cell],
        scratch_shapes=[
            extended_scratch(wide, 1),
            extended_scratch(wide, 1),
            extended_scratch(wide, 3),
            extended_scratch(wide, 3),
            extended_scratch(wide, 1),
            pltpu.VMEM((wide.planes, wide.rows, LANES), jnp.float32),
            pltpu.VMEM((wide.x, wide.tiles, wide.y, LANES), jnp.int32),
            extended_scratch(wide, 3),
            extended_scratch(wide, 1),
            extended_scratch(wide, 3),
            pltpu.SemaphoreType.DMA((assemble_copies(wide),)),
            pltpu.SemaphoreType.DMA((11 * wide.tiles,)),
        ],
        compiler_params=pltpu.CompilerParams(vmem_limit_bytes=VMEM_BYTES),
        cost_estimate=cost(1),
        name="step",
    )(flags, gather_lines(lines, hops[early:]), *arrays, *messages, *planes, *rows)


def solution(mesh):
    in_specs = (
        P(None, "bx", "by", "bz"),
        P(None, "bx", "by", "bz"),
        P("bx", "by", "bz"),
        P("bx", "by", "bz"),
        P("bx", "by", "bz"),
    )
    out_specs = (
        P(None, "bx", "by", "bz"),
        P(None, "bx", "by", "bz"),
        P(None, "bx", "by", "bz"),
        P("bx", "by", "bz"),
        P("bx", "by", "bz"),
    )
    return jax.shard_map(
        on_device, mesh=mesh, in_specs=in_specs, out_specs=out_specs, check_vma=False
    )
```

```python
import functools
import math
from typing import NamedTuple

import jax
import jax.numpy as jnp
from jax import lax
from jax.experimental import pallas as pl
from jax.experimental.pallas import tpu as pltpu
from jax.sharding import PartitionSpec as P

SWEEPS = 3
TIME_STEP = 0.6
RELAX_RATE = 0.8
CONSISTENT = 0.2

LANES = 128
ROWS = 8
MOMENTS = 7
MOMENTS_UNROLL = 12
STEP_UNROLL = 3
POSITION, VELOCITY, PINNED = 2, 3, 4
NARROW = 2
WIDE = SWEEPS + 2
VMEM_BYTES = 62 * 2**20


class Field(NamedTuple):
    group: int
    component: int
    low: int
    high: int
    skip: int
    low_at: int
    high_at: int
    full_low_at: int
    full_high_at: int
    start: int


class Plan:
    def __init__(self, groups, shape, inner=None, starts=None, cut=None):
        self.groups = groups
        self.inner = inner
        self.x, self.y, self.z = shape
        self.tiles = self.z // LANES
        self.low = max(low for _, low, _ in groups)
        self.high = max(high for _, _, high in groups)
        self.planes = self.low + self.x + self.high
        self.rows = self.y + 2 * ROWS
        self.fields = []
        at = [0] * 4
        lane_at = 0
        for group, (count, low, high) in enumerate(groups):
            skip = 0 if inner is None or group >= len(inner.groups) else inner.low
            for component in range(count):
                start = lane_at + low if starts is None else starts[len(self.fields)]
                self.fields.append(Field(group, component, low, high, skip, *at, start))
                for k, size in enumerate((low - skip, high - skip, low, high)):
                    at[k] += size
                lane_at += low + high
        assert lane_at <= LANES
        self.starts = [field.start for field in self.fields]
        self.packed_at = at
        depths = (self.low, self.high) * 2
        self.sizes = [one + -(-depth // self.tiles) for one, depth in zip(at, depths)]
        cuts = [] if cut is None else [(self.fields[cut].low_at, self.fields[cut].high_at)]
        self.parts = []
        for side in range(2):
            ends = [0, *(one[side] for one in cuts), self.sizes[side]]
            self.parts.append([b - a for a, b in zip(ends, ends[1:])])

    def value(self, group, component, get):
        if group == POSITION:
            return get(POSITION, component) + TIME_STEP * get(VELOCITY, component)
        if group == PINNED:
            return RELAX_RATE * (1.0 - get(PINNED, component).astype(jnp.float32))
        return get(group, component)

    def folded(self, k, at):
        return at + k // self.tiles, (k % self.tiles) * LANES


def round_up(value, step):
    return -(-value // step) * step


def from_behind(x, axis):
    count = lax.axis_size(axis)
    return lax.ppermute(x, axis, [(i, i + 1) for i in range(count - 1)])


def from_ahead(x, axis):
    count = lax.axis_size(axis)
    return lax.ppermute(x, axis, [(i + 1, i) for i in range(count - 1)])


def any_space():
    return pl.BlockSpec(memory_space=pl.ANY)


def in_vmem():
    return pl.BlockSpec(memory_space=pltpu.VMEM)


def in_smem():
    return pl.BlockSpec(memory_space=pltpu.SMEM)


def cost(microseconds):
    return pl.CostEstimate(
        flops=0, bytes_accessed=int(microseconds * 3.0e6), transcendentals=0
    )


def every_plane(count, body, together):
    together = together if count % together == 0 else 1

    def turn(j, _):
        for k in range(together):
            body(j * together + k)
        return 0

    lax.fori_loop(0, count // together, turn, 0)


def lane_index(shape):
    return lax.broadcasted_iota(jnp.int32, shape, len(shape) - 1)


def pack_lanes(plan, arrays):
    half = LANES // 2

    def kernel(*refs):
        out = refs[-1]
        lane = lane_index((plan.y, LANES))
        in_low_half = lane < half

        def plane(x, _):
            def edge(group, component):
                first, last = refs[2 * group], refs[2 * group + 1]
                return jnp.where(in_low_half, first[component, x], last[component, x])

            packed = jnp.zeros((plan.y, LANES), jnp.float32)
            for group, component, low, high, *_, start in plan.fields:
                moved = pltpu.roll(plan.value(group, component, edge), start, 1)
                packed = jnp.where((lane >= start - low) & (lane < start + high), moved, packed)
            out[x] = packed
            return 0

        for x in range(planes):
            plane(x, 0)

    planes = next(n for n in (16 if len(arrays) == 2 else 8, 4, 1) if plan.x % n == 0)
    specs, operands = [], []
    for (count, _, _), array in zip(plan.groups, arrays):
        block = (count, planes, plan.y, LANES)
        specs.append(pl.BlockSpec(block, lambda i: (0, i, 0, 0)))
        specs.append(pl.BlockSpec(block, lambda i: (0, i, 0, plan.tiles - 1)))
        operands += [array, array]
    return pl.pallas_call(
        kernel,
        grid=(plan.x // planes,),
        in_specs=specs,
        out_specs=pl.BlockSpec((planes, plan.y, LANES), lambda i: (i, 0, 0)),
        out_shape=jax.ShapeDtypeStruct((plan.x, plan.y, LANES), jnp.float32),
        compiler_params=pltpu.CompilerParams(vmem_limit_bytes=VMEM_BYTES),
        cost_estimate=cost(0.5),
        name="pack_lanes",
    )(*operands)


def exchange_lanes(plan, packed):
    lane = lane_index((1, 1, LANES))
    is_low = functools.reduce(
        jnp.logical_or,
        [(lane >= start - low) & (lane < start) for _, _, low, *_, start in plan.fields],
    )
    count = lax.axis_size("bz")
    if count == 2:
        got = lax.ppermute(packed, "bz", [(0, 1), (1, 0)])
        return jnp.where(is_low == (lax.axis_index("bz") == 1), got, 0.0)
    return jnp.where(is_low, from_behind(packed, "bz"), from_ahead(packed, "bz"))


def part_of(parts, at):
    for part in parts:
        if at < part.shape[0]:
            return part, at
        at -= part.shape[0]


def pack_planes(plan, flags, arrays, packed):
    needed = [
        max(low if to_low else high for _, low, high in plan.groups) for to_low in (True, False)
    ]
    depths = [(low, high) for _, low, high in plan.groups]
    if len(depths) > VELOCITY:
        depths[VELOCITY] = depths[POSITION]

    def kernel(*refs):
        groups = len(plan.groups)
        edge, refs = refs[0], refs[1:]
        own, packed_ref = refs[:groups], refs[groups]
        count = len(plan.parts[0])
        outs = refs[groups + 1 : groups + 1 + count], refs[groups + 1 + count : groups + 1 + 2 * count]
        edges, semaphores = refs[groups + 1 + 2 * count : -1], refs[-1]
        copies = []

        def copy(source, target):
            copies.append(pltpu.make_async_copy(source, target, semaphores.at[len(copies)]))
            copies[-1].start()

        for side, out in enumerate(outs):
            for group, array in enumerate(own):
                depth = depths[group][side]
                planes = pl.ds(plan.x - depth, depth) if side == 0 else pl.ds(0, depth)
                copy(array.at[:, planes], edges[2 * group + side])
            first = plan.x - needed[0] if side == 0 else 0
            at = plan.packed_at[side]
            for k in range(needed[side]):
                row, lanes = plan.folded(k, at)
                part, row = part_of(out, row)
                copy(packed_ref.at[first + k], part.at[row, :, pl.ds(lanes, LANES)])
        for one in copies:
            one.wait()
        for side, out in enumerate(outs):
            for field in plan.fields:
                at = (field.low_at, field.high_at)[side]
                depth = (field.low, field.high)[side] - field.skip

                def get(argument, part):
                    held = edges[2 * argument + side]
                    first = depths[argument][0] - field.low if side == 0 else field.skip
                    return held[part, first : first + depth]

                part, at = part_of(out, at)
                part[at : at + depth] = plan.value(field.group, field.component, get)

        for side, parts in enumerate(outs):

            @pl.when(edge[1 - side] == 0.0)
            def _(parts=parts):
                for part in parts:
                    part[...] = jnp.zeros(part.shape, jnp.float32)

    shapes = [(size, plan.y, plan.z) for side in plan.parts for size in side]
    scratch = [
        pltpu.VMEM((array.shape[0], depth, plan.y, plan.z), array.dtype)
        for array, pair in zip(arrays, depths)
        for depth in pair
    ]
    count = 2 * len(arrays) + sum(needed)
    outs = pl.pallas_call(
        kernel,
        in_specs=[in_smem()] + [any_space()] * (len(arrays) + 1),
        out_specs=[in_vmem()] * len(shapes),
        out_shape=[jax.ShapeDtypeStruct(shape, jnp.float32) for shape in shapes],
        scratch_shapes=scratch + [pltpu.SemaphoreType.DMA((count,))],
        compiler_params=pltpu.CompilerParams(vmem_limit_bytes=VMEM_BYTES),
        cost_estimate=cost(0.5),
        name="pack_planes",
    )(flags, *arrays, packed)
    return list(zip(outs[: len(plan.parts[0])], outs[len(plan.parts[0]) :]))


def pack_rows(plan, flags, arrays, packed, own, planes=(), inner_planes=()):
    groups = len(plan.groups)
    sizes, packed_at = plan.sizes[2:], plan.packed_at[2:]
    if own:
        sizes, packed_at = plan.sizes[:2], plan.packed_at[:2]

    def kernel(flags, *refs):
        for parity in range(2):
            up, down = refs[-2:] if parity == 0 else refs[:-3:-1]
            pl.when(flags[6] == parity)(functools.partial(pack, flags, list(refs[:-2]), up, down))

    def pack(flags, refs, up, down):
        up[...] = jnp.zeros(up.shape, jnp.float32)
        down[...] = jnp.zeros(down.shape, jnp.float32)

        def put(plane, field, first, last):
            low_at, high_at, skip = field.full_low_at, field.full_high_at, 0
            if own:
                low_at, high_at, skip = field.low_at, field.high_at, field.skip
            low, high = field.low - skip, field.high - skip
            up[plane, low_at : low_at + low, :] = last[ROWS - field.low : ROWS - skip, :]
            down[plane, high_at : high_at + high, :] = first[skip : field.high, :]

        def put_packed(plane, first, last, at):
            for k in range(plan.low):
                row, lanes = plan.folded(k, packed_at[0])
                source = ROWS - plan.low + k
                up[plane, row : row + 1, lanes : lanes + LANES] = last[
                    source : source + 1, at : at + LANES
                ]
            for k in range(plan.high):
                row, lanes = plan.folded(k, packed_at[1])
                down[plane, row : row + 1, lanes : lanes + LANES] = first[
                    k : k + 1, at : at + LANES
                ]

        base = 0
        if own:
            blocks = refs[: 2 * groups + 2]
            del refs[: 2 * groups + 2]
            base = plan.x

            def own_plane(x):
                for field in plan.fields:
                    first, last = [
                        plan.value(
                            *field[:2],
                            lambda argument, part: blocks[2 * argument + side][part, x],
                        )
                        for side in range(2)
                    ]
                    put(x, field, first, last)
                put_packed(x, blocks[-2].at[x], blocks[-1].at[x], 0)

            every_plane(plan.x, own_plane, 4)
        if planes:
            count = len(plan.parts[0])
            pairs = [tuple(refs[2 * k : 2 * k + 2]) for k in range(2 * count + 2)]
            if plan.inner is None:
                pairs = pairs[: 2 * count]
            sides = [pairs[:count], pairs[count : 2 * count]]
            inner_sides = [pairs[2 * count : 2 * count + 1], pairs[2 * count + 1 :]]

            def find(parts, at):
                part, at = part_of([first for first, _ in parts], at)
                pair = next(pair for pair in parts if pair[0] is part)
                return [ref.at[at] for ref in pair]

            for side in range(2):
                for k in range((plan.low, plan.high)[side]):
                    for field in plan.fields:
                        depth, at = (field.low, field.low_at) if side == 0 else (field.high, field.high_at)
                        j = plan.low - k if side == 0 else k + 1
                        if j > depth:
                            continue
                        if j > field.skip:
                            source = at + (depth - j if side == 0 else j - 1 - field.skip)
                            parts = sides[side]
                        else:
                            other = plan.inner.fields[field.group]
                            source = other.low_at + other.low - j if side == 0 else other.high_at + j - 1
                            parts = inner_sides[side]
                        put(base + k, field, *find(parts, source))
                    source, lanes = plan.folded(k, plan.packed_at[side])
                    put_packed(base + k, *find(sides[side], source), lanes)
                base += plan.low

        @pl.when(flags[3] == 0.0)
        def _():
            up[...] = jnp.zeros(up.shape, jnp.float32)

        @pl.when(flags[2] == 0.0)
        def _():
            down[...] = jnp.zeros(down.shape, jnp.float32)

    last = plan.y // ROWS - 1
    specs, operands = [in_smem()], [flags]
    if own:
        for array in arrays:
            block = (array.shape[0], plan.x, ROWS, plan.z)
            specs.append(pl.BlockSpec(block, lambda i: (0, 0, 0, 0)))
            specs.append(pl.BlockSpec(block, lambda i: (0, 0, last, 0)))
            operands += [array, array]
    for array in ([packed] if own else []) + [*planes, *inner_planes]:
        block = (array.shape[0], ROWS, array.shape[2])
        specs.append(pl.BlockSpec(block, lambda i: (0, 0, 0)))
        specs.append(pl.BlockSpec(block, lambda i: (0, last, 0)))
        operands += [array, array]
    count = plan.x * own + (plan.low + plan.high) * bool(planes)
    shapes = [(count, round_up(max(sizes), ROWS), plan.z)] * 2
    return pl.pallas_call(
        kernel,
        grid=(1,),
        in_specs=specs,
        out_specs=[pl.BlockSpec(shape, lambda i: (0, 0, 0)) for shape in shapes],
        out_shape=[jax.ShapeDtypeStruct(shape, jnp.float32) for shape in shapes],
        compiler_params=pltpu.CompilerParams(vmem_limit_bytes=VMEM_BYTES),
        cost_estimate=cost(0.5),
        name="pack_rows",
    )(*operands)


def exchange_planes(pair):
    count = lax.axis_size("bx")
    return [
        lax.ppermute(one, "bx", [(i, (i + step) % count) for i in range(count)])
        for one, step in zip(pair, (1, -1))
    ]


def exchange_rows(pair, to_self=True):
    count = lax.axis_size("by")
    got = []
    for parity, one in enumerate(pair):
        partner = list(range(count))
        for i in range(parity, count - 1, 2):
            partner[i], partner[i + 1] = i + 1, i
        pairs = [(i, j) for i, j in enumerate(partner) if to_self or i != j]
        got.append(lax.ppermute(one, "by", pairs))
    return got


def assemble(plan, flags, arrays, messages, inner, extended, packed_ext, pinned_own, semaphores):
    count = len(plan.parts[0])
    packed, below, above = messages[0], messages[1 : 1 + count], messages[1 + count : 1 + 2 * count]
    rest = messages[1 + 2 * count :]
    own_messages, halo_messages, halo_at = rest[:2], rest[-2:], plan.x if len(rest) == 2 else 0
    copies = []

    def copy(source, target):
        copies.append(
            pltpu.make_async_copy(source, target, semaphores.at[len(copies)])
        )
        copies[-1].start()

    own_rows = pl.ds(ROWS, plan.y)
    own_planes = pl.ds(plan.low, plan.x)
    for field in plan.fields:
        group, component, low, high, skip = field[:5]
        target = extended[group].at[component]
        after = plan.low + plan.x
        for t in range(plan.tiles):
            lanes = pl.ds(t * LANES, LANES)

            def planes(source, at, first, count):
                if count:
                    source, at = part_of(source, at)
                    copy(
                        source.at[pl.ds(at, count), :, lanes],
                        target.at[pl.ds(first, count), t, own_rows, :],
                    )

            place = target.at[own_planes, t, own_rows, :]
            if group == PINNED:
                place = pinned_own.at[:, t]
            copy(arrays[group].at[component, :, :, lanes], place)
            planes(below, field.low_at, plan.low - low, low - skip)
            planes(above, field.high_at, after + skip, high - skip)
            if skip:
                other = plan.inner.fields[group]
                planes(inner[:1], other.low_at, plan.low - skip, skip)
                planes(inner[1:2], other.high_at, after, skip)
    large = len(copies)
    copy(packed, packed_ext.at[own_planes, own_rows, :])
    for k in range(plan.low):
        source, lanes = plan.folded(k, plan.packed_at[0])
        part, source = part_of(below, source)
        copy(part.at[source, :, pl.ds(lanes, LANES)], packed_ext.at[k, own_rows, :])
    for k in range(plan.high):
        source, lanes = plan.folded(k, plan.packed_at[1])
        part, source = part_of(above, source)
        copy(
            part.at[source, :, pl.ds(lanes, LANES)],
            packed_ext.at[plan.low + plan.x + k, own_rows, :],
        )
    for one in copies[large:]:
        one.wait()

    top = ROWS + plan.y

    def fill(i, left, right, inner_left, inner_right, at, own):
        def rows(field, first, source, source_at, count):
            if count:
                for t in range(plan.tiles):
                    extended[field.group][field.component, i, t, first : first + count, :] = source[
                        at, source_at : source_at + count, t * LANES : (t + 1) * LANES
                    ]

        packed_at = plan.packed_at[:2] if own else plan.packed_at[2:]
        for field in plan.fields:
            low, high, skip = field.low, field.high, field.skip
            if own:
                rows(field, ROWS - low, left, field.low_at, low - skip)
                rows(field, top + skip, right, field.high_at, high - skip)
                if skip:
                    other = plan.inner.fields[field.group]
                    rows(field, ROWS - skip, inner_left, other.low_at, skip)
                    rows(field, top, inner_right, other.high_at, skip)
            else:
                rows(field, ROWS - low, left, field.full_low_at, low)
                rows(field, top, right, field.full_high_at, high)
        for k in range(plan.low):
            row, lanes = plan.folded(k, packed_at[0])
            to = ROWS - plan.low + k
            packed_ext[i, to : to + 1, :] = left[at, row : row + 1, lanes : lanes + LANES]
        for k in range(plan.high):
            row, lanes = plan.folded(k, packed_at[1])
            packed_ext[i, top + k : top + k + 1, :] = right[at, row : row + 1, lanes : lanes + LANES]
        tile = packed_ext[i]
        for field in plan.fields:
            extended[field.group][field.component, i, plan.tiles] = pltpu.roll(
                tile, (LANES - field.start) % LANES, 1
            )

    def fill_all(parity):
        def ordered(pair):
            return pair[::-1] if parity == 0 else pair

        own, halo = ordered(own_messages), ordered(halo_messages)
        inner_rows = (None, None) if inner is None else ordered(inner[2:4])

        def own_plane(x):
            fill(plan.low + x, *own, *inner_rows, x, True)

        def low_plane(k):
            fill(k, *halo, None, None, halo_at + k, False)

        def high_plane(k):
            fill(plan.low + plan.x + k, *halo, None, None, halo_at + plan.low + k, False)

        every_plane(plan.x, own_plane, 2)
        every_plane(plan.low, low_plane, 1)
        every_plane(plan.high, high_plane, 1)

    def finish_plane(x):
        i = plan.low + x
        for t in range(plan.tiles):
            at = (i, t, slice(ROWS, top))

            def get(argument, component):
                if argument == PINNED:
                    return pinned_own[x, t]
                return extended[argument][(component, *at)]

            for group, component in [(POSITION, c) for c in range(3)] + [(PINNED, 0)]:
                extended[group][(component, *at)] = plan.value(group, component, get)

    for parity in range(2):
        pl.when(flags[6] == parity)(functools.partial(fill_all, parity))
    for one in copies[:large]:
        one.wait()
    if pinned_own is not None:
        every_plane(plan.x, finish_plane, 2)


def assemble_copies(plan):
    skipping = sum(field.skip > 0 for field in plan.fields)
    return (3 * len(plan.fields) + 2 * skipping) * plan.tiles + 1 + plan.low + plan.high


def plane_loop(ref, first, last, row, body, carried, unroll):
    def turn(plane, carried, count):
        here = spot(ref, plane, row)
        pending = []
        for k in range(count):
            carried, stores = body(here.at_plane(k), carried)
            pending += stores
        for one in pending:
            store(*one)
        return carried

    count = last - first + 1
    carried = lax.fori_loop(
        0, count // unroll, lambda j, c: turn(first + j * unroll, c, unroll), carried
    )
    rest = count % unroll
    return turn(last + 1 - rest, carried, rest) if rest else carried


class Spot(NamedTuple):
    base: jax.Array
    plane: jax.Array
    planes: int = 0
    rows: int = 0

    def at_plane(self, step):
        return self._replace(planes=self.planes + step)

    def at_row(self, step):
        return self._replace(rows=self.rows + step)


def spot(ref, plane, row):
    return Spot(plane * (ref.shape[-3] * ref.shape[-2]) + row, plane)


def tile_rows(ref, component, at):
    planes, tiles, rows, lanes = ref.shape[-4:]
    first = (component * planes + at.planes) * tiles * rows + at.rows
    flat = ref.reshape(math.prod(ref.shape[:-1]), lanes)
    return flat, [at.base + (first + t * rows) for t in range(tiles)]


def load(ref, component, at):
    flat, starts = tile_rows(ref, component, at)
    return [flat[pl.ds(start, ROWS), :] for start in starts]


def store(ref, component, at, tiles):
    flat, starts = tile_rows(ref, component, at)
    for start, tile in zip(starts, tiles):
        flat[pl.ds(start, ROWS), :] = tile


def each(function, *tiles):
    return [function(*one) for one in zip(*tiles)]


def add(first, second):
    return each(lambda a, b: a + b, first, second)


def subtract(first, second):
    return each(lambda a, b: a - b, first, second)


def lane_below(tiles):
    lane = lane_index((ROWS, LANES))
    rolled = [pltpu.roll(tile, 1, 1) for tile in tiles]
    return [jnp.where(lane == 0, rolled[t - 1], rolled[t]) for t in range(len(tiles))]


def lane_above(tiles):
    lane = lane_index((ROWS, LANES))
    rolled = [pltpu.roll(tile, LANES - 1, 1) for tile in tiles]
    count = len(tiles)
    return [
        jnp.where(lane == LANES - 1, rolled[(t + 1) % count], rolled[t]) for t in range(count)
    ]


def chunks(first, last, body):
    count = -(-(last - first + 1) // ROWS)

    def one(j, _):
        body(jnp.minimum(first + j * ROWS, last - ROWS + 1))
        return 0

    lax.fori_loop(0, count, one, 0)


class Inside:
    def __init__(self, plan, flags):
        self.plan = plan
        self.flags = flags

    def tiles(self, row, scale):
        plan, flags = self.plan, self.flags
        rows = row + lax.broadcasted_iota(jnp.int32, (ROWS, LANES), 0)
        keep = jnp.where(rows < ROWS, flags[2], jnp.where(rows >= ROWS + plan.y, flags[3], 1.0))
        lane = lane_index((ROWS, LANES))
        edge = jnp.where(lane < LANES // 2, flags[5], flags[4])
        keep = scale * keep
        return [keep] * plan.tiles + [keep * edge]

    def plane(self, at):
        plan, flags = self.plan, self.flags
        i = at.plane + at.planes
        return jnp.where(
            i < plan.low, flags[0], jnp.where(i >= plan.low + plan.x, flags[1], 1.0)
        )


def force_pass(density, energy, force, mass, inside, planes, rows, unroll):
    def chunk(row):
        keep = inside.tiles(row, 0.4 * 0.25)

        def slab(at):
            here, under = load(density, 0, at), load(density, 0, at.at_row(-1))
            p = each(lambda a, b: a * b, here, load(energy, 0, at))
            p_under = each(lambda a, b: a * b, under, load(energy, 0, at.at_row(-1)))
            summed, stepped = add(p, p_under), subtract(p_under, p)
            weight = add(here, under)
            summed_z, stepped_z = lane_below(summed), lane_below(stepped)
            return (
                add(summed, summed_z),
                add(stepped, stepped_z),
                subtract(summed_z, summed),
                add(weight, lane_below(weight)),
            )

        def plane(at, before):
            now = slab(at)
            here = inside.plane(at)
            scale = [tile * here for tile in keep]
            stores = []
            for component in range(3):
                across = (subtract if component == 0 else add)(before[component], now[component])
                result = each(lambda a, b: a * b, scale, across)
                stores.append((force, component, at, result))
            result = each(lambda a, b: 0.125 * (a + b) + 6.0 * CONSISTENT, before[3], now[3])
            stores.append((mass, 0, at, result))
            return now, stores

        plane_loop(density, *planes, row, plane, slab(spot(density, planes[0] - 1, row)), unroll)

    chunks(*rows, chunk)


def face_sum(ref, component, at, before, here, after):
    total = add(add(before, after), add(lane_below(here), lane_above(here)))
    sides = add(load(ref, component, at.at_row(-1)), load(ref, component, at.at_row(1)))
    return add(total, sides)


def stencil_pass(ref, planes, rows, setup, use, unroll):
    def chunk(row):
        given = setup(row)

        def plane(at, carried):
            before, here = carried
            after = [load(ref, component, at.at_plane(1)) for component in range(3)]
            sums = [
                face_sum(ref, component, at, before[component], here[component], after[component])
                for component in range(3)
            ]
            return (here, after), use(at, here, sums, given)

        start = spot(ref, planes[0], row)
        first = [load(ref, component, start.at_plane(-1)) for component in range(3)]
        second = [load(ref, component, start) for component in range(3)]
        plane_loop(ref, *planes, row, plane, (first, second), unroll)

    chunks(*rows, chunk)


def whole_sum(tile):
    return jnp.sum(jnp.sum(tile, axis=0, keepdims=True), axis=1, keepdims=True)


def moments_kernel(plan, *refs):
    flags, density, energy = refs[:3]
    messages, out = refs[3:8], refs[8]
    density_ext, energy_ext, packed_ext, force, image, mass, semaphores = refs[9:]
    assemble(
        plan,
        flags,
        [density, energy],
        messages,
        None,
        [density_ext, energy_ext],
        packed_ext,
        None,
        semaphores,
    )
    inside = Inside(plan, flags)
    low, x, y = plan.low, plan.x, plan.y
    force_pass(
        density_ext,
        energy_ext,
        force,
        mass,
        inside,
        (low - 1, low + x + 1),
        (ROWS - 1, ROWS + y + 1),
        MOMENTS_UNROLL,
    )

    def multiply(at, here, sums, keep):
        weight = load(mass, 0, at)
        scale = [tile * inside.plane(at) for tile in keep]
        stores = []
        for component in range(3):
            result = each(
                lambda m, a, k, s: m * a + k * s, weight, here[component], scale, sums[component]
            )
            stores.append((image, component, at, result))
        return stores

    stencil_pass(
        force,
        (low, low + x),
        (ROWS, ROWS + y),
        lambda row: inside.tiles(row, CONSISTENT),
        multiply,
        MOMENTS_UNROLL,
    )

    own = range(plan.tiles)
    nothing = jnp.zeros((ROWS, LANES), jnp.float32)

    def first_chunk(j, sums):
        row = ROWS + j * ROWS

        def plane(at, sums):
            sums = list(sums)
            for component in range(3):
                f = load(force, component, at)
                v = load(image, component, at)
                for t in own:
                    sums[component] = sums[component] + f[t] * f[t]
                    sums[3 + component] = sums[3 + component] + f[t] * v[t]
            return tuple(sums), []

        return plane_loop(force, low, low + x - 1, row, plane, sums, MOMENTS_UNROLL)

    sums = lax.fori_loop(0, y // ROWS, first_chunk, (nothing,) * 6)
    sums = [whole_sum(one) for one in sums]
    square = sums[:3]
    shift = [
        jnp.where(square[c] > 0, sums[3 + c] / jnp.where(square[c] > 0, square[c], 1.0), 0.0)
        for c in range(3)
    ]

    def pair(component, at):
        f = load(force, component, at)
        v = load(image, component, at)
        return f, each(lambda a, b: a - shift[component] * b, v, f)

    def second_chunk(j, sums):
        row = ROWS + j * ROWS

        def plane(at, carried):
            here, sums = carried
            sums = list(sums)
            ahead = [pair(component, at.at_plane(1)) for component in range(3)]
            weight = load(mass, 0, at)
            for component in range(3):
                f, w = here[component]
                f_next, w_next = ahead[component]
                f_up, w_up = pair(component, at.at_row(1))
                f_high = add(add(f_next, f_up), lane_above(f))
                w_high = add(add(w_next, w_up), lane_above(w))
                for t in own:
                    k = 5 * component
                    heavy = weight[t] * w[t]
                    sums[k] = sums[k] + f[t] * w[t]
                    sums[k + 1] = sums[k + 1] + w[t] * w[t]
                    sums[k + 2] = sums[k + 2] + (
                        f[t] * heavy + CONSISTENT * (f[t] * w_high[t] + w[t] * f_high[t])
                    )
                    sums[k + 3] = sums[k + 3] + w[t] * (
                        heavy + (2.0 * CONSISTENT) * w_high[t]
                    )
                    sums[k + 4] = sums[k + 4] + f[t] * (
                        weight[t] * f[t] + (2.0 * CONSISTENT) * f_high[t]
                    )
            return (ahead, tuple(sums)), []

        start = [pair(component, spot(force, low, row)) for component in range(3)]
        return plane_loop(force, low, low + x - 1, row, plane, (start, sums), MOMENTS_UNROLL)[1]

    rest = lax.fori_loop(0, y // ROWS, second_chunk, (nothing,) * 15)
    lane = lane_index((1, LANES))
    line = jnp.zeros((1, LANES), jnp.float32)
    for c in range(3):
        values = [shift[c], square[c]] + [whole_sum(one) for one in rest[5 * c : 5 * c + 5]]
        for k, value in enumerate(values):
            line = jnp.where(lane == 3 * k + c, value, line)
    out[...] = line


def solve_weights(sums):
    got = [sums if k == 0 else pltpu.roll(sums, LANES - 3 * k, 1) for k in range(MOMENTS)]
    c, p0, q1, q2, q3, q4, q5 = got

    def total(value):
        return jnp.sum(value, axis=0, keepdims=True)

    norm_now = total(p0)
    alpha = norm_now / total(q1 + c * p0)
    a = 1.0 - alpha * c
    norm_next = total(a * a * p0 - 2.0 * a * alpha * q1 + alpha * alpha * q2)
    product = total(a * a * q5 - 2.0 * a * alpha * q3 + alpha * alpha * q4)
    ratio = norm_next / norm_now
    later = norm_next / (product - ratio * norm_next / alpha)
    lane = lane_index((1, LANES))

    def pick(value, component):
        return jnp.sum(jnp.where(lane == component, value, 0.0), axis=1, keepdims=True)

    on_force, on_image = alpha + later * (1.0 + ratio), -later * alpha
    return [(pick(on_force, k), pick(on_image, k)) for k in range(3)]


def step_kernel(plan, *refs):
    flags, sums, density, energy, position, velocity, pinned = refs[:7]
    messages, inner = refs[7:14], refs[14:18]
    velocity_new, accel, relaxed, density_new, energy_new = refs[18:23]
    (
        density_ext,
        energy_ext,
        moved,
        speed,
        free_ext,
        packed_ext,
        pinned_own,
        force,
        mass,
        other,
        semaphores,
        out_semaphores,
    ) = refs[23:]
    assemble(
        plan,
        flags,
        [density, energy, position, velocity, pinned],
        messages,
        inner,
        [density_ext, energy_ext, moved, speed, free_ext],
        packed_ext,
        pinned_own,
        semaphores,
    )
    inside = Inside(plan, flags)
    low, x, y = plan.low, plan.x, plan.y
    weights = solve_weights(sums[...])
    reach = SWEEPS + 1
    force_pass(
        density_ext,
        energy_ext,
        force,
        mass,
        inside,
        (low - reach, low + x + reach),
        (ROWS - reach, ROWS + y + reach),
        STEP_UNROLL,
    )

    def advance(at, here, sums, keep):
        weight = load(mass, 0, at)
        scale = [tile * inside.plane(at) for tile in keep]
        stores = []
        for component in range(3):
            on_force, on_image = weights[component]
            result = each(
                lambda m, a, k, s: on_force * a + on_image * (m * a + k * s),
                weight,
                here[component],
                scale,
                sums[component],
            )
            faster = each(lambda v, a: v + TIME_STEP * a, load(speed, component, at), result)
            further = each(
                lambda b, a: b + (TIME_STEP * TIME_STEP) * a, load(moved, component, at), result
            )
            stores += [
                (other, component, at, result),
                (speed, component, at, faster),
                (moved, component, at, further),
            ]
        return stores

    reach -= 1
    advanced = round_up(y + 2 * reach + 1, ROWS)
    stencil_pass(
        force,
        (low - reach, low + x + reach),
        (ROWS - reach, ROWS - reach + advanced - 1),
        lambda row: inside.tiles(row, CONSISTENT),
        advance,
        STEP_UNROLL,
    )

    out_copies = []

    def write(source, target, component, result=None):
        for t in range(plan.tiles):
            place = target if result is None else target.at[result]
            out_copies.append(
                pltpu.make_async_copy(
                    source.at[component, pl.ds(low, x), t, pl.ds(ROWS, y), :],
                    place.at[:, :, pl.ds(t * LANES, LANES)],
                    out_semaphores.at[len(out_copies)],
                )
            )
            out_copies[-1].start()

    for component in range(3):
        write(other, accel, component, component)
    accel_copies = len(out_copies)
    for component in range(3):
        write(speed, velocity_new, component, component)

    content = mass

    def content_chunk(row):
        def slab(at):
            under = [load(speed, component, at) for component in range(3)]
            over = [load(speed, component, at.at_row(1)) for component in range(3)]
            along_x = add(under[0], over[0])
            along_y = subtract(over[1], under[1])
            along_z = add(under[2], over[2])
            along_x = add(along_x, lane_above(along_x))
            along_y = add(along_y, lane_above(along_y))
            along_z = subtract(lane_above(along_z), along_z)
            return along_x, add(along_y, along_z)

        def plane(at, before):
            now = slab(at.at_plane(1))
            spread = add(subtract(now[0], before[0]), add(now[1], before[1]))
            held = load(energy_ext, 0, at)
            lagged = each(lambda e, s: e - (0.25 * 0.4 * TIME_STEP) * (e * s), held, spread)
            result = each(lambda d, e: d * e, load(density_ext, 0, at), lagged)
            return now, [(content, 0, at, result)]

        plane_loop(speed, low - 1, low + x, row, plane, slab(spot(speed, low - 1, row)), STEP_UNROLL)

    chunks(ROWS - 1, ROWS + y, content_chunk)

    for one in out_copies[:accel_copies]:
        one.wait()
    source, target = moved, other
    for _ in range(SWEEPS):
        reach -= 1

        def relax(at, here, sums, given, target=target):
            rate = load(free_ext, 0, at)
            stores = []
            for component in range(3):
                result = each(
                    lambda r, s, f: r + f * (s * (1.0 / 6.0) - r),
                    here[component],
                    sums[component],
                    rate,
                )
                stores.append((target, component, at, result))
            return stores

        stencil_pass(
            source,
            (low - reach, low + x + reach),
            (ROWS - reach, ROWS + y + reach),
            lambda row: None,
            relax,
            STEP_UNROLL,
        )
        source, target = target, (force if target is other else other)
    settled, free_buffer = source, target
    for component in range(3):
        write(settled, relaxed, component, component)

    quantities = (density_ext, content)

    def remap_chunk(row):
        def shift(component, at):
            return subtract(load(settled, component, at), load(moved, component, at))

        def slab(at):
            over = at.at_row(1)
            x_here = add(shift(0, at), shift(0, over))
            y_here, y_over = shift(1, at), shift(1, over)
            z_here = add(shift(2, at), shift(2, over))
            return (
                add(x_here, lane_above(x_here)),
                add(y_here, lane_above(y_here)),
                add(y_over, lane_above(y_over)),
                z_here,
                [load(one, 0, at) for one in quantities],
            )

        def flux(speeds, upper, lower):
            return each(lambda s, u, l: s * jnp.where(s > 0, u, l), speeds, upper, lower)

        def x_flux(speeds, upper, lower):
            return [flux(speeds, u, l) for u, l in zip(upper, lower)]

        def plane(at, carried):
            now, entering = carried
            ahead = slab(at.at_plane(1))
            leaving = x_flux(ahead[0], ahead[4], now[4])
            y_here, y_over, z_here = [add(now[k], ahead[k]) for k in (1, 2, 3)]
            stores = []
            for k, one in enumerate(quantities):
                held = now[4][k]
                under, over = [load(one, 0, at.at_row(step)) for step in (-1, 1)]
                through_z = flux(z_here, held, lane_below(held))
                change = subtract(leaving[k], entering[k])
                change = add(change, flux(y_over, over, held))
                change = subtract(change, flux(y_here, held, under))
                change = add(change, subtract(lane_above(through_z), through_z))
                result = each(lambda q, c: q + 0.25 * c, held, change)
                stores.append((free_buffer, k, at, result[: plan.tiles]))
            return (ahead, leaving), stores

        first = spot(settled, low, row)
        start = slab(first)
        before = [load(one, 0, first.at_plane(-1)) for one in quantities]
        plane_loop(settled, low, low + x - 1, row, plane, (start, x_flux(start[0], start[4], before)), STEP_UNROLL)

    chunks(ROWS, ROWS + y - 1, remap_chunk)
    write(free_buffer, density_new, 0)
    write(free_buffer, energy_new, 1)
    for one in out_copies[accel_copies:]:
        one.wait()


def line_hops():
    hops = []
    for axis in ("bz", "by", "bx"):
        step = 1
        while step < lax.axis_size(axis):
            hops.append((axis, step))
            step *= 2
    return hops


def gather_lines(line, hops):
    for axis, step in hops:
        count = lax.axis_size(axis)
        assert count & (count - 1) == 0
        got = lax.ppermute(line, axis, [(i, i ^ step) for i in range(count)])
        later = (lax.axis_index(axis) // step) % 2 == 1
        line = jnp.concatenate([jnp.where(later, got, line), jnp.where(later, line, got)])
    return line


def extended_scratch(plan, count):
    return pltpu.VMEM((count, plan.planes, plan.tiles + 1, plan.rows, LANES), jnp.float32)


def message_specs(planes, rows):
    return [any_space()] * planes + [in_vmem()] * rows


def on_device(position, velocity, density, energy, pinned):
    shape = density.shape
    arrays = [density[None], energy[None], position, velocity, pinned[None]]
    flags = jnp.stack(
        [
            jnp.float32(limit)
            for axis in ("bx", "by", "bz")
            for limit in (
                lax.axis_index(axis) > 0,
                lax.axis_index(axis) < lax.axis_size(axis) - 1,
            )
        ]
        + [(lax.axis_index("by") % 2).astype(jnp.float32)]
    )
    groups = [
        (1, WIDE, WIDE),
        (1, WIDE, WIDE),
        (3, SWEEPS, SWEEPS + 1),
        (3, 1, 2),
        (1, SWEEPS - 1, SWEEPS),
    ]
    narrow = Plan([(1, NARROW, NARROW)] * 2, shape)
    wide = Plan(groups, shape, narrow, cut=None)
    cells = arrays[:2]

    packed = exchange_lanes(narrow, pack_lanes(narrow, cells))
    planes = exchange_planes(*pack_planes(narrow, flags, cells, packed))
    wide_lanes = pack_lanes(wide, arrays)
    planes, wide_lanes = lax.optimization_barrier((planes, wide_lanes))
    wide_packed = exchange_lanes(wide, wide_lanes)
    rows = exchange_rows(pack_rows(narrow, flags, cells, packed, True, planes))

    (wide_planes,) = pack_planes(wide, flags, arrays, wide_packed)
    wide_rows = pack_rows(wide, flags, arrays, wide_packed, True)
    rows, wide_planes, wide_rows = lax.optimization_barrier((rows, wide_planes, wide_rows))
    wide_planes = exchange_planes(wide_planes)
    wide_rows = exchange_rows(wide_rows, to_self=False)

    line = pl.pallas_call(
        functools.partial(moments_kernel, narrow),
        in_specs=[in_smem()] + [any_space()] * 2 + message_specs(3, 2),
        out_specs=in_vmem(),
        out_shape=jax.ShapeDtypeStruct((1, LANES), jnp.float32),
        scratch_shapes=[
            extended_scratch(narrow, 1),
            extended_scratch(narrow, 1),
            pltpu.VMEM((narrow.planes, narrow.rows, LANES), jnp.float32),
            extended_scratch(narrow, 3),
            extended_scratch(narrow, 3),
            extended_scratch(narrow, 1),
            pltpu.SemaphoreType.DMA((assemble_copies(narrow),)),
        ],
        compiler_params=pltpu.CompilerParams(vmem_limit_bytes=VMEM_BYTES),
        cost_estimate=cost(1),
        name="moments",
    )(flags, *cells, packed, *planes, *rows)

    line, wide_rows = lax.optimization_barrier((line, wide_rows))
    hops = line_hops()
    early = len(hops) - 3
    lines = gather_lines(line, hops[:early])
    lines, wide_planes = lax.optimization_barrier((lines, wide_planes))
    corners = pack_rows(wide, flags, None, None, False, wide_planes, planes)
    lines, corners = lax.optimization_barrier((lines, corners))
    corners = exchange_rows(corners)
    messages = [wide_packed, *wide_planes, *wide_rows, *corners]
    nodes = jax.ShapeDtypeStruct((3, *shape), jnp.float32)
    cell = jax.ShapeDtypeStruct(shape, jnp.float32)
    return pl.pallas_call(
        functools.partial(step_kernel, wide),
        in_specs=[in_smem(), in_vmem()] + [any_space()] * 5 + message_specs(3, 4) + message_specs(2, 2),
        out_specs=[any_space()] * 5,
        out_shape=[nodes, nodes, nodes, cell, cell],
        scratch_shapes=[
            extended_scratch(wide, 1),
            extended_scratch(wide, 1),
            extended_scratch(wide, 3),
            extended_scratch(wide, 3),
            extended_scratch(wide, 1),
            pltpu.VMEM((wide.planes, wide.rows, LANES), jnp.float32),
            pltpu.VMEM((wide.x, wide.tiles, wide.y, LANES), jnp.int32),
            extended_scratch(wide, 3),
            extended_scratch(wide, 1),
            extended_scratch(wide, 3),
            pltpu.SemaphoreType.DMA((assemble_copies(wide),)),
            pltpu.SemaphoreType.DMA((11 * wide.tiles,)),
        ],
        compiler_params=pltpu.CompilerParams(vmem_limit_bytes=VMEM_BYTES),
        cost_estimate=cost(1),
        name="step",
    )(flags, gather_lines(lines, hops[early:]), *arrays, *messages, *planes, *rows)


def solution(mesh):
    in_specs = (
        P(None, "bx", "by", "bz"),
        P(None, "bx", "by", "bz"),
        P("bx", "by", "bz"),
        P("bx", "by", "bz"),
        P("bx", "by", "bz"),
    )
    out_specs = (
        P(None, "bx", "by", "bz"),
        P(None, "bx", "by", "bz"),
        P(None, "bx", "by", "bz"),
        P("bx", "by", "bz"),
        P("bx", "by", "bz"),
    )
    return jax.shard_map(
        on_device, mesh=mesh, in_specs=in_specs, out_specs=out_specs, check_vma=False
    )
```

```python
import functools
import math
from typing import NamedTuple

import jax
import jax.numpy as jnp
from jax import lax
from jax.experimental import pallas as pl
from jax.experimental.pallas import tpu as pltpu
from jax.sharding import PartitionSpec as P

SWEEPS = 3
TIME_STEP = 0.6
RELAX_RATE = 0.8
CONSISTENT = 0.2

LANES = 128
ROWS = 8
MOMENTS = 7
MOMENTS_UNROLL = 18
STEP_UNROLL = 13
POSITION, VELOCITY, PINNED = 2, 3, 4
NARROW = 2
WIDE = SWEEPS + 2
VMEM_BYTES = 62 * 2**20


class Field(NamedTuple):
    group: int
    component: int
    low: int
    high: int
    skip: int
    low_at: int
    high_at: int
    full_low_at: int
    full_high_at: int
    start: int


class Plan:
    def __init__(self, groups, shape, inner=None, starts=None, cut=None):
        self.groups = groups
        self.inner = inner
        self.x, self.y, self.z = shape
        self.tiles = self.z // LANES
        self.low = max(low for _, low, _ in groups)
        self.high = max(high for _, _, high in groups)
        self.planes = self.low + self.x + self.high
        self.rows = self.y + 2 * ROWS
        self.fields = []
        at = [0] * 4
        lane_at = 0
        for group, (count, low, high) in enumerate(groups):
            skip = 0 if inner is None or group >= len(inner.groups) else inner.low
            for component in range(count):
                start = lane_at + low if starts is None else starts[len(self.fields)]
                self.fields.append(Field(group, component, low, high, skip, *at, start))
                for k, size in enumerate((low - skip, high - skip, low, high)):
                    at[k] += size
                lane_at += low + high
        assert lane_at <= LANES
        self.starts = [field.start for field in self.fields]
        self.packed_at = at
        depths = (self.low, self.high) * 2
        self.sizes = [one + -(-depth // self.tiles) for one, depth in zip(at, depths)]
        cuts = [] if cut is None else [(self.fields[cut].low_at, self.fields[cut].high_at)]
        self.parts = []
        for side in range(2):
            ends = [0, *(one[side] for one in cuts), self.sizes[side]]
            self.parts.append([b - a for a, b in zip(ends, ends[1:])])

    def value(self, group, component, get):
        if group == POSITION:
            return get(POSITION, component) + TIME_STEP * get(VELOCITY, component)
        if group == PINNED:
            return RELAX_RATE * (1.0 - get(PINNED, component).astype(jnp.float32))
        return get(group, component)

    def folded(self, k, at):
        return at + k // self.tiles, (k % self.tiles) * LANES


def round_up(value, step):
    return -(-value // step) * step


def from_behind(x, axis):
    count = lax.axis_size(axis)
    return lax.ppermute(x, axis, [(i, i + 1) for i in range(count - 1)])


def from_ahead(x, axis):
    count = lax.axis_size(axis)
    return lax.ppermute(x, axis, [(i + 1, i) for i in range(count - 1)])


def any_space():
    return pl.BlockSpec(memory_space=pl.ANY)


def in_vmem():
    return pl.BlockSpec(memory_space=pltpu.VMEM)


def in_smem():
    return pl.BlockSpec(memory_space=pltpu.SMEM)


def cost(microseconds):
    return pl.CostEstimate(
        flops=0, bytes_accessed=int(microseconds * 3.0e6), transcendentals=0
    )


def every_plane(count, body, together):
    together = together if count % together == 0 else 1

    def turn(j, _):
        for k in range(together):
            body(j * together + k)
        return 0

    lax.fori_loop(0, count // together, turn, 0)


def lane_index(shape):
    return lax.broadcasted_iota(jnp.int32, shape, len(shape) - 1)


def pack_lanes(plan, arrays):
    half = LANES // 2

    def kernel(*refs):
        out = refs[-1]
        lane = lane_index((plan.y, LANES))
        in_low_half = lane < half

        def plane(x, _):
            def edge(group, component):
                first, last = refs[2 * group], refs[2 * group + 1]
                return jnp.where(in_low_half, first[component, x], last[component, x])

            packed = jnp.zeros((plan.y, LANES), jnp.float32)
            for group, component, low, high, *_, start in plan.fields:
                moved = pltpu.roll(plan.value(group, component, edge), start, 1)
                packed = jnp.where((lane >= start - low) & (lane < start + high), moved, packed)
            out[x] = packed
            return 0

        for x in range(planes):
            plane(x, 0)

    planes = next(n for n in (16 if len(arrays) == 2 else 8, 4, 1) if plan.x % n == 0)
    specs, operands = [], []
    for (count, _, _), array in zip(plan.groups, arrays):
        block = (count, planes, plan.y, LANES)
        specs.append(pl.BlockSpec(block, lambda i: (0, i, 0, 0)))
        specs.append(pl.BlockSpec(block, lambda i: (0, i, 0, plan.tiles - 1)))
        operands += [array, array]
    return pl.pallas_call(
        kernel,
        grid=(plan.x // planes,),
        in_specs=specs,
        out_specs=pl.BlockSpec((planes, plan.y, LANES), lambda i: (i, 0, 0)),
        out_shape=jax.ShapeDtypeStruct((plan.x, plan.y, LANES), jnp.float32),
        compiler_params=pltpu.CompilerParams(vmem_limit_bytes=VMEM_BYTES),
        cost_estimate=cost(0.5),
        name="pack_lanes",
    )(*operands)


def exchange_lanes(plan, packed):
    lane = lane_index((1, 1, LANES))
    is_low = functools.reduce(
        jnp.logical_or,
        [(lane >= start - low) & (lane < start) for _, _, low, *_, start in plan.fields],
    )
    count = lax.axis_size("bz")
    if count == 2:
        got = lax.ppermute(packed, "bz", [(0, 1), (1, 0)])
        return jnp.where(is_low == (lax.axis_index("bz") == 1), got, 0.0)
    return jnp.where(is_low, from_behind(packed, "bz"), from_ahead(packed, "bz"))


def part_of(parts, at):
    for part in parts:
        if at < part.shape[0]:
            return part, at
        at -= part.shape[0]


def pack_planes(plan, flags, arrays, packed):
    needed = [
        max(low if to_low else high for _, low, high in plan.groups) for to_low in (True, False)
    ]
    depths = [(low, high) for _, low, high in plan.groups]
    if len(depths) > VELOCITY:
        depths[VELOCITY] = depths[POSITION]

    def kernel(*refs):
        groups = len(plan.groups)
        edge, refs = refs[0], refs[1:]
        own, packed_ref = refs[:groups], refs[groups]
        count = len(plan.parts[0])
        outs = refs[groups + 1 : groups + 1 + count], refs[groups + 1 + count : groups + 1 + 2 * count]
        edges, semaphores = refs[groups + 1 + 2 * count : -1], refs[-1]
        copies = []

        def copy(source, target):
            copies.append(pltpu.make_async_copy(source, target, semaphores.at[len(copies)]))
            copies[-1].start()

        for side, out in enumerate(outs):
            for group, array in enumerate(own):
                depth = depths[group][side]
                planes = pl.ds(plan.x - depth, depth) if side == 0 else pl.ds(0, depth)
                copy(array.at[:, planes], edges[2 * group + side])
            first = plan.x - needed[0] if side == 0 else 0
            at = plan.packed_at[side]
            for k in range(needed[side]):
                row, lanes = plan.folded(k, at)
                part, row = part_of(out, row)
                copy(packed_ref.at[first + k], part.at[row, :, pl.ds(lanes, LANES)])
        for one in copies:
            one.wait()
        for side, out in enumerate(outs):
            for field in plan.fields:
                at = (field.low_at, field.high_at)[side]
                depth = (field.low, field.high)[side] - field.skip

                def get(argument, part):
                    held = edges[2 * argument + side]
                    first = depths[argument][0] - field.low if side == 0 else field.skip
                    return held[part, first : first + depth]

                part, at = part_of(out, at)
                part[at : at + depth] = plan.value(field.group, field.component, get)

        for side, parts in enumerate(outs):

            @pl.when(edge[1 - side] == 0.0)
            def _(parts=parts):
                for part in parts:
                    part[...] = jnp.zeros(part.shape, jnp.float32)

    shapes = [(size, plan.y, plan.z) for side in plan.parts for size in side]
    scratch = [
        pltpu.VMEM((array.shape[0], depth, plan.y, plan.z), array.dtype)
        for array, pair in zip(arrays, depths)
        for depth in pair
    ]
    count = 2 * len(arrays) + sum(needed)
    outs = pl.pallas_call(
        kernel,
        in_specs=[in_smem()] + [any_space()] * (len(arrays) + 1),
        out_specs=[in_vmem()] * len(shapes),
        out_shape=[jax.ShapeDtypeStruct(shape, jnp.float32) for shape in shapes],
        scratch_shapes=scratch + [pltpu.SemaphoreType.DMA((count,))],
        compiler_params=pltpu.CompilerParams(vmem_limit_bytes=VMEM_BYTES),
        cost_estimate=cost(0.5),
        name="pack_planes",
    )(flags, *arrays, packed)
    return list(zip(outs[: len(plan.parts[0])], outs[len(plan.parts[0]) :]))


def pack_rows(plan, flags, arrays, packed, own, planes=(), inner_planes=()):
    groups = len(plan.groups)
    sizes, packed_at = plan.sizes[2:], plan.packed_at[2:]
    if own:
        sizes, packed_at = plan.sizes[:2], plan.packed_at[:2]

    def kernel(flags, *refs):
        for parity in range(2):
            up, down = refs[-2:] if parity == 0 else refs[:-3:-1]
            pl.when(flags[6] == parity)(functools.partial(pack, flags, list(refs[:-2]), up, down))

    def pack(flags, refs, up, down):
        up[...] = jnp.zeros(up.shape, jnp.float32)
        down[...] = jnp.zeros(down.shape, jnp.float32)

        def put(plane, field, first, last):
            low_at, high_at, skip = field.full_low_at, field.full_high_at, 0
            if own:
                low_at, high_at, skip = field.low_at, field.high_at, field.skip
            low, high = field.low - skip, field.high - skip
            up[plane, low_at : low_at + low, :] = last[ROWS - field.low : ROWS - skip, :]
            down[plane, high_at : high_at + high, :] = first[skip : field.high, :]

        def put_packed(plane, first, last, at):
            for k in range(plan.low):
                row, lanes = plan.folded(k, packed_at[0])
                source = ROWS - plan.low + k
                up[plane, row : row + 1, lanes : lanes + LANES] = last[
                    source : source + 1, at : at + LANES
                ]
            for k in range(plan.high):
                row, lanes = plan.folded(k, packed_at[1])
                down[plane, row : row + 1, lanes : lanes + LANES] = first[
                    k : k + 1, at : at + LANES
                ]

        base = 0
        if own:
            blocks = refs[: 2 * groups + 2]
            del refs[: 2 * groups + 2]
            base = plan.x

            def own_plane(x):
                for field in plan.fields:
                    first, last = [
                        plan.value(
                            *field[:2],
                            lambda argument, part: blocks[2 * argument + side][part, x],
                        )
                        for side in range(2)
                    ]
                    put(x, field, first, last)
                put_packed(x, blocks[-2].at[x], blocks[-1].at[x], 0)

            every_plane(plan.x, own_plane, 4)
        if planes:
            count = len(plan.parts[0])
            pairs = [tuple(refs[2 * k : 2 * k + 2]) for k in range(2 * count + 2)]
            if plan.inner is None:
                pairs = pairs[: 2 * count]
            sides = [pairs[:count], pairs[count : 2 * count]]
            inner_sides = [pairs[2 * count : 2 * count + 1], pairs[2 * count + 1 :]]

            def find(parts, at):
                part, at = part_of([first for first, _ in parts], at)
                pair = next(pair for pair in parts if pair[0] is part)
                return [ref.at[at] for ref in pair]

            for side in range(2):
                for k in range((plan.low, plan.high)[side]):
                    for field in plan.fields:
                        depth, at = (field.low, field.low_at) if side == 0 else (field.high, field.high_at)
                        j = plan.low - k if side == 0 else k + 1
                        if j > depth:
                            continue
                        if j > field.skip:
                            source = at + (depth - j if side == 0 else j - 1 - field.skip)
                            parts = sides[side]
                        else:
                            other = plan.inner.fields[field.group]
                            source = other.low_at + other.low - j if side == 0 else other.high_at + j - 1
                            parts = inner_sides[side]
                        put(base + k, field, *find(parts, source))
                    source, lanes = plan.folded(k, plan.packed_at[side])
                    put_packed(base + k, *find(sides[side], source), lanes)
                base += plan.low

        @pl.when(flags[3] == 0.0)
        def _():
            up[...] = jnp.zeros(up.shape, jnp.float32)

        @pl.when(flags[2] == 0.0)
        def _():
            down[...] = jnp.zeros(down.shape, jnp.float32)

    last = plan.y // ROWS - 1
    specs, operands = [in_smem()], [flags]
    if own:
        for array in arrays:
            block = (array.shape[0], plan.x, ROWS, plan.z)
            specs.append(pl.BlockSpec(block, lambda i: (0, 0, 0, 0)))
            specs.append(pl.BlockSpec(block, lambda i: (0, 0, last, 0)))
            operands += [array, array]
    for array in ([packed] if own else []) + [*planes, *inner_planes]:
        block = (array.shape[0], ROWS, array.shape[2])
        specs.append(pl.BlockSpec(block, lambda i: (0, 0, 0)))
        specs.append(pl.BlockSpec(block, lambda i: (0, last, 0)))
        operands += [array, array]
    count = plan.x * own + (plan.low + plan.high) * bool(planes)
    shapes = [(count, round_up(max(sizes), ROWS), plan.z)] * 2
    return pl.pallas_call(
        kernel,
        grid=(1,),
        in_specs=specs,
        out_specs=[pl.BlockSpec(shape, lambda i: (0, 0, 0)) for shape in shapes],
        out_shape=[jax.ShapeDtypeStruct(shape, jnp.float32) for shape in shapes],
        compiler_params=pltpu.CompilerParams(vmem_limit_bytes=VMEM_BYTES),
        cost_estimate=cost(0.5),
        name="pack_rows",
    )(*operands)


def exchange_planes(pair):
    count = lax.axis_size("bx")
    return [
        lax.ppermute(one, "bx", [(i, (i + step) % count) for i in range(count)])
        for one, step in zip(pair, (1, -1))
    ]


def exchange_rows(pair, to_self=True):
    count = lax.axis_size("by")
    got = []
    for parity, one in enumerate(pair):
        partner = list(range(count))
        for i in range(parity, count - 1, 2):
            partner[i], partner[i + 1] = i + 1, i
        pairs = [(i, j) for i, j in enumerate(partner) if to_self or i != j]
        got.append(lax.ppermute(one, "by", pairs))
    return got


def assemble(plan, flags, arrays, messages, inner, extended, packed_ext, pinned_own, semaphores):
    count = len(plan.parts[0])
    packed, below, above = messages[0], messages[1 : 1 + count], messages[1 + count : 1 + 2 * count]
    rest = messages[1 + 2 * count :]
    own_messages, halo_messages, halo_at = rest[:2], rest[-2:], plan.x if len(rest) == 2 else 0
    copies = []

    def copy(source, target):
        copies.append(
            pltpu.make_async_copy(source, target, semaphores.at[len(copies)])
        )
        copies[-1].start()

    own_rows = pl.ds(ROWS, plan.y)
    own_planes = pl.ds(plan.low, plan.x)
    for field in plan.fields:
        group, component, low, high, skip = field[:5]
        target = extended[group].at[component]
        after = plan.low + plan.x
        for t in range(plan.tiles):
            lanes = pl.ds(t * LANES, LANES)

            def planes(source, at, first, count):
                if count:
                    source, at = part_of(source, at)
                    copy(
                        source.at[pl.ds(at, count), :, lanes],
                        target.at[pl.ds(first, count), t, own_rows, :],
                    )

            place = target.at[own_planes, t, own_rows, :]
            if group == PINNED:
                place = pinned_own.at[:, t]
            copy(arrays[group].at[component, :, :, lanes], place)
            planes(below, field.low_at, plan.low - low, low - skip)
            planes(above, field.high_at, after + skip, high - skip)
            if skip:
                other = plan.inner.fields[group]
                planes(inner[:1], other.low_at, plan.low - skip, skip)
                planes(inner[1:2], other.high_at, after, skip)
    large = len(copies)
    copy(packed, packed_ext.at[own_planes, own_rows, :])
    for k in range(plan.low):
        source, lanes = plan.folded(k, plan.packed_at[0])
        part, source = part_of(below, source)
        copy(part.at[source, :, pl.ds(lanes, LANES)], packed_ext.at[k, own_rows, :])
    for k in range(plan.high):
        source, lanes = plan.folded(k, plan.packed_at[1])
        part, source = part_of(above, source)
        copy(
            part.at[source, :, pl.ds(lanes, LANES)],
            packed_ext.at[plan.low + plan.x + k, own_rows, :],
        )
    for one in copies[large:]:
        one.wait()

    top = ROWS + plan.y

    def fill(i, left, right, inner_left, inner_right, at, own):
        def rows(field, first, source, source_at, count):
            if count:
                for t in range(plan.tiles):
                    extended[field.group][field.component, i, t, first : first + count, :] = source[
                        at, source_at : source_at + count, t * LANES : (t + 1) * LANES
                    ]

        packed_at = plan.packed_at[:2] if own else plan.packed_at[2:]
        for field in plan.fields:
            low, high, skip = field.low, field.high, field.skip
            if own:
                rows(field, ROWS - low, left, field.low_at, low - skip)
                rows(field, top + skip, right, field.high_at, high - skip)
                if skip:
                    other = plan.inner.fields[field.group]
                    rows(field, ROWS - skip, inner_left, other.low_at, skip)
                    rows(field, top, inner_right, other.high_at, skip)
            else:
                rows(field, ROWS - low, left, field.full_low_at, low)
                rows(field, top, right, field.full_high_at, high)
        for k in range(plan.low):
            row, lanes = plan.folded(k, packed_at[0])
            to = ROWS - plan.low + k
            packed_ext[i, to : to + 1, :] = left[at, row : row + 1, lanes : lanes + LANES]
        for k in range(plan.high):
            row, lanes = plan.folded(k, packed_at[1])
            packed_ext[i, top + k : top + k + 1, :] = right[at, row : row + 1, lanes : lanes + LANES]
        tile = packed_ext[i]
        for field in plan.fields:
            extended[field.group][field.component, i, plan.tiles] = pltpu.roll(
                tile, (LANES - field.start) % LANES, 1
            )

    def fill_all(parity):
        def ordered(pair):
            return pair[::-1] if parity == 0 else pair

        own, halo = ordered(own_messages), ordered(halo_messages)
        inner_rows = (None, None) if inner is None else ordered(inner[2:4])

        def own_plane(x):
            fill(plan.low + x, *own, *inner_rows, x, True)

        def low_plane(k):
            fill(k, *halo, None, None, halo_at + k, False)

        def high_plane(k):
            fill(plan.low + plan.x + k, *halo, None, None, halo_at + plan.low + k, False)

        every_plane(plan.x, own_plane, 2)
        every_plane(plan.low, low_plane, 1)
        every_plane(plan.high, high_plane, 1)

    def finish_plane(x):
        i = plan.low + x
        for t in range(plan.tiles):
            at = (i, t, slice(ROWS, top))

            def get(argument, component):
                if argument == PINNED:
                    return pinned_own[x, t]
                return extended[argument][(component, *at)]

            for group, component in [(POSITION, c) for c in range(3)] + [(PINNED, 0)]:
                extended[group][(component, *at)] = plan.value(group, component, get)

    for parity in range(2):
        pl.when(flags[6] == parity)(functools.partial(fill_all, parity))
    for one in copies[:large]:
        one.wait()
    if pinned_own is not None:
        every_plane(plan.x, finish_plane, 2)


def assemble_copies(plan):
    skipping = sum(field.skip > 0 for field in plan.fields)
    return (3 * len(plan.fields) + 2 * skipping) * plan.tiles + 1 + plan.low + plan.high


def plane_loop(ref, first, last, row, body, carried, unroll):
    def turn(plane, carried, count):
        here = spot(ref, plane, row)
        pending = []
        for k in range(count):
            carried, stores = body(here.at_plane(k), carried)
            pending += stores
        for one in pending:
            store(*one)
        return carried

    count = last - first + 1
    carried = lax.fori_loop(
        0, count // unroll, lambda j, c: turn(first + j * unroll, c, unroll), carried
    )
    rest = count % unroll
    return turn(last + 1 - rest, carried, rest) if rest else carried


class Spot(NamedTuple):
    base: jax.Array
    plane: jax.Array
    planes: int = 0
    rows: int = 0

    def at_plane(self, step):
        return self._replace(planes=self.planes + step)

    def at_row(self, step):
        return self._replace(rows=self.rows + step)


def spot(ref, plane, row):
    return Spot(plane * (ref.shape[-3] * ref.shape[-2]) + row, plane)


def tile_rows(ref, component, at):
    planes, tiles, rows, lanes = ref.shape[-4:]
    first = (component * planes + at.planes) * tiles * rows + at.rows
    flat = ref.reshape(math.prod(ref.shape[:-1]), lanes)
    return flat, [at.base + (first + t * rows) for t in range(tiles)]


def load(ref, component, at):
    flat, starts = tile_rows(ref, component, at)
    return [flat[pl.ds(start, ROWS), :] for start in starts]


def store(ref, component, at, tiles):
    flat, starts = tile_rows(ref, component, at)
    for start, tile in zip(starts, tiles):
        flat[pl.ds(start, ROWS), :] = tile


def each(function, *tiles):
    return [function(*one) for one in zip(*tiles)]


def add(first, second):
    return each(lambda a, b: a + b, first, second)


def subtract(first, second):
    return each(lambda a, b: a - b, first, second)


def lane_below(tiles):
    lane = lane_index((ROWS, LANES))
    rolled = [pltpu.roll(tile, 1, 1) for tile in tiles]
    return [jnp.where(lane == 0, rolled[t - 1], rolled[t]) for t in range(len(tiles))]


def lane_above(tiles):
    lane = lane_index((ROWS, LANES))
    rolled = [pltpu.roll(tile, LANES - 1, 1) for tile in tiles]
    count = len(tiles)
    return [
        jnp.where(lane == LANES - 1, rolled[(t + 1) % count], rolled[t]) for t in range(count)
    ]


def chunks(first, last, body):
    count = -(-(last - first + 1) // ROWS)

    def one(j, _):
        body(jnp.minimum(first + j * ROWS, last - ROWS + 1))
        return 0

    lax.fori_loop(0, count, one, 0)


class Inside:
    def __init__(self, plan, flags):
        self.plan = plan
        self.flags = flags

    def tiles(self, row, scale):
        plan, flags = self.plan, self.flags
        rows = row + lax.broadcasted_iota(jnp.int32, (ROWS, LANES), 0)
        keep = jnp.where(rows < ROWS, flags[2], jnp.where(rows >= ROWS + plan.y, flags[3], 1.0))
        lane = lane_index((ROWS, LANES))
        edge = jnp.where(lane < LANES // 2, flags[5], flags[4])
        keep = scale * keep
        return [keep] * plan.tiles + [keep * edge]

    def plane(self, at):
        plan, flags = self.plan, self.flags
        i = at.plane + at.planes
        return jnp.where(
            i < plan.low, flags[0], jnp.where(i >= plan.low + plan.x, flags[1], 1.0)
        )


def force_pass(density, energy, force, mass, inside, planes, rows, unroll):
    def chunk(row):
        keep = inside.tiles(row, 0.4 * 0.25)

        def slab(at):
            here, under = load(density, 0, at), load(density, 0, at.at_row(-1))
            p = each(lambda a, b: a * b, here, load(energy, 0, at))
            p_under = each(lambda a, b: a * b, under, load(energy, 0, at.at_row(-1)))
            summed, stepped = add(p, p_under), subtract(p_under, p)
            weight = add(here, under)
            summed_z, stepped_z = lane_below(summed), lane_below(stepped)
            return (
                add(summed, summed_z),
                add(stepped, stepped_z),
                subtract(summed_z, summed),
                add(weight, lane_below(weight)),
            )

        def plane(at, before):
            now = slab(at)
            here = inside.plane(at)
            scale = [tile * here for tile in keep]
            stores = []
            for component in range(3):
                across = (subtract if component == 0 else add)(before[component], now[component])
                result = each(lambda a, b: a * b, scale, across)
                stores.append((force, component, at, result))
            result = each(lambda a, b: 0.125 * (a + b) + 6.0 * CONSISTENT, before[3], now[3])
            stores.append((mass, 0, at, result))
            return now, stores

        plane_loop(density, *planes, row, plane, slab(spot(density, planes[0] - 1, row)), unroll)

    chunks(*rows, chunk)


def face_sum(ref, component, at, before, here, after):
    total = add(add(before, after), add(lane_below(here), lane_above(here)))
    sides = add(load(ref, component, at.at_row(-1)), load(ref, component, at.at_row(1)))
    return add(total, sides)


def stencil_pass(ref, planes, rows, setup, use, unroll):
    def chunk(row):
        given = setup(row)

        def plane(at, carried):
            before, here = carried
            after = [load(ref, component, at.at_plane(1)) for component in range(3)]
            sums = [
                face_sum(ref, component, at, before[component], here[component], after[component])
                for component in range(3)
            ]
            return (here, after), use(at, here, sums, given)

        start = spot(ref, planes[0], row)
        first = [load(ref, component, start.at_plane(-1)) for component in range(3)]
        second = [load(ref, component, start) for component in range(3)]
        plane_loop(ref, *planes, row, plane, (first, second), unroll)

    chunks(*rows, chunk)


def whole_sum(tile):
    return jnp.sum(jnp.sum(tile, axis=0, keepdims=True), axis=1, keepdims=True)


def moments_kernel(plan, *refs):
    flags, density, energy = refs[:3]
    messages, out = refs[3:8], refs[8]
    density_ext, energy_ext, packed_ext, force, image, mass, semaphores = refs[9:]
    assemble(
        plan,
        flags,
        [density, energy],
        messages,
        None,
        [density_ext, energy_ext],
        packed_ext,
        None,
        semaphores,
    )
    inside = Inside(plan, flags)
    low, x, y = plan.low, plan.x, plan.y
    force_pass(
        density_ext,
        energy_ext,
        force,
        mass,
        inside,
        (low - 1, low + x + 1),
        (ROWS - 1, ROWS + y + 1),
        MOMENTS_UNROLL,
    )

    def multiply(at, here, sums, keep):
        weight = load(mass, 0, at)
        scale = [tile * inside.plane(at) for tile in keep]
        stores = []
        for component in range(3):
            result = each(
                lambda m, a, k, s: m * a + k * s, weight, here[component], scale, sums[component]
            )
            stores.append((image, component, at, result))
        return stores

    stencil_pass(
        force,
        (low, low + x),
        (ROWS, ROWS + y),
        lambda row: inside.tiles(row, CONSISTENT),
        multiply,
        MOMENTS_UNROLL,
    )

    own = range(plan.tiles)
    nothing = jnp.zeros((ROWS, LANES), jnp.float32)

    def first_chunk(j, sums):
        row = ROWS + j * ROWS

        def plane(at, sums):
            sums = list(sums)
            for component in range(3):
                f = load(force, component, at)
                v = load(image, component, at)
                for t in own:
                    sums[component] = sums[component] + f[t] * f[t]
                    sums[3 + component] = sums[3 + component] + f[t] * v[t]
            return tuple(sums), []

        return plane_loop(force, low, low + x - 1, row, plane, sums, MOMENTS_UNROLL)

    sums = lax.fori_loop(0, y // ROWS, first_chunk, (nothing,) * 6)
    sums = [whole_sum(one) for one in sums]
    square = sums[:3]
    shift = [
        jnp.where(square[c] > 0, sums[3 + c] / jnp.where(square[c] > 0, square[c], 1.0), 0.0)
        for c in range(3)
    ]

    def pair(component, at):
        f = load(force, component, at)
        v = load(image, component, at)
        return f, each(lambda a, b: a - shift[component] * b, v, f)

    def second_chunk(j, sums):
        row = ROWS + j * ROWS

        def plane(at, carried):
            here, sums = carried
            sums = list(sums)
            ahead = [pair(component, at.at_plane(1)) for component in range(3)]
            weight = load(mass, 0, at)
            for component in range(3):
                f, w = here[component]
                f_next, w_next = ahead[component]
                f_up, w_up = pair(component, at.at_row(1))
                f_high = add(add(f_next, f_up), lane_above(f))
                w_high = add(add(w_next, w_up), lane_above(w))
                for t in own:
                    k = 5 * component
                    heavy = weight[t] * w[t]
                    sums[k] = sums[k] + f[t] * w[t]
                    sums[k + 1] = sums[k + 1] + w[t] * w[t]
                    sums[k + 2] = sums[k + 2] + (
                        f[t] * heavy + CONSISTENT * (f[t] * w_high[t] + w[t] * f_high[t])
                    )
                    sums[k + 3] = sums[k + 3] + w[t] * (
                        heavy + (2.0 * CONSISTENT) * w_high[t]
                    )
                    sums[k + 4] = sums[k + 4] + f[t] * (
                        weight[t] * f[t] + (2.0 * CONSISTENT) * f_high[t]
                    )
            return (ahead, tuple(sums)), []

        start = [pair(component, spot(force, low, row)) for component in range(3)]
        return plane_loop(force, low, low + x - 1, row, plane, (start, sums), MOMENTS_UNROLL)[1]

    rest = lax.fori_loop(0, y // ROWS, second_chunk, (nothing,) * 15)
    lane = lane_index((1, LANES))
    line = jnp.zeros((1, LANES), jnp.float32)
    for c in range(3):
        values = [shift[c], square[c]] + [whole_sum(one) for one in rest[5 * c : 5 * c + 5]]
        for k, value in enumerate(values):
            line = jnp.where(lane == 3 * k + c, value, line)
    out[...] = line


def solve_weights(sums):
    got = [sums if k == 0 else pltpu.roll(sums, LANES - 3 * k, 1) for k in range(MOMENTS)]
    c, p0, q1, q2, q3, q4, q5 = got

    def total(value):
        return jnp.sum(value, axis=0, keepdims=True)

    norm_now = total(p0)
    alpha = norm_now / total(q1 + c * p0)
    a = 1.0 - alpha * c
    norm_next = total(a * a * p0 - 2.0 * a * alpha * q1 + alpha * alpha * q2)
    product = total(a * a * q5 - 2.0 * a * alpha * q3 + alpha * alpha * q4)
    ratio = norm_next / norm_now
    later = norm_next / (product - ratio * norm_next / alpha)
    lane = lane_index((1, LANES))

    def pick(value, component):
        return jnp.sum(jnp.where(lane == component, value, 0.0), axis=1, keepdims=True)

    on_force, on_image = alpha + later * (1.0 + ratio), -later * alpha
    return [(pick(on_force, k), pick(on_image, k)) for k in range(3)]


def step_kernel(plan, *refs):
    flags, sums, density, energy, position, velocity, pinned = refs[:7]
    messages, inner = refs[7:14], refs[14:18]
    velocity_new, accel, relaxed, density_new, energy_new = refs[18:23]
    (
        density_ext,
        energy_ext,
        moved,
        speed,
        free_ext,
        packed_ext,
        pinned_own,
        force,
        mass,
        other,
        semaphores,
        out_semaphores,
    ) = refs[23:]
    assemble(
        plan,
        flags,
        [density, energy, position, velocity, pinned],
        messages,
        inner,
        [density_ext, energy_ext, moved, speed, free_ext],
        packed_ext,
        pinned_own,
        semaphores,
    )
    inside = Inside(plan, flags)
    low, x, y = plan.low, plan.x, plan.y
    weights = solve_weights(sums[...])
    reach = SWEEPS + 1
    force_pass(
        density_ext,
        energy_ext,
        force,
        mass,
        inside,
        (low - reach, low + x + reach),
        (ROWS - reach, ROWS + y + reach),
        STEP_UNROLL,
    )

    def advance(at, here, sums, keep):
        weight = load(mass, 0, at)
        scale = [tile * inside.plane(at) for tile in keep]
        stores = []
        for component in range(3):
            on_force, on_image = weights[component]
            result = each(
                lambda m, a, k, s: on_force * a + on_image * (m * a + k * s),
                weight,
                here[component],
                scale,
                sums[component],
            )
            faster = each(lambda v, a: v + TIME_STEP * a, load(speed, component, at), result)
            further = each(
                lambda b, a: b + (TIME_STEP * TIME_STEP) * a, load(moved, component, at), result
            )
            stores += [
                (other, component, at, result),
                (speed, component, at, faster),
                (moved, component, at, further),
            ]
        return stores

    reach -= 1
    advanced = round_up(y + 2 * reach + 1, ROWS)
    stencil_pass(
        force,
        (low - reach, low + x + reach),
        (ROWS - reach, ROWS - reach + advanced - 1),
        lambda row: inside.tiles(row, CONSISTENT),
        advance,
        STEP_UNROLL,
    )

    out_copies = []

    def write(source, target, component, result=None):
        for t in range(plan.tiles):
            place = target if result is None else target.at[result]
            out_copies.append(
                pltpu.make_async_copy(
                    source.at[component, pl.ds(low, x), t, pl.ds(ROWS, y), :],
                    place.at[:, :, pl.ds(t * LANES, LANES)],
                    out_semaphores.at[len(out_copies)],
                )
            )
            out_copies[-1].start()

    for component in range(3):
        write(other, accel, component, component)
    accel_copies = len(out_copies)
    for component in range(3):
        write(speed, velocity_new, component, component)

    content = mass

    def content_chunk(row):
        def slab(at):
            under = [load(speed, component, at) for component in range(3)]
            over = [load(speed, component, at.at_row(1)) for component in range(3)]
            along_x = add(under[0], over[0])
            along_y = subtract(over[1], under[1])
            along_z = add(under[2], over[2])
            along_x = add(along_x, lane_above(along_x))
            along_y = add(along_y, lane_above(along_y))
            along_z = subtract(lane_above(along_z), along_z)
            return along_x, add(along_y, along_z)

        def plane(at, before):
            now = slab(at.at_plane(1))
            spread = add(subtract(now[0], before[0]), add(now[1], before[1]))
            held = load(energy_ext, 0, at)
            lagged = each(lambda e, s: e - (0.25 * 0.4 * TIME_STEP) * (e * s), held, spread)
            result = each(lambda d, e: d * e, load(density_ext, 0, at), lagged)
            return now, [(content, 0, at, result)]

        plane_loop(speed, low - 1, low + x, row, plane, slab(spot(speed, low - 1, row)), STEP_UNROLL)

    chunks(ROWS - 1, ROWS + y, content_chunk)

    for one in out_copies[:accel_copies]:
        one.wait()
    source, target = moved, other
    for _ in range(SWEEPS):
        reach -= 1

        def relax(at, here, sums, given, target=target):
            rate = load(free_ext, 0, at)
            stores = []
            for component in range(3):
                result = each(
                    lambda r, s, f: r + f * (s * (1.0 / 6.0) - r),
                    here[component],
                    sums[component],
                    rate,
                )
                stores.append((target, component, at, result))
            return stores

        stencil_pass(
            source,
            (low - reach, low + x + reach),
            (ROWS - reach, ROWS + y + reach),
            lambda row: None,
            relax,
            STEP_UNROLL,
        )
        source, target = target, (force if target is other else other)
    settled, free_buffer = source, target
    for component in range(3):
        write(settled, relaxed, component, component)

    quantities = (density_ext, content)

    def remap_chunk(row):
        def shift(component, at):
            return subtract(load(settled, component, at), load(moved, component, at))

        def slab(at):
            over = at.at_row(1)
            x_here = add(shift(0, at), shift(0, over))
            y_here, y_over = shift(1, at), shift(1, over)
            z_here = add(shift(2, at), shift(2, over))
            return (
                add(x_here, lane_above(x_here)),
                add(y_here, lane_above(y_here)),
                add(y_over, lane_above(y_over)),
                z_here,
                [load(one, 0, at) for one in quantities],
            )

        def flux(speeds, upper, lower):
            return each(lambda s, u, l: s * jnp.where(s > 0, u, l), speeds, upper, lower)

        def x_flux(speeds, upper, lower):
            return [flux(speeds, u, l) for u, l in zip(upper, lower)]

        def plane(at, carried):
            now, entering = carried
            ahead = slab(at.at_plane(1))
            leaving = x_flux(ahead[0], ahead[4], now[4])
            y_here, y_over, z_here = [add(now[k], ahead[k]) for k in (1, 2, 3)]
            stores = []
            for k, one in enumerate(quantities):
                held = now[4][k]
                under, over = [load(one, 0, at.at_row(step)) for step in (-1, 1)]
                through_z = flux(z_here, held, lane_below(held))
                change = subtract(leaving[k], entering[k])
                change = add(change, flux(y_over, over, held))
                change = subtract(change, flux(y_here, held, under))
                change = add(change, subtract(lane_above(through_z), through_z))
                result = each(lambda q, c: q + 0.25 * c, held, change)
                stores.append((free_buffer, k, at, result[: plan.tiles]))
            return (ahead, leaving), stores

        first = spot(settled, low, row)
        start = slab(first)
        before = [load(one, 0, first.at_plane(-1)) for one in quantities]
        plane_loop(settled, low, low + x - 1, row, plane, (start, x_flux(start[0], start[4], before)), STEP_UNROLL)

    chunks(ROWS, ROWS + y - 1, remap_chunk)
    write(free_buffer, density_new, 0)
    write(free_buffer, energy_new, 1)
    for one in out_copies[accel_copies:]:
        one.wait()


def line_hops():
    hops = []
    for axis in ("bz", "by", "bx"):
        step = 1
        while step < lax.axis_size(axis):
            hops.append((axis, step))
            step *= 2
    return hops


def gather_lines(line, hops):
    for axis, step in hops:
        count = lax.axis_size(axis)
        assert count & (count - 1) == 0
        got = lax.ppermute(line, axis, [(i, i ^ step) for i in range(count)])
        later = (lax.axis_index(axis) // step) % 2 == 1
        line = jnp.concatenate([jnp.where(later, got, line), jnp.where(later, line, got)])
    return line


def extended_scratch(plan, count):
    return pltpu.VMEM((count, plan.planes, plan.tiles + 1, plan.rows, LANES), jnp.float32)


def message_specs(planes, rows):
    return [any_space()] * planes + [in_vmem()] * rows


def on_device(position, velocity, density, energy, pinned):
    shape = density.shape
    arrays = [density[None], energy[None], position, velocity, pinned[None]]
    flags = jnp.stack(
        [
            jnp.float32(limit)
            for axis in ("bx", "by", "bz")
            for limit in (
                lax.axis_index(axis) > 0,
                lax.axis_index(axis) < lax.axis_size(axis) - 1,
            )
        ]
        + [(lax.axis_index("by") % 2).astype(jnp.float32)]
    )
    groups = [
        (1, WIDE, WIDE),
        (1, WIDE, WIDE),
        (3, SWEEPS, SWEEPS + 1),
        (3, 1, 2),
        (1, SWEEPS - 1, SWEEPS),
    ]
    narrow = Plan([(1, NARROW, NARROW)] * 2, shape)
    wide = Plan(groups, shape, narrow, cut=None)
    cells = arrays[:2]

    packed = exchange_lanes(narrow, pack_lanes(narrow, cells))
    planes = exchange_planes(*pack_planes(narrow, flags, cells, packed))
    wide_lanes = pack_lanes(wide, arrays)
    planes, wide_lanes = lax.optimization_barrier((planes, wide_lanes))
    wide_packed = exchange_lanes(wide, wide_lanes)
    rows = exchange_rows(pack_rows(narrow, flags, cells, packed, True, planes))

    (wide_planes,) = pack_planes(wide, flags, arrays, wide_packed)
    wide_rows = pack_rows(wide, flags, arrays, wide_packed, True)
    rows, wide_planes, wide_rows = lax.optimization_barrier((rows, wide_planes, wide_rows))
    wide_planes = exchange_planes(wide_planes)
    wide_rows = exchange_rows(wide_rows, to_self=False)

    line = pl.pallas_call(
        functools.partial(moments_kernel, narrow),
        in_specs=[in_smem()] + [any_space()] * 2 + message_specs(3, 2),
        out_specs=in_vmem(),
        out_shape=jax.ShapeDtypeStruct((1, LANES), jnp.float32),
        scratch_shapes=[
            extended_scratch(narrow, 1),
            extended_scratch(narrow, 1),
            pltpu.VMEM((narrow.planes, narrow.rows, LANES), jnp.float32),
            extended_scratch(narrow, 3),
            extended_scratch(narrow, 3),
            extended_scratch(narrow, 1),
            pltpu.SemaphoreType.DMA((assemble_copies(narrow),)),
        ],
        compiler_params=pltpu.CompilerParams(vmem_limit_bytes=VMEM_BYTES),
        cost_estimate=cost(1),
        name="moments",
    )(flags, *cells, packed, *planes, *rows)

    line, wide_rows = lax.optimization_barrier((line, wide_rows))
    hops = line_hops()
    early = len(hops) - 3
    lines = gather_lines(line, hops[:early])
    lines, wide_planes = lax.optimization_barrier((lines, wide_planes))
    corners = pack_rows(wide, flags, None, None, False, wide_planes, planes)
    lines, corners = lax.optimization_barrier((lines, corners))
    corners = exchange_rows(corners)
    messages = [wide_packed, *wide_planes, *wide_rows, *corners]
    nodes = jax.ShapeDtypeStruct((3, *shape), jnp.float32)
    cell = jax.ShapeDtypeStruct(shape, jnp.float32)
    return pl.pallas_call(
        functools.partial(step_kernel, wide),
        in_specs=[in_smem(), in_vmem()] + [any_space()] * 5 + message_specs(3, 4) + message_specs(2, 2),
        out_specs=[any_space()] * 5,
        out_shape=[nodes, nodes, nodes, cell, cell],
        scratch_shapes=[
            extended_scratch(wide, 1),
            extended_scratch(wide, 1),
            extended_scratch(wide, 3),
            extended_scratch(wide, 3),
            extended_scratch(wide, 1),
            pltpu.VMEM((wide.planes, wide.rows, LANES), jnp.float32),
            pltpu.VMEM((wide.x, wide.tiles, wide.y, LANES), jnp.int32),
            extended_scratch(wide, 3),
            extended_scratch(wide, 1),
            extended_scratch(wide, 3),
            pltpu.SemaphoreType.DMA((assemble_copies(wide),)),
            pltpu.SemaphoreType.DMA((11 * wide.tiles,)),
        ],
        compiler_params=pltpu.CompilerParams(vmem_limit_bytes=VMEM_BYTES),
        cost_estimate=cost(1),
        name="step",
    )(flags, gather_lines(lines, hops[early:]), *arrays, *messages, *planes, *rows)


def solution(mesh):
    in_specs = (
        P(None, "bx", "by", "bz"),
        P(None, "bx", "by", "bz"),
        P("bx", "by", "bz"),
        P("bx", "by", "bz"),
        P("bx", "by", "bz"),
    )
    out_specs = (
        P(None, "bx", "by", "bz"),
        P(None, "bx", "by", "bz"),
        P(None, "bx", "by", "bz"),
        P("bx", "by", "bz"),
        P("bx", "by", "bz"),
    )
    return jax.shard_map(
        on_device, mesh=mesh, in_specs=in_specs, out_specs=out_specs, check_vma=False
    )
```
